32 devices in a mesh: ent: 8 (over z, y), rep: 4 (over x, core).
Axes of the slice: x: 2, y: 2, z: 4, core: 2. Of those that a mesh axis runs over, the one named last changes fastest.
Arguments:
- entity_emb: bfloat16 [73728, 256], P(('ent', 'rep')), may hold values from -5 to 5
- relation_emb: bfloat16 [474, 256], replicated, may hold values from -60 to 60
- in_weight: bfloat16 [256, 256], replicated, may hold values from -0.375 to 0.375
- out_weight: bfloat16 [256, 256], replicated, may hold values from -0.375 to 0.375
- loop_weight: bfloat16 [256, 256], replicated, may hold values from -0.375 to 0.375
- rel_weight: bfloat16 [256, 256], replicated, may hold values from -0.375 to 0.375
- loop_rel: float32 [256], replicated, may hold values from -4 to 4
- edge_src: int32 [576, 768], P(('ent', 'rep')), may hold values from 0 to 3327, as said below
- edge_dst: int32 [576, 768], P(('ent', 'rep')), may hold values from 0 to 127
- edge_rel: int32 [576, 768], P(('ent', 'rep')), may hold values from 0 to 473
- export_rows: int32 [8, 128], P('ent'), may hold values from 0 to 9215, as said below
- query_head: int32 [256], replicated, may hold values from 0 to 73727
- query_rel: int32 [256], replicated, may hold values from 0 to 473
Outputs:
- log_probs: float32 [256, 73728], P(None, ('ent', 'rep'))
- expected_tail: float32 [256, 256], P('rep')
The draws below stay inside these ranges and needn't reach their ends.
Inputs may be any that keep to these rules, and one draw needn't show every extreme that they name: Each row of export_rows begins with a list of entries; the slots past the list's length hold filler values that no edge names. Some list fills the whole row. `edge_src`: A value j + 2304 with j >= 0 always names a list entry of export_rows, never filler.
All inputs are finite; a program needn't handle non-finite values.
Results may differ from the reference program's by a relative error of at most 0.0094.
Values may be sent and summed in bfloat16 or wider, within the bound.
No kernel may reach another device: no remote copies, remote signals or barrier semaphores. Data moves between devices by JAX's collectives and lax.ppermute only.
A program may use at most 64 MiB of HBM per device.

```python
import jax
import jax.numpy as jnp
from jax import lax

D = 256
REL = 474
BLK = 128
EPB = 768
BND = 128
QUERIES = 256
SUB = 2304
ENT_SH = 9216
ENTITIES = 73728
BLOCKS = 576
SLOTS = 1024


def live_counts(key):
    shard_count = SLOTS // BND
    base_key = jax.random.fold_in(key, 5151)
    shard_ids = jnp.arange(shard_count, dtype=jnp.int32)
    is_hub = (jax.random.randint(base_key, (shard_count,), 0, 16) == 0) | (shard_ids == shard_count - 1)
    is_hub = is_hub & (shard_ids != 0)
    modest = jax.random.randint(jax.random.fold_in(base_key, 1), (shard_count,), max(1, BND // 4), BND // 3 + 1)
    return jnp.where(is_hub, BND, modest)


def draw_export_rows(key, part):
    shard_count = SLOTS // BND
    counts = live_counts(key)
    row_ids = jax.random.randint(jax.random.fold_in(key, 6262), (shard_count, BND), 0, ENT_SH)
    slot_ids = jnp.arange(BND, dtype=jnp.int32)[None, :]
    row_ids = jnp.where(slot_ids < counts[:, None], row_ids, ENT_SH - 1)
    row_ids = row_ids.at[0, BND - 1].set(0)
    return row_ids.astype(jnp.int32)


def draw_edge_src(key, part):
    shard_count = SLOTS // BND
    counts = live_counts(key)
    base_key = jax.random.fold_in(key, 7373)
    shape = (BLOCKS, EPB)
    is_near = jax.random.randint(jax.random.fold_in(base_key, 1), shape, 0, 2) == 0
    near_ids = jax.random.randint(jax.random.fold_in(base_key, 2), shape, 0, SUB)
    owner_ids = jax.random.randint(jax.random.fold_in(base_key, 3), shape, 0, shard_count)
    slot_ids = jax.random.randint(jax.random.fold_in(base_key, 4), shape, 0, 1 << 20) % counts[owner_ids]
    sources = jnp.where(is_near, near_ids, SUB + owner_ids * BND + slot_ids)
    sources = sources.at[0, 0].set(SUB + SLOTS - 1)
    sources = sources.at[0, 1].set(0)
    return sources.astype(jnp.int32)


def draw_relation_emb(key, part):
    values = jnp.clip(jax.random.normal(jax.random.fold_in(key, 11), (REL, D), jnp.float32), -5.0, 5.0)
    return values.astype(jnp.bfloat16)


def touch_ends(entries, stream_key, smallest, top_value):
    spot = [jax.random.randint(jax.random.fold_in(stream_key, axis), (), 0, length) for axis, length in enumerate(entries.shape)]
    widest = entries.shape.index(max(entries.shape))
    next_to = spot[:widest] + [(spot[widest] + 1) % entries.shape[widest]] + spot[widest + 1:]
    return entries.at[tuple(spot)].set(smallest).at[tuple(next_to)].set(top_value)


def levels(own_key, shape, pieces, smallest, high):
    factor_of = 1.0
    for dim, blocks in pieces:
        steps = jax.random.uniform(jax.random.fold_in(jax.random.fold_in(own_key, 6), dim), (blocks,), jnp.float32, smallest / len(pieces), high / len(pieces))
        factor_of = factor_of * jnp.repeat(jnp.exp(steps), shape[dim] // blocks).reshape((-1,) + (1,) * (len(shape) - 1 - dim))
    return factor_of


def centred(key, dims, deviation, limit, split=(), kind=jnp.bfloat16):
    values = deviation * jax.random.normal(key, dims, jnp.float32)
    if split:
        values = values * levels(key, dims, split, -0.22, 0.18)
    return jnp.clip(values, -limit, limit).astype(kind)


def setup_inputs(seed: int = 0) -> dict:
    splits = jax.random.split(jax.random.key(seed), 14)
    entity_emb = centred(splits[0], (ENTITIES, D), 1.0, 5.0, ((0, 32),))
    relation_emb = draw_relation_emb(jax.random.fold_in(splits[13], 71), 0)
    in_weight = centred(splits[2], (D, D), D ** -0.5, 0.375)
    out_weight = centred(splits[3], (D, D), D ** -0.5, 0.375)
    loop_weight = centred(splits[4], (D, D), D ** -0.5, 0.375)
    rel_weight = centred(splits[5], (D, D), D ** -0.5, 0.375)
    loop_rel = centred(splits[6], (D,), 1.0, 4.0, (), jnp.float32)
    edge_src = draw_edge_src(jax.random.fold_in(splits[13], 71), 0)
    edge_dst = touch_ends(jax.random.randint(splits[8], (BLOCKS, EPB), 0, BLK), jax.random.fold_in(splits[8], 1), 0, BLK - 1).astype(jnp.int32)
    edge_rel = touch_ends(jax.random.randint(splits[9], (BLOCKS, EPB), 0, REL), jax.random.fold_in(splits[9], 1), 0, REL - 1).astype(jnp.int32)
    export_rows = draw_export_rows(jax.random.fold_in(splits[13], 71), 0)
    query_head = touch_ends(jax.random.randint(splits[11], (QUERIES,), 0, ENTITIES), jax.random.fold_in(splits[11], 1), 0, ENTITIES - 1).astype(jnp.int32)
    query_rel = touch_ends(jax.random.randint(splits[12], (QUERIES,), 0, REL), jax.random.fold_in(splits[12], 1), 0, REL - 1).astype(jnp.int32)
    return dict(entity_emb=entity_emb, relation_emb=relation_emb, in_weight=in_weight, out_weight=out_weight, loop_weight=loop_weight, rel_weight=rel_weight, loop_rel=loop_rel, edge_src=edge_src, edge_dst=edge_dst, edge_rel=edge_rel, export_rows=export_rows, query_head=query_head, query_rel=query_rel)


def reference(entity_emb, relation_emb, in_weight, out_weight, loop_weight, rel_weight, loop_rel, edge_src, edge_dst, edge_rel, export_rows, query_head, query_rel):
    per_group = SUB // BLK
    group_count = ENTITIES // SUB
    half_rel = REL // 2
    rel_full = jnp.dot(relation_emb, rel_weight, preferred_element_type=jnp.float32)

    def one_group(group_id):
        sources = lax.dynamic_slice_in_dim(edge_src, group_id * per_group, per_group, 0)
        targets = lax.dynamic_slice_in_dim(edge_dst, group_id * per_group, per_group, 0)
        relation_ids = lax.dynamic_slice_in_dim(edge_rel, group_id * per_group, per_group, 0).reshape(-1)
        far_slot = jnp.clip(sources - SUB, 0, SLOTS - 1)
        owner_ids = far_slot // BND
        listed = export_rows[owner_ids, far_slot % BND]
        source = jnp.where(sources < SUB, group_id * SUB + sources, owner_ids * ENT_SH + listed).reshape(-1)
        source_rows = entity_emb[source].astype(jnp.float32)
        composed = (source_rows * relation_emb[relation_ids].astype(jnp.float32)).astype(jnp.bfloat16)
        composed = lax.optimization_barrier(composed).astype(jnp.float32)
        target = (jnp.arange(per_group, dtype=jnp.int32)[:, None] * BLK + targets).reshape(-1)
        inward = relation_ids < half_rel
        seg_in = jnp.where(inward, target, SUB)
        seg_out = jnp.where(inward, SUB, target)
        unit = jnp.ones((target.shape[0],), jnp.float32)
        sum_in = jax.ops.segment_sum(composed, seg_in, SUB + 1)[:SUB]
        sum_out = jax.ops.segment_sum(composed, seg_out, SUB + 1)[:SUB]
        count_in = jax.ops.segment_sum(unit, seg_in, SUB + 1)[:SUB]
        count_out = jax.ops.segment_sum(unit, seg_out, SUB + 1)[:SUB]
        agg_in = (sum_in / jnp.maximum(count_in, 1.0)[:, None]).astype(jnp.bfloat16)
        agg_out = (sum_out / jnp.maximum(count_out, 1.0)[:, None]).astype(jnp.bfloat16)
        own_rows = lax.dynamic_slice_in_dim(entity_emb, group_id * SUB, SUB, 0)
        own_loop = (own_rows.astype(jnp.float32) * loop_rel).astype(jnp.bfloat16)
        preact = jnp.dot(agg_in, in_weight, preferred_element_type=jnp.float32)
        preact = preact + jnp.dot(agg_out, out_weight, preferred_element_type=jnp.float32)
        preact = preact + jnp.dot(own_loop, loop_weight, preferred_element_type=jnp.float32)
        return jnp.tanh(preact).astype(jnp.bfloat16)

    hidden = lax.map(one_group, jnp.arange(group_count, dtype=jnp.int32)).reshape(ENTITIES, D)
    head_rows = hidden[query_head].astype(jnp.float32)
    query_vec = (head_rows * rel_full[query_rel]).astype(jnp.bfloat16)
    scores = lax.dot_general(query_vec, hidden, (((1,), (1,)), ((), ())), preferred_element_type=jnp.float32)
    row_top = jnp.max(scores, axis=1)
    weights = jnp.exp(scores - row_top[:, None])
    row_total = jnp.sum(weights, axis=1)
    log_probs = scores - row_top[:, None] - jnp.log(row_total)[:, None]
    weighted = jnp.dot(weights, hidden.astype(jnp.float32), precision=lax.Precision.HIGHEST)
    expected_tail = weighted / row_total[:, None]
    return (log_probs, expected_tail)
```

```python
import functools

import jax
import jax.numpy as jnp
from jax import lax
from jax.experimental import pallas as pl
from jax.experimental.pallas import tpu as pltpu
from jax.sharding import PartitionSpec as P

BLK = 128
CHUNK = 1024
BF16 = jnp.bfloat16
F32 = jnp.float32
BOTH = ("ent", "rep")
NT = (((1,), (1,)), ((), ()))
VMEM_LIMIT = 56 * 2**20


def one_hot(index, rows):
    where = lax.broadcasted_iota(jnp.int16, (rows, index.shape[1]), 0) == index.astype(jnp.int16)
    return jnp.where(where, jnp.asarray(1, BF16), jnp.asarray(0, BF16))


def layer_kernel(
    half_rel,
    src_ref,
    dst_ref,
    rel_ref,
    emb_ref,
    near_ref,
    far_ref,
    relation_ref,
    in_ref,
    out_ref,
    loop_ref,
    loop_rel_ref,
    head_ref,
    hidden_ref,
    heads_ref,
    gathered_ref,
):
    rows_dev = emb_ref.shape[0]
    far_chunks = far_ref.shape[0]

    def one_block(i, carry):
        src = src_ref[pl.ds(i, 1), :]
        rel = rel_ref[pl.ds(i, 1), :]
        gathered = jnp.dot(
            near_ref[...], one_hot(src, rows_dev), preferred_element_type=F32
        )
        if far_chunks == 1:
            gathered += jnp.dot(
                far_ref[0], one_hot(src - rows_dev, CHUNK), preferred_element_type=F32
            )
        else:
            gathered_ref[...] = gathered

            def one_chunk(j, carry):
                gathered_ref[...] += jnp.dot(
                    far_ref[j],
                    one_hot(src - rows_dev - j * CHUNK, CHUNK),
                    preferred_element_type=F32,
                )
                return carry

            lax.fori_loop(0, far_chunks, one_chunk, 0)
            gathered = gathered_ref[...]
        relation = jnp.dot(
            relation_ref[...], one_hot(rel, relation_ref.shape[1]), preferred_element_type=F32
        )
        composed = (gathered * relation).astype(BF16)
        key = dst_ref[pl.ds(i, 1), :] + jnp.where(rel >= half_rel, BLK, 0)
        selector = (
            lax.broadcasted_iota(jnp.int32, (2 * BLK, key.shape[1]), 0) == key
        ).astype(F32)
        counts = jnp.sum(selector, axis=1, keepdims=True)
        sums = lax.dot_general(selector.astype(BF16), composed, NT, preferred_element_type=F32)
        agg = (sums / jnp.maximum(counts, 1.0)).astype(BF16)
        here = pl.ds(pl.multiple_of(i * BLK, BLK), BLK)
        own = (emb_ref[here, :].astype(F32) * loop_rel_ref[...]).astype(BF16)
        preact = jnp.dot(agg[:BLK], in_ref[...], preferred_element_type=F32)
        preact += jnp.dot(agg[BLK:], out_ref[...], preferred_element_type=F32)
        preact += jnp.dot(own, loop_ref[...], preferred_element_type=F32)
        hidden_ref[here, :] = jnp.tanh(preact).astype(BF16)
        return carry

    lax.fori_loop(0, src_ref.shape[0], one_block, 0)
    picks = lax.broadcasted_iota(jnp.int32, (head_ref.shape[0], rows_dev), 1) == head_ref[...]
    heads_ref[...] = jnp.dot(
        picks.astype(F32).astype(BF16), hidden_ref[...], preferred_element_type=F32
    ).astype(BF16)


def score_kernel(heads_ref, rel_ref, hidden_ref, scores_ref, weighted_ref, stats_ref):
    query = (heads_ref[...].astype(F32) * rel_ref[...]).astype(BF16)
    scores = lax.dot_general(query, hidden_ref[...], NT, preferred_element_type=F32)
    scores_ref[...] = scores
    top = jnp.max(scores, axis=1, keepdims=True)
    high = top.astype(BF16)
    low = (top - high.astype(F32)).astype(BF16)
    top = high.astype(F32) + low.astype(F32)
    weights = jnp.exp(scores - top)
    total = jnp.sum(weights, axis=1, keepdims=True)
    weighted_ref[...] = jnp.dot(
        weights.astype(BF16), hidden_ref[...], preferred_element_type=F32
    ).astype(BF16)
    total_high = total.astype(BF16)
    total_low = (total - total_high.astype(F32)).astype(BF16)
    lanes = lax.broadcasted_iota(jnp.int32, (query.shape[0], 128), 1)
    wide = jnp.where(lanes == 0, high.astype(F32), 0.0)
    wide = jnp.where(lanes == 1, low.astype(F32), wide)
    wide = jnp.where(lanes == 2, total_high.astype(F32), wide)
    wide = jnp.where(lanes == 3, total_low.astype(F32), wide)
    stats_ref[...] = jnp.transpose(wide)[: stats_ref.shape[0]].astype(BF16)


def body(
    entity_emb,
    relation_emb,
    in_weight,
    out_weight,
    loop_weight,
    rel_weight,
    loop_rel,
    edge_src,
    edge_dst,
    edge_rel,
    export_rows,
    query_head,
    query_rel,
):
    groups = lax.axis_size("ent")
    copies = lax.axis_size("rep")
    devices = groups * copies
    group = lax.axis_index("ent")
    member = lax.axis_index("rep")
    device = group * copies + member
    rows_dev, columns = entity_emb.shape
    queries = query_head.shape[0]
    batch_rows = queries // copies
    share = -(-batch_rows // groups)
    padded = share * devices

    listed = export_rows[0]
    slots = listed.shape[0]
    is_owned = listed // rows_dev == member
    picked = jnp.take(entity_emb, listed % rows_dev, axis=0)
    offered = jnp.where(is_owned[:, None], picked, jnp.zeros_like(picked))
    pieces = lax.all_to_all(offered, "rep", 0, 0, tiled=True)
    mine = jnp.sum(
        pieces.reshape(copies, slots // copies, columns).astype(F32), axis=0
    ).astype(BF16)
    spread = jnp.broadcast_to(mine[None], (devices,) + mine.shape)
    table = lax.all_to_all(spread, BOTH, 0, 0).reshape(groups * slots, columns)
    far_count = -(-(groups * slots) // CHUNK) * CHUNK
    far = jnp.pad(table, ((0, far_count - groups * slots), (0, 0)))
    far = far.reshape(far_count // CHUNK, CHUNK, columns).transpose(0, 2, 1)

    relations = relation_emb.shape[0]
    rel_count = -(-relations // 256) * 256
    relation_t = jnp.pad(relation_emb, ((0, rel_count - relations), (0, 0))).T
    local_head = jnp.pad(
        query_head - device * rows_dev, (0, padded - queries), constant_values=-1
    )[:, None]

    hidden, heads = pl.pallas_call(
        functools.partial(layer_kernel, relations // 2),
        out_shape=(
            jax.ShapeDtypeStruct((rows_dev, columns), BF16),
            jax.ShapeDtypeStruct((padded, columns), BF16),
        ),
        scratch_shapes=[pltpu.VMEM((columns, edge_src.shape[1]), F32)],
        compiler_params=pltpu.CompilerParams(vmem_limit_bytes=VMEM_LIMIT),
    )(
        edge_src,
        edge_dst,
        edge_rel,
        entity_emb,
        entity_emb.T,
        far,
        relation_t,
        in_weight,
        out_weight,
        loop_weight,
        loop_rel[None],
        local_head,
    )

    parts = lax.all_to_all(heads, BOTH, 0, 0, tiled=True).reshape(devices, share, columns)
    own_heads = jnp.sum(parts.astype(F32), axis=0).astype(BF16)
    head_rows = lax.all_to_all(
        jnp.broadcast_to(own_heads[None], (devices, share, columns)), BOTH, 0, 0
    ).reshape(padded, columns)[:queries]
    query_factor = jnp.dot(
        jnp.take(relation_emb, query_rel, axis=0), rel_weight, preferred_element_type=F32
    )

    scores, weighted, stats = pl.pallas_call(
        score_kernel,
        out_shape=(
            jax.ShapeDtypeStruct((queries, rows_dev), F32),
            jax.ShapeDtypeStruct((queries, columns), BF16),
            jax.ShapeDtypeStruct((16, queries), BF16),
        ),
        compiler_params=pltpu.CompilerParams(vmem_limit_bytes=VMEM_LIMIT),
    )(head_rows, query_factor, hidden)

    split = weighted.reshape(copies, batch_rows, columns)
    split = jnp.pad(split, ((0, 0), (0, share * groups - batch_rows), (0, 0)))
    split = split.reshape(copies, groups, share, columns).transpose(1, 0, 2, 3)
    split = split.reshape(devices, share * columns)
    figures = jnp.broadcast_to(stats[:4].reshape(1, 4 * queries), (devices, 4 * queries))
    payload = jnp.concatenate([split, figures], axis=1).reshape(devices, -1, 128)
    received = lax.all_to_all(payload, BOTH, 0, 0).reshape(devices, -1)
    sums = received[:, : share * columns].reshape(devices, share, columns).astype(F32)
    figures = received[:, share * columns :].reshape(devices, 4, queries).astype(F32)
    tops = figures[:, 0] + figures[:, 1]
    totals = figures[:, 2] + figures[:, 3]
    row_top = jnp.max(tops, axis=0)
    scale = jnp.exp(tops - row_top)
    row_total = jnp.sum(totals * scale, axis=0)
    factor = jnp.pad(
        (scale / row_total).reshape(devices, copies, batch_rows),
        ((0, 0), (0, 0), (0, share * groups - batch_rows)),
    ).reshape(devices, -1)
    own_factor = lax.dynamic_slice_in_dim(
        factor, (member * groups + group) * share, share, 1
    )
    own_expected = jnp.sum(sums * own_factor[:, :, None], axis=0)
    expected_tail = lax.all_to_all(
        jnp.broadcast_to(own_expected[None], (groups, share, columns)), "ent", 0, 0
    ).reshape(groups * share, columns)[:batch_rows]
    log_probs = scores - (row_top + jnp.log(row_total))[:, None]
    return (log_probs, expected_tail)


def solution(mesh):
    placed = (
        P(("ent", "rep"), None),
        P(),
        P(),
        P(),
        P(),
        P(),
        P(),
        P(("ent", "rep"), None),
        P(("ent", "rep"), None),
        P(("ent", "rep"), None),
        P("ent", None),
        P(),
        P(),
    )
    return jax.shard_map(
        body,
        mesh=mesh,
        in_specs=placed,
        out_specs=(P(None, ("ent", "rep")), P("rep", None)),
        check_vma=False,
    )
```

```python
import functools

import jax
import jax.numpy as jnp
from jax import lax
from jax.experimental import pallas as pl
from jax.experimental.pallas import tpu as pltpu
from jax.sharding import PartitionSpec as P

BLK = 128
CHUNK = 1024
BF16 = jnp.bfloat16
F32 = jnp.float32
BOTH = ("ent", "rep")
NT = (((1,), (1,)), ((), ()))
TN = (((0,), (0,)), ((), ()))
VMEM_LIMIT = 56 * 2**20
NEAR_LIMIT = 56 * 2**20


def one_hot(index, rows):
    where = lax.broadcasted_iota(jnp.int16, (rows, index.shape[1]), 0) == index.astype(jnp.int16)
    return jnp.where(where, jnp.asarray(1, BF16), jnp.asarray(0, BF16))


def one_hot_wide(index, rows):
    where = lax.broadcasted_iota(jnp.int32, (rows, index.shape[1]), 0) == index
    return where.astype(F32).astype(BF16)


def near_kernel(
    first, count, src_ref, rel_ref, near_ref, relation_ref, *rest
):
    mixed_ref, held_ref, sems = rest[-3:]
    rows_dev = near_ref.shape[1]

    def save(i, slot):
        return pltpu.make_async_copy(held_ref.at[slot], mixed_ref.at[i], sems.at[slot])

    def one_block(i, carry):
        slot = lax.rem(i, 2)
        src = src_ref[pl.ds(first + i, 1), :]
        rel = rel_ref[pl.ds(first + i, 1), :]
        gathered = jnp.dot(near_ref[...], one_hot(src, rows_dev), preferred_element_type=F32)
        relation = jnp.dot(
            relation_ref[...], one_hot(rel, relation_ref.shape[1]), preferred_element_type=F32
        )
        mixed = jnp.where(src < rows_dev, gathered, 1.0) * relation

        @pl.when(i >= 2)
        def _():
            save(first + i - 2, slot).wait()

        held_ref[slot] = mixed.astype(BF16)
        save(first + i, slot).start()
        return carry

    lax.fori_loop(0, count, one_block, 0)
    for i in range(max(count - 2, 0), count):
        save(first + i, i % 2).wait()


def far_kernel(
    half_rel,
    src_ref,
    dst_ref,
    rel_ref,
    emb_ref,
    far_ref,
    in_ref,
    out_ref,
    loop_ref,
    loop_rel_ref,
    head_ref,
    mixed_ref,
    hidden_ref,
    heads_ref,
    far_t_ref,
    gathered_ref,
    held_ref,
    sems,
):
    rows_dev = emb_ref.shape[0]
    blocks = src_ref.shape[0]
    far_chunks = far_ref.shape[0]

    def load(i, slot):
        return pltpu.make_async_copy(mixed_ref.at[i], held_ref.at[slot], sems.at[slot])

    load(0, 0).start()

    def turn(j, carry):
        far_t_ref[j] = jnp.transpose(far_ref[j])
        return carry

    lax.fori_loop(0, far_chunks, turn, 0)

    def one_block(i, carry):
        slot = lax.rem(i, 2)

        @pl.when(i + 1 < blocks)
        def _():
            load(i + 1, 1 - slot).start()

        load(i, slot).wait()
        src = src_ref[pl.ds(i, 1), :]
        rel = rel_ref[pl.ds(i, 1), :]
        if far_chunks == 1:
            gathered = jnp.dot(
                far_t_ref[0], one_hot(src - rows_dev, CHUNK), preferred_element_type=F32
            )
        else:
            gathered_ref[...] = jnp.zeros_like(gathered_ref)

            def one_chunk(j, carry):
                gathered_ref[...] += jnp.dot(
                    far_t_ref[j],
                    one_hot(src - rows_dev - j * CHUNK, CHUNK),
                    preferred_element_type=F32,
                )
                return carry

            lax.fori_loop(0, far_chunks, one_chunk, 0)
            gathered = gathered_ref[...]
        mixed = held_ref[slot].astype(F32)
        composed = (jnp.where(src < rows_dev, 1.0, gathered) * mixed).astype(BF16)
        key = dst_ref[pl.ds(i, 1), :] + jnp.where(rel >= half_rel, BLK, 0)
        selector = (
            lax.broadcasted_iota(jnp.int32, (2 * BLK, key.shape[1]), 0) == key
        ).astype(F32)
        counts = jnp.sum(selector, axis=1, keepdims=True)
        sums = lax.dot_general(selector.astype(BF16), composed, NT, preferred_element_type=F32)
        agg = (sums / jnp.maximum(counts, 1.0)).astype(BF16)
        here = pl.ds(pl.multiple_of(i * BLK, BLK), BLK)
        own = (emb_ref[here, :].astype(F32) * loop_rel_ref[...]).astype(BF16)
        preact = jnp.dot(agg[:BLK], in_ref[...], preferred_element_type=F32)
        preact += jnp.dot(agg[BLK:], out_ref[...], preferred_element_type=F32)
        preact += jnp.dot(own, loop_ref[...], preferred_element_type=F32)
        hidden_ref[here, :] = jnp.tanh(preact).astype(BF16)
        return carry

    lax.fori_loop(0, blocks, one_block, 0)
    picks = one_hot_wide(head_ref[...], rows_dev)
    heads_ref[...] = lax.dot_general(
        picks, hidden_ref[...], TN, preferred_element_type=F32
    ).astype(BF16)


def pick_kernel(index_ref, emb_ref, offered_ref):
    picks = one_hot_wide(index_ref[...], emb_ref.shape[0])
    offered_ref[...] = lax.dot_general(
        picks, emb_ref[...], TN, preferred_element_type=F32
    ).astype(BF16)


def near_call(first, count, blocks, src, rel, near, relation, mixed=None):
    columns, edges = near.shape[0], src.shape[1]
    flops = 2 * count * edges * columns * (near.shape[1] + relation.shape[1])
    anywhere = pl.BlockSpec(memory_space=pltpu.HBM)
    whole = pl.BlockSpec(memory_space=pltpu.VMEM)
    more = () if mixed is None else (mixed,)
    return pl.pallas_call(
        functools.partial(near_kernel, first, count),
        out_shape=jax.ShapeDtypeStruct((blocks, columns, edges), BF16),
        in_specs=[whole] * 4 + [anywhere] * len(more),
        out_specs=anywhere,
        input_output_aliases={4: 0} if more else {},
        scratch_shapes=[
            pltpu.VMEM((2, columns, edges), BF16),
            pltpu.SemaphoreType.DMA((2,)),
        ],
        compiler_params=pltpu.CompilerParams(vmem_limit_bytes=NEAR_LIMIT),
        cost_estimate=pl.CostEstimate(
            flops=flops, bytes_accessed=2 * count * edges * columns, transcendentals=0
        ),
    )(src, rel, near, relation, *more)


def score_kernel(heads_ref, rel_ref, hidden_ref, scores_ref, weighted_ref, stats_ref):
    query = (heads_ref[...].astype(F32) * rel_ref[...]).astype(BF16)
    scores = lax.dot_general(query, hidden_ref[...], NT, preferred_element_type=F32)
    scores_ref[...] = scores
    top = jnp.max(scores, axis=1, keepdims=True)
    high = top.astype(BF16)
    low = (top - high.astype(F32)).astype(BF16)
    top = high.astype(F32) + low.astype(F32)
    weights = jnp.exp(scores - top)
    total = jnp.sum(weights, axis=1, keepdims=True)
    weighted_ref[...] = jnp.dot(
        weights.astype(BF16), hidden_ref[...], preferred_element_type=F32
    ).astype(BF16)
    total_high = total.astype(BF16)
    total_low = (total - total_high.astype(F32)).astype(BF16)
    lanes = lax.broadcasted_iota(jnp.int32, (query.shape[0], 128), 1)
    wide = jnp.where(lanes == 0, high.astype(F32), 0.0)
    wide = jnp.where(lanes == 1, low.astype(F32), wide)
    wide = jnp.where(lanes == 2, total_high.astype(F32), wide)
    wide = jnp.where(lanes == 3, total_low.astype(F32), wide)
    stats_ref[...] = jnp.transpose(wide)[: stats_ref.shape[0]].astype(BF16)


def body(
    entity_emb,
    relation_emb,
    in_weight,
    out_weight,
    loop_weight,
    rel_weight,
    loop_rel,
    edge_src,
    edge_dst,
    edge_rel,
    export_rows,
    query_head,
    query_rel,
):
    groups = lax.axis_size("ent")
    copies = lax.axis_size("rep")
    devices = groups * copies
    group = lax.axis_index("ent")
    member = lax.axis_index("rep")
    device = group * copies + member
    rows_dev, columns = entity_emb.shape
    queries = query_head.shape[0]
    batch_rows = queries // copies
    share = -(-batch_rows // groups)
    padded = share * devices

    blocks = edge_src.shape[0]
    relations = relation_emb.shape[0]
    rel_count = -(-relations // 256) * 256
    relation_t = jnp.pad(relation_emb, ((0, rel_count - relations), (0, 0))).T
    near_t = entity_emb.T
    early = max(blocks * 5 // 18, 1)

    slots = export_rows.shape[1]
    offered = pl.pallas_call(
        pick_kernel,
        out_shape=jax.ShapeDtypeStruct((slots, columns), BF16),
        compiler_params=pltpu.CompilerParams(vmem_limit_bytes=NEAR_LIMIT),
    )(export_rows - member * rows_dev, entity_emb)
    pieces = lax.all_to_all(offered, "rep", 0, 0, tiled=True)
    mixed = near_call(0, early, blocks, edge_src, edge_rel, near_t, relation_t)
    mine = jnp.sum(
        pieces.reshape(copies, slots // copies, columns).astype(F32), axis=0
    ).astype(BF16)
    mine, mixed = lax.optimization_barrier((mine, mixed))
    spread = jnp.broadcast_to(mine[None], (devices,) + mine.shape)
    table = lax.all_to_all(spread, BOTH, 0, 0).reshape(groups * slots, columns)
    mixed = near_call(
        early, blocks - early, blocks, edge_src, edge_rel, near_t, relation_t, mixed
    )
    far_count = -(-(groups * slots) // CHUNK) * CHUNK
    far = jnp.pad(table, ((0, far_count - groups * slots), (0, 0)))
    far = far.reshape(far_count // CHUNK, CHUNK, columns)

    local_head = jnp.pad(
        query_head - device * rows_dev, (0, padded - queries), constant_values=-1
    )[None]
    whole = pl.BlockSpec(memory_space=pltpu.VMEM)
    hidden, heads = pl.pallas_call(
        functools.partial(far_kernel, relations // 2),
        out_shape=(
            jax.ShapeDtypeStruct((rows_dev, columns), BF16),
            jax.ShapeDtypeStruct((padded, columns), BF16),
        ),
        in_specs=[whole] * 10 + [pl.BlockSpec(memory_space=pltpu.HBM)],
        out_specs=(whole, whole),
        scratch_shapes=[
            pltpu.VMEM((far.shape[0], columns, CHUNK), BF16),
            pltpu.VMEM((columns, edge_src.shape[1]), F32),
            pltpu.VMEM((2, columns, edge_src.shape[1]), BF16),
            pltpu.SemaphoreType.DMA((2,)),
        ],
        compiler_params=pltpu.CompilerParams(vmem_limit_bytes=VMEM_LIMIT),
    )(
        edge_src,
        edge_dst,
        edge_rel,
        entity_emb,
        far,
        in_weight,
        out_weight,
        loop_weight,
        loop_rel[None],
        local_head,
        mixed,
    )

    parts = lax.all_to_all(heads, BOTH, 0, 0, tiled=True).reshape(devices, share, columns)
    own_heads = jnp.sum(parts.astype(F32), axis=0).astype(BF16)
    head_rows = lax.all_to_all(
        jnp.broadcast_to(own_heads[None], (devices, share, columns)), BOTH, 0, 0
    ).reshape(padded, columns)[:queries]
    query_factor = jnp.dot(
        jnp.take(relation_emb, query_rel, axis=0), rel_weight, preferred_element_type=F32
    )

    scores, weighted, stats = pl.pallas_call(
        score_kernel,
        out_shape=(
            jax.ShapeDtypeStruct((queries, rows_dev), F32),
            jax.ShapeDtypeStruct((queries, columns), BF16),
            jax.ShapeDtypeStruct((16, queries), BF16),
        ),
        compiler_params=pltpu.CompilerParams(vmem_limit_bytes=VMEM_LIMIT),
    )(head_rows, query_factor, hidden)

    split = weighted.reshape(copies, batch_rows, columns)
    split = jnp.pad(split, ((0, 0), (0, share * groups - batch_rows), (0, 0)))
    split = split.reshape(copies, groups, share, columns).transpose(1, 0, 2, 3)
    split = split.reshape(devices, share * columns)
    figures = jnp.broadcast_to(stats[:4].reshape(1, 4 * queries), (devices, 4 * queries))
    payload = jnp.concatenate([split, figures], axis=1).reshape(devices, -1, 128)
    received = lax.all_to_all(payload, BOTH, 0, 0).reshape(devices, -1)
    sums = received[:, : share * columns].reshape(devices, share, columns).astype(F32)
    figures = received[:, share * columns :].reshape(devices, 4, queries).astype(F32)
    tops = figures[:, 0] + figures[:, 1]
    totals = figures[:, 2] + figures[:, 3]
    row_top = jnp.max(tops, axis=0)
    scale = jnp.exp(tops - row_top)
    row_total = jnp.sum(totals * scale, axis=0)
    factor = jnp.pad(
        (scale / row_total).reshape(devices, copies, batch_rows),
        ((0, 0), (0, 0), (0, share * groups - batch_rows)),
    ).reshape(devices, -1)
    own_factor = lax.dynamic_slice_in_dim(
        factor, (member * groups + group) * share, share, 1
    )
    own_expected = jnp.sum(sums * own_factor[:, :, None], axis=0)
    expected_tail = lax.all_to_all(
        jnp.broadcast_to(own_expected[None], (groups, share, columns)), "ent", 0, 0
    ).reshape(groups * share, columns)[:batch_rows]
    log_probs = scores - (row_top + jnp.log(row_total))[:, None]
    return (log_probs, expected_tail)


def solution(mesh):
    placed = (
        P(("ent", "rep"), None),
        P(),
        P(),
        P(),
        P(),
        P(),
        P(),
        P(("ent", "rep"), None),
        P(("ent", "rep"), None),
        P(("ent", "rep"), None),
        P("ent", None),
        P(),
        P(),
    )
    return jax.shard_map(
        body,
        mesh=mesh,
        in_specs=placed,
        out_specs=(P(None, ("ent", "rep")), P("rep", None)),
        check_vma=False,
    )
```

```python
import functools

import jax
import jax.numpy as jnp
from jax import lax
from jax.experimental import pallas as pl
from jax.experimental.pallas import tpu as pltpu
from jax.sharding import PartitionSpec as P

BLK = 128
CHUNK = 1024
BF16 = jnp.bfloat16
F32 = jnp.float32
BOTH = ("ent", "rep")
NT = (((1,), (1,)), ((), ()))
TN = (((0,), (0,)), ((), ()))
VMEM_LIMIT = 56 * 2**20
STEP = 2
AHEAD = 5


def one_hot(index, rows):
    where = lax.broadcasted_iota(jnp.int16, (rows, index.shape[1]), 0) == index.astype(jnp.int16)
    return jnp.where(where, jnp.asarray(1, BF16), jnp.asarray(0, BF16))


def one_hot_wide(index, rows):
    where = lax.broadcasted_iota(jnp.int32, (rows, index.shape[1]), 0) == index
    return where.astype(F32).astype(BF16)


def order_blocks(head_ref, first_block, blocks, flag_ref, order_ref):
    def clear(b, carry):
        flag_ref[b] = 0
        return carry

    def mark(q, carry):
        block = lax.shift_right_arithmetic(head_ref[q], BLK.bit_length() - 1) - first_block
        flag_ref[jnp.where((block >= 0) & (block < blocks), block, blocks)] = 1
        return carry

    def place(wanted, b, position):
        taken = flag_ref[b] == wanted
        order_ref[jnp.where(taken, position, blocks + 1)] = b
        return position + taken.astype(jnp.int32)

    lax.fori_loop(0, blocks, clear, 0)
    lax.fori_loop(0, head_ref.shape[0], mark, 0, unroll=8)
    found = lax.fori_loop(0, blocks, functools.partial(place, 1), 0)
    lax.fori_loop(0, blocks, functools.partial(place, 0), found)
    order_ref[blocks] = found


def head_steps(order_ref, blocks):
    return (order_ref[blocks] + STEP - 1) // STEP


def near_kernel(part, ahead, *refs):
    if part == 0:
        base_ref, head_ref, src_ref, rel_ref, near_ref, relation_ref = refs[:6]
        mixed_ref, order_ref, held_ref, sems, flag_ref = refs[6:]
    else:
        order_ref, src_ref, rel_ref, near_ref, relation_ref, _ = refs[:6]
        mixed_ref, held_ref, sems = refs[6:]
    blocks = src_ref.shape[0]
    rows_dev = near_ref.shape[1]
    steps = blocks // STEP
    if part == 0:
        order_blocks(head_ref, base_ref[0], blocks, flag_ref, order_ref)
        start, stop = 0, 1
    else:
        middle = jnp.maximum(head_steps(order_ref, blocks), ahead)
        start, stop = (1, middle) if part == 1 else (middle, steps)
    count = stop - start

    def save(step, slot):
        return pltpu.make_async_copy(held_ref.at[slot], mixed_ref.at[step], sems.at[slot])

    def one_step(i, carry):
        slot = lax.rem(i, 2)

        @pl.when(i >= 2)
        def _():
            save(start + i - 2, slot).wait()

        for u in range(STEP):
            block = order_ref[(start + i) * STEP + u]
            src = src_ref[pl.ds(block, 1), :]
            rel = rel_ref[pl.ds(block, 1), :]
            gathered = jnp.dot(near_ref[...], one_hot(src, rows_dev), preferred_element_type=F32)
            relation = jnp.dot(
                relation_ref[...],
                one_hot(rel, relation_ref.shape[1]),
                preferred_element_type=F32,
            )
            mixed = jnp.where(src < rows_dev, gathered, 1.0) * relation
            held_ref[slot, u] = mixed.astype(BF16)
        save(start + i, slot).start()
        return carry

    lax.fori_loop(0, count, one_step, 0)
    for back in (2, 1):

        @pl.when(jnp.int32(count) >= back)
        def _():
            save(start + count - back, lax.rem(jnp.int32(count) - back + 2, 2)).wait()


def far_kernel(
    half_rel,
    last,
    order_ref,
    src_ref,
    dst_ref,
    rel_ref,
    emb_ref,
    far_ref,
    in_ref,
    out_ref,
    loop_ref,
    loop_rel_ref,
    extra_ref,
    mixed_ref,
    hidden_ref,
    *rest,
):
    far_t_ref, gathered_ref, agg_ref, held_ref, sems = rest[-5:]
    rows_dev = emb_ref.shape[0]
    blocks = src_ref.shape[0]
    far_chunks = far_ref.shape[0]
    middle = head_steps(order_ref, blocks)
    start, stop = (middle, blocks // STEP) if last else (0, middle)

    def load(step, slot):
        return pltpu.make_async_copy(mixed_ref.at[step], held_ref.at[slot], sems.at[slot])

    @pl.when(start < stop)
    def _():
        load(start, 0).start()

    def turn(j, carry):
        far_t_ref[j] = jnp.transpose(far_ref[j])
        return carry

    lax.fori_loop(0, far_chunks, turn, 0)
    hidden_ref[...] = extra_ref[...] if last else jnp.zeros_like(hidden_ref)

    def look_up(src, u):
        if far_chunks == 1:
            return jnp.dot(
                far_t_ref[0], one_hot(src - rows_dev, CHUNK), preferred_element_type=F32
            )
        gathered_ref[u] = jnp.zeros(gathered_ref.shape[1:], F32)

        def one_chunk(j, carry):
            gathered_ref[u] += jnp.dot(
                far_t_ref[j],
                one_hot(src - rows_dev - j * CHUNK, CHUNK),
                preferred_element_type=F32,
            )
            return carry

        lax.fori_loop(0, far_chunks, one_chunk, 0)
        return gathered_ref[u]

    def one_step(i, carry):
        slot = lax.rem(i, 2)

        @pl.when(start + i + 1 < stop)
        def _():
            load(start + i + 1, 1 - slot).start()

        load(start + i, slot).wait()
        rows = [pl.ds(order_ref[(start + i) * STEP + u], 1) for u in range(STEP)]
        srcs = [src_ref[row, :] for row in rows]
        found = [look_up(src, u) for u, src in enumerate(srcs)]
        composed = [
            (jnp.where(srcs[u] < rows_dev, 1.0, found[u]) * held_ref[slot, u].astype(F32)).astype(
                BF16
            )
            for u in range(STEP)
        ]
        for u, row in enumerate(rows):
            key = dst_ref[row, :] + jnp.where(rel_ref[row, :] >= half_rel, BLK, 0)
            selector = (
                lax.broadcasted_iota(jnp.int32, (2 * BLK, key.shape[1]), 0) == key
            ).astype(F32)
            counts = jnp.sum(selector, axis=1, keepdims=True)
            sums = lax.dot_general(
                selector.astype(BF16), composed[u], NT, preferred_element_type=F32
            )
            agg = (sums / jnp.maximum(counts, 1.0)).astype(BF16)
            here = pl.ds(pl.multiple_of(((start + i) * STEP + u) * BLK, BLK), BLK)
            agg_ref[0, here, :] = agg[:BLK]
            agg_ref[1, here, :] = agg[BLK:]
        return carry

    lax.fori_loop(0, stop - start, one_step, 0)

    def finish(i, carry):
        here = pl.ds(pl.multiple_of(i * STEP * BLK, STEP * BLK), STEP * BLK)
        rows = [
            pl.ds(pl.multiple_of(order_ref[i * STEP + u] * BLK, BLK), BLK) for u in range(STEP)
        ]
        own = jnp.concatenate([emb_ref[row, :] for row in rows], axis=0)
        own = (own.astype(F32) * loop_rel_ref[...]).astype(BF16)
        preact = jnp.dot(agg_ref[0, here, :], in_ref[...], preferred_element_type=F32)
        preact += jnp.dot(agg_ref[1, here, :], out_ref[...], preferred_element_type=F32)
        preact += jnp.dot(own, loop_ref[...], preferred_element_type=F32)
        hidden = jnp.tanh(preact).astype(BF16)
        for u, row in enumerate(rows):
            hidden_ref[row, :] = hidden[u * BLK : (u + 1) * BLK]
        return carry

    lax.fori_loop(start, stop, finish, 0)
    if not last:
        picks = one_hot_wide(extra_ref[...], rows_dev)
        rest[0][...] = lax.dot_general(
            picks, hidden_ref[...], TN, preferred_element_type=F32
        ).astype(BF16)


def pick_kernel(index_ref, emb_ref, offered_ref):
    picks = one_hot_wide(index_ref[...], emb_ref.shape[0])
    offered_ref[...] = lax.dot_general(
        picks, emb_ref[...], TN, preferred_element_type=F32
    ).astype(BF16)


SMEM = pl.BlockSpec(memory_space=pltpu.SMEM)
WHOLE = pl.BlockSpec(memory_space=pltpu.VMEM)
HBM = pl.BlockSpec(memory_space=pltpu.HBM)


def near_call(part, ahead, src, rel, near, relation, more):
    columns, edges = near.shape[0], src.shape[1]
    blocks = src.shape[0]
    steps = blocks // STEP
    count = STEP * (1, ahead - 1, steps - ahead)[part]
    flops = 2 * count * edges * columns * (near.shape[1] + relation.shape[1])
    mixed_type = jax.ShapeDtypeStruct((steps, STEP, columns, edges), BF16)
    order_type = jax.ShapeDtypeStruct((blocks + 2,), jnp.int32)
    scratch = [
        pltpu.VMEM((2, STEP, columns, edges), BF16),
        pltpu.SemaphoreType.DMA((2,)),
    ]
    settings = dict(
        compiler_params=pltpu.CompilerParams(vmem_limit_bytes=VMEM_LIMIT),
        cost_estimate=pl.CostEstimate(
            flops=flops, bytes_accessed=2 * count * edges * columns, transcendentals=0
        ),
    )
    if part == 0:
        return pl.pallas_call(
            functools.partial(near_kernel, part, ahead),
            out_shape=(mixed_type, order_type),
            in_specs=[SMEM] * 2 + [WHOLE] * 4,
            out_specs=(HBM, SMEM),
            scratch_shapes=scratch + [pltpu.SMEM((blocks + 1,), jnp.int32)],
            **settings,
        )(*more, src, rel, near, relation)
    mixed, order = more
    return pl.pallas_call(
        functools.partial(near_kernel, part, ahead),
        out_shape=mixed_type,
        in_specs=[SMEM] + [WHOLE] * 4 + [HBM],
        out_specs=HBM,
        input_output_aliases={5: 0},
        scratch_shapes=scratch,
        **settings,
    )(order, src, rel, near, relation, mixed)


def far_call(half_rel, last, order, edges, emb, far, weights, extra, mixed, padded):
    rows_dev, columns = emb.shape
    blocks, width = edges[0].shape
    hidden_type = jax.ShapeDtypeStruct((rows_dev, columns), BF16)
    heads_type = jax.ShapeDtypeStruct((padded, columns), BF16)
    return pl.pallas_call(
        functools.partial(far_kernel, half_rel, last),
        out_shape=hidden_type if last else (hidden_type, heads_type),
        in_specs=[SMEM] + [WHOLE] * 10 + [HBM],
        out_specs=WHOLE if last else (WHOLE, WHOLE),
        scratch_shapes=[
            pltpu.VMEM((far.shape[0], columns, CHUNK), BF16),
            pltpu.VMEM((STEP, columns, width if far.shape[0] > 1 else 128), F32),
            pltpu.VMEM((2, rows_dev, columns), BF16),
            pltpu.VMEM((2, STEP, columns, width), BF16),
            pltpu.SemaphoreType.DMA((2,)),
        ],
        compiler_params=pltpu.CompilerParams(vmem_limit_bytes=VMEM_LIMIT),
        cost_estimate=pl.CostEstimate(
            flops=blocks * width * columns * far.shape[0] * CHUNK,
            bytes_accessed=blocks * width * columns,
            transcendentals=0,
        ),
    )(order, *edges, emb, far, *weights, extra, mixed)


def score_kernel(heads_ref, rel_ref, hidden_ref, scores_ref, weighted_ref, stats_ref):
    query = (heads_ref[...].astype(F32) * rel_ref[...]).astype(BF16)
    scores = lax.dot_general(query, hidden_ref[...], NT, preferred_element_type=F32)
    scores_ref[...] = scores
    top = jnp.max(scores, axis=1, keepdims=True)
    high = top.astype(BF16)
    low = (top - high.astype(F32)).astype(BF16)
    top = high.astype(F32) + low.astype(F32)
    weights = jnp.exp(scores - top)
    total = jnp.sum(weights, axis=1, keepdims=True)
    weighted_ref[...] = jnp.dot(
        weights.astype(BF16), hidden_ref[...], preferred_element_type=F32
    ).astype(BF16)
    total_high = total.astype(BF16)
    total_low = (total - total_high.astype(F32)).astype(BF16)
    lanes = lax.broadcasted_iota(jnp.int32, (query.shape[0], 128), 1)
    wide = jnp.where(lanes == 0, high.astype(F32), 0.0)
    wide = jnp.where(lanes == 1, low.astype(F32), wide)
    wide = jnp.where(lanes == 2, total_high.astype(F32), wide)
    wide = jnp.where(lanes == 3, total_low.astype(F32), wide)
    stats_ref[...] = jnp.transpose(wide)[: stats_ref.shape[0]].astype(BF16)


def body(
    entity_emb,
    relation_emb,
    in_weight,
    out_weight,
    loop_weight,
    rel_weight,
    loop_rel,
    edge_src,
    edge_dst,
    edge_rel,
    export_rows,
    query_head,
    query_rel,
):
    groups = lax.axis_size("ent")
    copies = lax.axis_size("rep")
    devices = groups * copies
    group = lax.axis_index("ent")
    member = lax.axis_index("rep")
    device = group * copies + member
    rows_dev, columns = entity_emb.shape
    queries = query_head.shape[0]
    batch_rows = queries // copies
    share = -(-batch_rows // groups)
    padded = share * devices

    blocks = edge_src.shape[0]
    relations = relation_emb.shape[0]
    rel_count = -(-relations // 256) * 256
    relation_t = jnp.pad(relation_emb, ((0, rel_count - relations), (0, 0))).T
    near_t = entity_emb.T
    ahead = min(AHEAD, blocks // STEP)

    slots = export_rows.shape[1]
    offered = pl.pallas_call(
        pick_kernel,
        out_shape=jax.ShapeDtypeStruct((slots, columns), BF16),
        compiler_params=pltpu.CompilerParams(vmem_limit_bytes=VMEM_LIMIT),
    )(export_rows - member * rows_dev, entity_emb)
    pieces = lax.all_to_all(offered, "rep", 0, 0, tiled=True)
    mixed, order = near_call(
        0, ahead, edge_src, edge_rel, near_t, relation_t, ((device * blocks)[None], query_head)
    )
    mine = jnp.sum(
        pieces.reshape(copies, slots // copies, columns).astype(F32), axis=0
    ).astype(BF16)
    mine, mixed = lax.optimization_barrier((mine, mixed))
    spread = jnp.broadcast_to(mine[None], (devices,) + mine.shape)
    table = lax.all_to_all(spread, BOTH, 0, 0).reshape(groups * slots, columns)
    mixed = near_call(1, ahead, edge_src, edge_rel, near_t, relation_t, (mixed, order))
    far_count = -(-(groups * slots) // CHUNK) * CHUNK
    far = jnp.pad(table, ((0, far_count - groups * slots), (0, 0)))
    far = far.reshape(far_count // CHUNK, CHUNK, columns)

    local_head = jnp.pad(
        query_head - device * rows_dev, (0, padded - queries), constant_values=-1
    )[None]
    weights = (in_weight, out_weight, loop_weight, loop_rel[None])
    edges = (edge_src, edge_dst, edge_rel)
    half_rel = relations // 2
    hidden, heads = far_call(
        half_rel, False, order, edges, entity_emb, far, weights, local_head, mixed, padded
    )
    heads, mixed = lax.optimization_barrier((heads, mixed))
    parts = lax.all_to_all(heads, BOTH, 0, 0, tiled=True).reshape(devices, share, columns)
    mixed = near_call(2, ahead, edge_src, edge_rel, near_t, relation_t, (mixed, order))
    own_heads = jnp.sum(parts.astype(F32), axis=0).astype(BF16)
    own_heads, mixed = lax.optimization_barrier((own_heads, mixed))
    head_rows = lax.all_to_all(
        jnp.broadcast_to(own_heads[None], (devices, share, columns)), BOTH, 0, 0
    ).reshape(padded, columns)[:queries]
    hidden = far_call(
        half_rel, True, order, edges, entity_emb, far, weights, hidden, mixed, padded
    )
    query_factor = jnp.dot(
        jnp.take(relation_emb, query_rel, axis=0), rel_weight, preferred_element_type=F32
    )

    scores, weighted, stats = pl.pallas_call(
        score_kernel,
        out_shape=(
            jax.ShapeDtypeStruct((queries, rows_dev), F32),
            jax.ShapeDtypeStruct((queries, columns), BF16),
            jax.ShapeDtypeStruct((16, queries), BF16),
        ),
        compiler_params=pltpu.CompilerParams(vmem_limit_bytes=VMEM_LIMIT),
    )(head_rows, query_factor, hidden)

    split = weighted.reshape(copies, batch_rows, columns)
    split = jnp.pad(split, ((0, 0), (0, share * groups - batch_rows), (0, 0)))
    split = split.reshape(copies, groups, share, columns).transpose(1, 0, 2, 3)
    split = split.reshape(devices, share * columns)
    figures = jnp.broadcast_to(stats[:4].reshape(1, 4 * queries), (devices, 4 * queries))
    payload = jnp.concatenate([split, figures], axis=1).reshape(devices, -1, 128)
    received = lax.all_to_all(payload, BOTH, 0, 0).reshape(devices, -1)
    sums = received[:, : share * columns].reshape(devices, share, columns).astype(F32)
    figures = received[:, share * columns :].reshape(devices, 4, queries).astype(F32)
    tops = figures[:, 0] + figures[:, 1]
    totals = figures[:, 2] + figures[:, 3]
    row_top = jnp.max(tops, axis=0)
    scale = jnp.exp(tops - row_top)
    row_total = jnp.sum(totals * scale, axis=0)
    factor = jnp.pad(
        (scale / row_total).reshape(devices, copies, batch_rows),
        ((0, 0), (0, 0), (0, share * groups - batch_rows)),
    ).reshape(devices, -1)
    own_factor = lax.dynamic_slice_in_dim(
        factor, (member * groups + group) * share, share, 1
    )
    own_expected = jnp.sum(sums * own_factor[:, :, None], axis=0)
    expected_tail = lax.all_to_all(
        jnp.broadcast_to(own_expected[None], (groups, share, columns)), "ent", 0, 0
    ).reshape(groups * share, columns)[:batch_rows]
    log_probs = scores - (row_top + jnp.log(row_total))[:, None]
    return (log_probs, expected_tail)


def solution(mesh):
    placed = (
        P(("ent", "rep"), None),
        P(),
        P(),
        P(),
        P(),
        P(),
        P(),
        P(("ent", "rep"), None),
        P(("ent", "rep"), None),
        P(("ent", "rep"), None),
        P("ent", None),
        P(),
        P(),
    )
    return jax.shard_map(
        body,
        mesh=mesh,
        in_specs=placed,
        out_specs=(P(None, ("ent", "rep")), P("rep", None)),
        check_vma=False,
    )
```

```python
import functools

import jax
import jax.numpy as jnp
from jax import lax
from jax.experimental import pallas as pl
from jax.experimental.pallas import tpu as pltpu
from jax.sharding import PartitionSpec as P

BLK = 128
CHUNK = 1024
BF16 = jnp.bfloat16
F32 = jnp.float32
BOTH = ("ent", "rep")
NT = (((1,), (1,)), ((), ()))
TN = (((0,), (0,)), ((), ()))
VMEM_LIMIT = 56 * 2**20
STEP = 2
AHEAD = 5


def one_hot(index, rows):
    where = lax.broadcasted_iota(jnp.int16, (rows, index.shape[1]), 0) == index.astype(jnp.int16)
    return jnp.where(where, jnp.asarray(1, BF16), jnp.asarray(0, BF16))


def one_hot_wide(index, rows):
    where = lax.broadcasted_iota(jnp.int32, (rows, index.shape[1]), 0) == index
    return where.astype(F32).astype(BF16)


def is_outside(src, rows_dev):
    return jnp.where(src < rows_dev, 0.0, 1.0).astype(BF16)


def order_blocks(head_ref, first_block, blocks, flag_ref, order_ref):
    def clear(b, carry):
        flag_ref[b] = 0
        return carry

    def mark(q, carry):
        block = lax.shift_right_arithmetic(head_ref[q], BLK.bit_length() - 1) - first_block
        flag_ref[jnp.where((block >= 0) & (block < blocks), block, blocks)] = 1
        return carry

    def place(wanted, b, position):
        taken = flag_ref[b] == wanted
        order_ref[jnp.where(taken, position, blocks + 1)] = b
        return position + taken.astype(jnp.int32)

    lax.fori_loop(0, blocks, clear, 0)
    lax.fori_loop(0, head_ref.shape[0], mark, 0, unroll=8)
    found = lax.fori_loop(0, blocks, functools.partial(place, 1), 0)
    lax.fori_loop(0, blocks, functools.partial(place, 0), found)
    order_ref[blocks] = found


def middle_step(order_ref, blocks, ahead):
    return jnp.maximum((order_ref[blocks] + STEP - 1) // STEP, ahead)


def near_kernel(rest, ahead, *refs):
    if rest:
        order_ref, src_ref, rel_ref, near_ref, relation_ref, _ = refs[:6]
        mixed_ref, held_ref, sems = refs[6:]
    else:
        base_ref, head_ref, src_ref, rel_ref, near_ref, relation_ref = refs[:6]
        mixed_ref, order_ref, held_ref, sems, flag_ref = refs[6:]
    blocks = src_ref.shape[0]
    rows_dev = near_ref.shape[1]
    steps = blocks // STEP
    if not rest:
        order_blocks(head_ref, base_ref[0], blocks, flag_ref, order_ref)
    middle = middle_step(order_ref, blocks, ahead)
    start, stop = (middle, steps) if rest else (0, middle)
    count = stop - start

    def save(step, slot):
        return pltpu.make_async_copy(held_ref.at[slot], mixed_ref.at[step], sems.at[slot])

    def one_step(i, carry):
        slot = lax.rem(i, 2)

        @pl.when(i >= 2)
        def _():
            save(start + i - 2, slot).wait()

        for u in range(STEP):
            block = order_ref[(start + i) * STEP + u]
            src = src_ref[pl.ds(block, 1), :]
            rel = rel_ref[pl.ds(block, 1), :]
            gathered = jnp.dot(near_ref[...], one_hot(src, rows_dev), preferred_element_type=F32)
            relation = jnp.dot(
                relation_ref[...],
                one_hot(rel, relation_ref.shape[1]),
                preferred_element_type=F32,
            )
            is_far = is_outside(src, rows_dev)
            held_ref[slot, u] = (gathered.astype(BF16) + is_far) * relation.astype(BF16)
        save(start + i, slot).start()
        return carry

    lax.fori_loop(0, count, one_step, 0)
    for back in (2, 1):

        @pl.when(count >= back)
        def _():
            save(start + count - back, lax.rem(count - back, 2)).wait()


def far_kernel(
    half_rel,
    last,
    ahead,
    base_ref,
    order_ref,
    src_ref,
    dst_ref,
    rel_ref,
    emb_ref,
    far_ref,
    in_ref,
    out_ref,
    loop_ref,
    loop_rel_ref,
    *rest,
):
    far_t_ref, gathered_ref, agg_ref, held_ref, sems = rest[-5:]
    if last:
        before_ref, query_rel_ref, relation_ref, rel_weight_ref = rest[:4]
        mixed_ref, hidden_ref, factor_ref = rest[4:7]
    else:
        head_ref, mixed_ref, hidden_ref, heads_ref = rest[:4]
    rows_dev = emb_ref.shape[0]
    blocks = src_ref.shape[0]
    far_chunks = far_ref.shape[0]
    middle = middle_step(order_ref, blocks, ahead)
    start, stop = (middle, blocks // STEP) if last else (0, middle)

    def load(step, slot):
        return pltpu.make_async_copy(mixed_ref.at[step], held_ref.at[slot], sems.at[slot])

    @pl.when(start < stop)
    def _():
        load(start, 0).start()

    def turn(j, carry):
        far_t_ref[j] = jnp.transpose(far_ref[j])
        return carry

    lax.fori_loop(0, far_chunks, turn, 0)
    hidden_ref[...] = before_ref[...] if last else jnp.zeros_like(hidden_ref)

    def look_up(src, u):
        if far_chunks == 1:
            return jnp.dot(
                far_t_ref[0], one_hot(src - rows_dev, CHUNK), preferred_element_type=F32
            )
        gathered_ref[u] = jnp.zeros(gathered_ref.shape[1:], F32)

        def one_chunk(j, carry):
            gathered_ref[u] += jnp.dot(
                far_t_ref[j],
                one_hot(src - rows_dev - j * CHUNK, CHUNK),
                preferred_element_type=F32,
            )
            return carry

        lax.fori_loop(0, far_chunks, one_chunk, 0)
        return gathered_ref[u]

    def one_step(i, carry):
        slot = lax.rem(i, 2)

        @pl.when(start + i + 1 < stop)
        def _():
            load(start + i + 1, 1 - slot).start()

        load(start + i, slot).wait()
        rows = [pl.ds(order_ref[(start + i) * STEP + u], 1) for u in range(STEP)]
        srcs = [src_ref[row, :] for row in rows]
        found = [look_up(src, u) for u, src in enumerate(srcs)]
        composed = [
            (found[u].astype(BF16) + (1 - is_outside(srcs[u], rows_dev))) * held_ref[slot, u]
            for u in range(STEP)
        ]
        for u, row in enumerate(rows):
            key = dst_ref[row, :] + jnp.where(rel_ref[row, :] >= half_rel, BLK, 0)
            selector = one_hot(key, 2 * BLK)
            counts = selector[:, :128]
            for lane in range(128, selector.shape[1], 128):
                counts = counts + selector[:, lane : lane + 128]
            counts = jnp.sum(counts.astype(F32), axis=1, keepdims=True)
            sums = lax.dot_general(selector, composed[u], NT, preferred_element_type=F32)
            agg = (sums * (1.0 / jnp.maximum(counts, 1.0))).astype(BF16)
            here = pl.ds(pl.multiple_of(((start + i) * STEP + u) * BLK, BLK), BLK)
            agg_ref[0, here, :] = agg[:BLK]
            agg_ref[1, here, :] = agg[BLK:]
        return carry

    lax.fori_loop(0, stop - start, one_step, 0)

    def finish(i, carry):
        here = pl.ds(pl.multiple_of(i * STEP * BLK, STEP * BLK), STEP * BLK)
        rows = [
            pl.ds(pl.multiple_of(order_ref[i * STEP + u] * BLK, BLK), BLK) for u in range(STEP)
        ]
        own = jnp.concatenate([emb_ref[row, :] for row in rows], axis=0)
        own = (own.astype(F32) * loop_rel_ref[...]).astype(BF16)
        preact = jnp.dot(agg_ref[0, here, :], in_ref[...], preferred_element_type=F32)
        preact += jnp.dot(agg_ref[1, here, :], out_ref[...], preferred_element_type=F32)
        preact += jnp.dot(own, loop_ref[...], preferred_element_type=F32)
        hidden = jnp.tanh(preact).astype(BF16)
        for u, row in enumerate(rows):
            hidden_ref[row, :] = hidden[u * BLK : (u + 1) * BLK]
        return carry

    lax.fori_loop(start, stop, finish, 0)
    if last:
        picks = one_hot(query_rel_ref[...], relation_ref.shape[1])
        rows = lax.dot_general(
            picks, relation_ref[...], (((0,), (1,)), ((), ())), preferred_element_type=F32
        )
        factor_ref[...] = jnp.dot(
            rows.astype(BF16), rel_weight_ref[...], preferred_element_type=F32
        )
    else:
        picks = one_hot_wide(head_ref[...] - base_ref[0] * BLK, rows_dev)
        heads_ref[...] = lax.dot_general(
            picks, hidden_ref[...], TN, preferred_element_type=F32
        ).astype(BF16)


def pick_kernel(base_ref, index_ref, emb_ref, offered_ref):
    picks = one_hot(index_ref[...] - base_ref[0], emb_ref.shape[0])
    offered_ref[...] = lax.dot_general(
        picks, emb_ref[...], TN, preferred_element_type=F32
    ).astype(BF16)


SMEM = pl.BlockSpec(memory_space=pltpu.SMEM)
WHOLE = pl.BlockSpec(memory_space=pltpu.VMEM)
HBM = pl.BlockSpec(memory_space=pltpu.HBM)


def near_call(rest, ahead, src, rel, near, relation, more):
    columns, edges = near.shape[0], src.shape[1]
    blocks = src.shape[0]
    steps = blocks // STEP
    count = STEP * (steps - ahead if rest else ahead)
    flops = 2 * count * edges * columns * (near.shape[1] + relation.shape[1])
    mixed_type = jax.ShapeDtypeStruct((steps, STEP, columns, edges), BF16)
    order_type = jax.ShapeDtypeStruct((blocks + 2,), jnp.int32)
    scratch = [
        pltpu.VMEM((2, STEP, columns, edges), BF16),
        pltpu.SemaphoreType.DMA((2,)),
    ]
    settings = dict(
        compiler_params=pltpu.CompilerParams(vmem_limit_bytes=VMEM_LIMIT),
        cost_estimate=pl.CostEstimate(
            flops=flops, bytes_accessed=2 * count * edges * columns, transcendentals=0
        ),
    )
    if not rest:
        return pl.pallas_call(
            functools.partial(near_kernel, rest, ahead),
            out_shape=(mixed_type, order_type),
            in_specs=[SMEM] * 2 + [WHOLE] * 4,
            out_specs=(HBM, SMEM),
            scratch_shapes=scratch + [pltpu.SMEM((blocks + 1,), jnp.int32)],
            **settings,
        )(*more, src, rel, near, relation)
    mixed, order = more
    return pl.pallas_call(
        functools.partial(near_kernel, rest, ahead),
        out_shape=mixed_type,
        in_specs=[SMEM] + [WHOLE] * 4 + [HBM],
        out_specs=HBM,
        input_output_aliases={5: 0},
        scratch_shapes=scratch,
        **settings,
    )(order, src, rel, near, relation, mixed)


def far_call(half_rel, last, ahead, scalars, edges, emb, far, weights, more, mixed, second):
    rows_dev, columns = emb.shape
    blocks, width = edges[0].shape
    return pl.pallas_call(
        functools.partial(far_kernel, half_rel, last, ahead),
        out_shape=(jax.ShapeDtypeStruct((rows_dev, columns), BF16), second),
        in_specs=[SMEM] * 2 + [WHOLE] * (9 + len(more)) + [HBM],
        out_specs=(WHOLE, WHOLE),
        scratch_shapes=[
            pltpu.VMEM((far.shape[0], columns, CHUNK), BF16),
            pltpu.VMEM((STEP, columns, width if far.shape[0] > 1 else 128), F32),
            pltpu.VMEM((2, rows_dev, columns), BF16),
            pltpu.VMEM((2, STEP, columns, width), BF16),
            pltpu.SemaphoreType.DMA((2,)),
        ],
        compiler_params=pltpu.CompilerParams(vmem_limit_bytes=VMEM_LIMIT),
        cost_estimate=pl.CostEstimate(
            flops=blocks * width * columns * far.shape[0] * CHUNK,
            bytes_accessed=blocks * width * columns,
            transcendentals=0,
        ),
    )(*scalars, *edges, emb, far, *weights, *more, mixed)


def score_kernel(heads_ref, rel_ref, hidden_ref, scores_ref, weighted_ref, stats_ref):
    query = (heads_ref[...].astype(F32) * rel_ref[...]).astype(BF16)
    scores = lax.dot_general(query, hidden_ref[...], NT, preferred_element_type=F32)
    scores_ref[...] = scores
    top = jnp.max(scores, axis=1, keepdims=True)
    high = top.astype(BF16)
    low = (top - high.astype(F32)).astype(BF16)
    top = high.astype(F32) + low.astype(F32)
    weights = jnp.exp(scores - top)
    total = jnp.sum(weights, axis=1, keepdims=True)
    weighted_ref[...] = jnp.dot(
        weights.astype(BF16), hidden_ref[...], preferred_element_type=F32
    ).astype(BF16)
    total_high = total.astype(BF16)
    total_low = (total - total_high.astype(F32)).astype(BF16)
    lanes = lax.broadcasted_iota(jnp.int32, (query.shape[0], 128), 1)
    wide = jnp.where(lanes == 0, high.astype(F32), 0.0)
    wide = jnp.where(lanes == 1, low.astype(F32), wide)
    wide = jnp.where(lanes == 2, total_high.astype(F32), wide)
    wide = jnp.where(lanes == 3, total_low.astype(F32), wide)
    stats_ref[...] = jnp.transpose(wide)[: stats_ref.shape[0]].astype(BF16)


def body(
    entity_emb,
    relation_emb,
    in_weight,
    out_weight,
    loop_weight,
    rel_weight,
    loop_rel,
    edge_src,
    edge_dst,
    edge_rel,
    export_rows,
    query_head,
    query_rel,
):
    groups = lax.axis_size("ent")
    copies = lax.axis_size("rep")
    devices = groups * copies
    group = lax.axis_index("ent")
    member = lax.axis_index("rep")
    device = group * copies + member
    rows_dev, columns = entity_emb.shape
    queries = query_head.shape[0]
    batch_rows = queries // copies
    share = -(-batch_rows // groups)
    padded = share * devices

    blocks = edge_src.shape[0]
    relations = relation_emb.shape[0]
    rel_count = -(-relations // 256) * 256
    relation_t = jnp.pad(relation_emb, ((0, rel_count - relations), (0, 0))).T
    near_t = entity_emb.T
    ahead = min(AHEAD, blocks // STEP)

    slots = export_rows.shape[1]
    offered = pl.pallas_call(
        pick_kernel,
        out_shape=jax.ShapeDtypeStruct((slots, columns), BF16),
        in_specs=[SMEM, WHOLE, WHOLE],
        out_specs=WHOLE,
        compiler_params=pltpu.CompilerParams(vmem_limit_bytes=VMEM_LIMIT),
    )((member * rows_dev)[None], export_rows, entity_emb)
    pieces = lax.all_to_all(offered, "rep", 0, 0, tiled=True)
    mine = jnp.sum(
        pieces.reshape(copies, slots // copies, columns).astype(F32), axis=0
    ).astype(BF16)
    mine, near_t = lax.optimization_barrier((mine, near_t))
    spread = jnp.broadcast_to(mine[None], (devices,) + mine.shape)
    table = lax.all_to_all(spread, BOTH, 0, 0).reshape(groups * slots, columns)
    base = (device * blocks)[None]
    mixed, order = near_call(
        False, ahead, edge_src, edge_rel, near_t, relation_t, (base, query_head)
    )
    far_count = -(-(groups * slots) // CHUNK) * CHUNK
    far = jnp.pad(table, ((0, far_count - groups * slots), (0, 0)))
    far = far.reshape(far_count // CHUNK, CHUNK, columns)

    heads_row = jnp.pad(query_head, (0, padded - queries), constant_values=-1)[None]
    weights = (in_weight, out_weight, loop_weight, loop_rel[None])
    edges = (edge_src, edge_dst, edge_rel)
    half_rel = relations // 2
    hidden, heads = far_call(
        half_rel,
        False,
        ahead,
        (base, order),
        edges,
        entity_emb,
        far,
        weights,
        (heads_row,),
        mixed,
        jax.ShapeDtypeStruct((padded, columns), BF16),
    )
    heads, mixed = lax.optimization_barrier((heads, mixed))
    parts = lax.all_to_all(heads, BOTH, 0, 0, tiled=True).reshape(devices, share, columns)
    mixed = near_call(True, ahead, edge_src, edge_rel, near_t, relation_t, (mixed, order))
    own_heads = jnp.sum(parts.astype(F32), axis=0).astype(BF16)
    own_heads, mixed = lax.optimization_barrier((own_heads, mixed))
    head_rows = lax.all_to_all(
        jnp.broadcast_to(own_heads[None], (devices, share, columns)), BOTH, 0, 0
    ).reshape(padded, columns)[:queries]
    hidden, query_factor = far_call(
        half_rel,
        True,
        ahead,
        (base, order),
        edges,
        entity_emb,
        far,
        weights,
        (hidden, query_rel[None], relation_t, rel_weight),
        mixed,
        jax.ShapeDtypeStruct((queries, columns), F32),
    )

    scores, weighted, stats = pl.pallas_call(
        score_kernel,
        out_shape=(
            jax.ShapeDtypeStruct((queries, rows_dev), F32),
            jax.ShapeDtypeStruct((queries, columns), BF16),
            jax.ShapeDtypeStruct((16, queries), BF16),
        ),
        compiler_params=pltpu.CompilerParams(vmem_limit_bytes=VMEM_LIMIT),
    )(head_rows, query_factor, hidden)

    split = weighted.reshape(copies, batch_rows, columns)
    split = jnp.pad(split, ((0, 0), (0, share * groups - batch_rows), (0, 0)))
    split = split.reshape(copies, groups, share, columns).transpose(1, 0, 2, 3)
    split = split.reshape(devices, share * columns)
    figures = jnp.broadcast_to(stats[:4].reshape(1, 4 * queries), (devices, 4 * queries))
    payload = jnp.concatenate([split, figures], axis=1).reshape(devices, -1, 128)
    received = lax.all_to_all(payload, BOTH, 0, 0).reshape(devices, -1)
    sums = received[:, : share * columns].reshape(devices, share, columns).astype(F32)
    figures = received[:, share * columns :].reshape(devices, 4, queries).astype(F32)
    tops = figures[:, 0] + figures[:, 1]
    totals = figures[:, 2] + figures[:, 3]
    row_top = jnp.max(tops, axis=0)
    scale = jnp.exp(tops - row_top)
    row_total = jnp.sum(totals * scale, axis=0)
    factor = jnp.pad(
        (scale / row_total).reshape(devices, copies, batch_rows),
        ((0, 0), (0, 0), (0, share * groups - batch_rows)),
    ).reshape(devices, -1)
    own_factor = lax.dynamic_slice_in_dim(
        factor, (member * groups + group) * share, share, 1
    )
    own_expected = jnp.sum(sums * own_factor[:, :, None], axis=0)
    expected_tail = lax.all_to_all(
        jnp.broadcast_to(own_expected[None], (groups, share, columns)), "ent", 0, 0
    ).reshape(groups * share, columns)[:batch_rows]
    log_probs = scores - (row_top + jnp.log(row_total))[:, None]
    return (log_probs, expected_tail)


def solution(mesh):
    placed = (
        P(("ent", "rep"), None),
        P(),
        P(),
        P(),
        P(),
        P(),
        P(),
        P(("ent", "rep"), None),
        P(("ent", "rep"), None),
        P(("ent", "rep"), None),
        P("ent", None),
        P(),
        P(),
    )
    return jax.shard_map(
        body,
        mesh=mesh,
        in_specs=placed,
        out_specs=(P(None, ("ent", "rep")), P("rep", None)),
        check_vma=False,
    )
```

```python
import functools

import jax
import jax.numpy as jnp
from jax import lax
from jax.experimental import pallas as pl
from jax.experimental.pallas import tpu as pltpu
from jax.sharding import PartitionSpec as P

BLK = 128
CHUNK = 1024
BF16 = jnp.bfloat16
F32 = jnp.float32
BOTH = ("ent", "rep")
NT = (((1,), (1,)), ((), ()))
TN = (((0,), (0,)), ((), ()))
VMEM_LIMIT = 56 * 2**20
STEP = 2
AHEAD = 6
SCORE_LIMIT = 24 * 2**20


def one_hot(index, rows):
    where = lax.broadcasted_iota(jnp.int16, (rows, index.shape[1]), 0) == index.astype(jnp.int16)
    return jnp.where(where, jnp.asarray(1, BF16), jnp.asarray(0, BF16))


def one_hot_wide(index, rows):
    where = lax.broadcasted_iota(jnp.int32, (rows, index.shape[1]), 0) == index
    return where.astype(F32).astype(BF16)


def is_outside(src, rows_dev):
    return jnp.where(src < rows_dev, 0.0, 1.0).astype(BF16)


def order_blocks(head_ref, first_block, blocks, order_ref):
    def mark(q, marks):
        block = lax.shift_right_arithmetic(head_ref[q], BLK.bit_length() - 1) - first_block
        inside = (block >= 0) & (block < blocks)
        return marks | jnp.where(inside, lax.shift_left(1, jnp.where(inside, block, 0)), 0)

    marks = lax.fori_loop(0, head_ref.shape[0], mark, jnp.int32(0), unroll=16)
    position = jnp.int32(0)
    for wanted in (1, 0):
        for b in range(blocks):
            taken = (lax.shift_right_logical(marks, b) & 1) == wanted
            order_ref[jnp.where(taken, position, blocks + 1)] = jnp.int32(b)
            position = position + taken.astype(jnp.int32)
        if wanted:
            found = position
    order_ref[blocks] = found


def middle_step(order_ref, blocks, ahead):
    return jnp.maximum((order_ref[blocks] + STEP - 1) // STEP, ahead)


def near_kernel(rest, ahead, *refs):
    if rest:
        order_ref, src_ref, rel_ref, near_ref, relation_ref, _ = refs[:6]
        mixed_ref, held_ref, sems = refs[6:]
    else:
        base_ref, head_ref, src_ref, rel_ref, near_ref, relation_ref = refs[:6]
        mixed_ref, order_ref, held_ref, sems = refs[6:]
    blocks = src_ref.shape[0]
    rows_dev = near_ref.shape[1]
    steps = blocks // STEP
    if not rest:
        order_blocks(head_ref, base_ref[0], blocks, order_ref)
    middle = middle_step(order_ref, blocks, ahead)
    start, stop = (middle, steps) if rest else (0, middle)
    count = stop - start

    def save(step, slot):
        return pltpu.make_async_copy(held_ref.at[slot], mixed_ref.at[step], sems.at[slot])

    def one_step(i, carry):
        slot = lax.rem(i, 2)

        @pl.when(i >= 2)
        def _():
            save(start + i - 2, slot).wait()

        for u in range(STEP):
            block = order_ref[(start + i) * STEP + u]
            src = src_ref[pl.ds(block, 1), :]
            rel = rel_ref[pl.ds(block, 1), :]
            gathered = jnp.dot(near_ref[...], one_hot(src, rows_dev), preferred_element_type=F32)
            relation = jnp.dot(
                relation_ref[...],
                one_hot(rel, relation_ref.shape[1]),
                preferred_element_type=F32,
            )
            is_far = is_outside(src, rows_dev)
            held_ref[slot, u] = (gathered.astype(BF16) + is_far) * relation.astype(BF16)
        save(start + i, slot).start()
        return carry

    lax.fori_loop(0, count, one_step, 0)
    for back in (2, 1):

        @pl.when(count >= back)
        def _():
            save(start + count - back, lax.rem(count - back, 2)).wait()


def far_kernel(
    half_rel,
    last,
    ahead,
    base_ref,
    order_ref,
    src_ref,
    dst_ref,
    rel_ref,
    emb_ref,
    far_ref,
    in_ref,
    out_ref,
    loop_ref,
    loop_rel_ref,
    *rest,
):
    far_t_ref, gathered_ref, agg_ref, held_ref, own_ref, made_ref, sems, own_sems, out_sems = rest[-9:]
    if last:
        query_rel_ref, relation_ref, rel_weight_ref, mixed_ref, _ = rest[:5]
        hidden_ref, factor_ref = rest[5:7]
    else:
        head_ref, mixed_ref, hidden_ref, heads_ref = rest[:4]
    blocks = src_ref.shape[0]
    rows_dev = blocks * BLK
    far_chunks = far_ref.shape[0]
    middle = middle_step(order_ref, blocks, ahead)
    start, stop = (middle, blocks // STEP) if last else (0, middle)

    def load(step, slot):
        return pltpu.make_async_copy(mixed_ref.at[step], held_ref.at[slot], sems.at[slot])

    def block_rows(step, u):
        return pl.ds(pl.multiple_of(order_ref[step * STEP + u] * BLK, BLK), BLK)

    def load_own(step, u):
        slot = lax.rem(step, 2)
        return pltpu.make_async_copy(
            emb_ref.at[block_rows(step, u)], own_ref.at[slot, u], own_sems.at[slot, u]
        )

    def give(step, u):
        rows = block_rows(step, u)
        return pltpu.make_async_copy(
            made_ref.at[rows], hidden_ref.at[rows], out_sems.at[step * STEP + u]
        )

    @pl.when(start < stop)
    def _():
        load(start, 0).start()

    def turn(j, carry):
        far_t_ref[j] = jnp.transpose(far_ref[j])
        return carry

    lax.fori_loop(0, far_chunks, turn, 0)
    if not last:
        made_ref[...] = jnp.zeros_like(made_ref)

    def look_up(src, u):
        if far_chunks == 1:
            return jnp.dot(
                far_t_ref[0], one_hot(src - rows_dev, CHUNK), preferred_element_type=F32
            )
        gathered_ref[u] = jnp.zeros(gathered_ref.shape[1:], F32)

        def one_chunk(j, carry):
            gathered_ref[u] += jnp.dot(
                far_t_ref[j],
                one_hot(src - rows_dev - j * CHUNK, CHUNK),
                preferred_element_type=F32,
            )
            return carry

        lax.fori_loop(0, far_chunks, one_chunk, 0)
        return gathered_ref[u]

    def finish(step, slot):
        own = own_ref[slot].reshape(STEP * BLK, own_ref.shape[-1])
        own = (own.astype(F32) * loop_rel_ref[...]).astype(BF16)
        preact = jnp.dot(agg_ref[0, slot], in_ref[...], preferred_element_type=F32)
        preact += jnp.dot(agg_ref[1, slot], out_ref[...], preferred_element_type=F32)
        preact += jnp.dot(own, loop_ref[...], preferred_element_type=F32)
        hidden = jnp.tanh(preact).astype(BF16)
        for u in range(STEP):
            made_ref[block_rows(step, u), :] = hidden[u * BLK : (u + 1) * BLK]

    def one_step(i, carry):
        slot = lax.rem(i, 2)
        step = start + i
        before = jnp.maximum(step - 1, start)

        @pl.when(i > 0)
        def _():
            for u in range(STEP):
                load_own(before, u).wait()

        for u in range(STEP):
            load_own(step, u).start()

        @pl.when(start + i + 1 < stop)
        def _():
            load(start + i + 1, 1 - slot).start()

        load(start + i, slot).wait()
        finish(before, lax.rem(step + 1, 2))
        rows = [pl.ds(order_ref[(start + i) * STEP + u], 1) for u in range(STEP)]
        srcs = [src_ref[row, :] for row in rows]
        found = [look_up(src, u) for u, src in enumerate(srcs)]
        composed = [
            (found[u].astype(BF16) + (1 - is_outside(srcs[u], rows_dev))) * held_ref[slot, u]
            for u in range(STEP)
        ]
        for u, row in enumerate(rows):
            key = dst_ref[row, :] + jnp.where(rel_ref[row, :] >= half_rel, BLK, 0)
            selector = one_hot(key, 2 * BLK)
            counts = selector[:, :128]
            for lane in range(128, selector.shape[1], 128):
                counts = counts + selector[:, lane : lane + 128]
            counts = jnp.sum(counts.astype(F32), axis=1, keepdims=True)
            sums = lax.dot_general(selector, composed[u], NT, preferred_element_type=F32)
            agg = (sums * (1.0 / jnp.maximum(counts, 1.0))).astype(BF16)
            here = pl.ds(u * BLK, BLK)
            agg_ref[0, lax.rem(step, 2), here, :] = agg[:BLK]
            agg_ref[1, lax.rem(step, 2), here, :] = agg[BLK:]

        @pl.when(i > 0)
        def _():
            for u in range(STEP):
                give(before, u).start()

        return carry

    lax.fori_loop(0, stop - start, one_step, 0)

    @pl.when(start < stop)
    def _():
        for u in range(STEP):
            load_own(stop - 1, u).wait()
        finish(stop - 1, lax.rem(stop - 1, 2))
        for u in range(STEP):
            give(stop - 1, u).start()

    if last:
        picks = one_hot(query_rel_ref[...], relation_ref.shape[1])
        rows = lax.dot_general(
            picks, relation_ref[...], (((0,), (1,)), ((), ())), preferred_element_type=F32
        )
        factor_ref[...] = jnp.dot(
            rows.astype(BF16), rel_weight_ref[...], preferred_element_type=F32
        )
    else:
        picks = one_hot_wide(head_ref[...] - base_ref[0] * BLK, rows_dev)
        heads_ref[...] = lax.dot_general(
            picks, made_ref[...], TN, preferred_element_type=F32
        ).astype(BF16)

    def gave(step, carry):
        for u in range(STEP):
            give(step, u).wait()
        return carry

    lax.fori_loop(start, stop, gave, 0)


def pick_kernel(base_ref, index_ref, emb_ref, offered_ref):
    picks = one_hot(index_ref[...] - base_ref[0], emb_ref.shape[0])
    offered_ref[...] = lax.dot_general(
        picks, emb_ref[...], TN, preferred_element_type=F32
    ).astype(BF16)


SMEM = pl.BlockSpec(memory_space=pltpu.SMEM)
WHOLE = pl.BlockSpec(memory_space=pltpu.VMEM)
HBM = pl.BlockSpec(memory_space=pltpu.HBM)


def near_call(rest, ahead, src, rel, near, relation, more):
    columns, edges = near.shape[0], src.shape[1]
    blocks = src.shape[0]
    steps = blocks // STEP
    count = STEP * (steps - ahead if rest else ahead)
    flops = 2 * count * edges * columns * (near.shape[1] + relation.shape[1])
    mixed_type = jax.ShapeDtypeStruct((steps, STEP, columns, edges), BF16)
    order_type = jax.ShapeDtypeStruct((blocks + 2,), jnp.int32)
    scratch = [
        pltpu.VMEM((2, STEP, columns, edges), BF16),
        pltpu.SemaphoreType.DMA((2,)),
    ]
    settings = dict(
        compiler_params=pltpu.CompilerParams(vmem_limit_bytes=VMEM_LIMIT),
        cost_estimate=pl.CostEstimate(
            flops=flops, bytes_accessed=2 * count * edges * columns, transcendentals=0
        ),
    )
    if not rest:
        return pl.pallas_call(
            functools.partial(near_kernel, rest, ahead),
            out_shape=(mixed_type, order_type),
            in_specs=[SMEM] * 2 + [WHOLE] * 4,
            out_specs=(HBM, SMEM),
            scratch_shapes=scratch,
            **settings,
        )(*more, src, rel, near, relation)
    mixed, order = more
    return pl.pallas_call(
        functools.partial(near_kernel, rest, ahead),
        out_shape=mixed_type,
        in_specs=[SMEM] + [WHOLE] * 4 + [HBM],
        out_specs=HBM,
        input_output_aliases={5: 0},
        scratch_shapes=scratch,
        **settings,
    )(order, src, rel, near, relation, mixed)


def far_call(half_rel, last, ahead, scalars, edges, emb, far, weights, more, kept, second):
    rows_dev, columns = emb.shape
    blocks, width = edges[0].shape
    return pl.pallas_call(
        functools.partial(far_kernel, half_rel, last, ahead),
        out_shape=(jax.ShapeDtypeStruct((rows_dev, columns), BF16), second),
        in_specs=[SMEM] * 2 + [WHOLE] * 3 + [HBM] + [WHOLE] * (5 + len(more)) + [HBM] * (2 if last else 1),
        out_specs=(HBM, WHOLE),
        input_output_aliases={12 + len(more): 0} if last else {},
        scratch_shapes=[
            pltpu.VMEM((far.shape[0], columns, CHUNK), BF16),
            pltpu.VMEM((STEP, columns, width if far.shape[0] > 1 else 128), F32),
            pltpu.VMEM((2, 2, STEP * BLK, columns), BF16),
            pltpu.VMEM((2, STEP, columns, width), BF16),
            pltpu.VMEM((2, STEP, BLK, columns), BF16),
            pltpu.VMEM((rows_dev, columns), BF16),
            pltpu.SemaphoreType.DMA((2,)),
            pltpu.SemaphoreType.DMA((2, STEP)),
            pltpu.SemaphoreType.DMA((blocks,)),
        ],
        compiler_params=pltpu.CompilerParams(vmem_limit_bytes=VMEM_LIMIT),
        cost_estimate=pl.CostEstimate(
            flops=blocks * width * columns * far.shape[0] * CHUNK,
            bytes_accessed=blocks * width * columns,
            transcendentals=0,
        ),
    )(*scalars, *edges, emb, far, *weights, *more, *kept)


def score_kernel(packed, groups, heads_ref, rel_ref, hidden_ref, scores_ref, *outs):
    query = (heads_ref[...].astype(F32) * rel_ref[...]).astype(BF16)
    scores = lax.dot_general(query, hidden_ref[...], NT, preferred_element_type=F32)
    scores_ref[...] = scores
    top = jnp.max(scores, axis=1, keepdims=True)
    high = top.astype(BF16).astype(F32)
    low = (top - high).astype(BF16).astype(F32)
    top = high + low
    weights = jnp.exp(scores - top)
    total = jnp.sum(weights, axis=1, keepdims=True)
    weighted = jnp.dot(weights.astype(BF16), hidden_ref[...], preferred_element_type=F32)
    total_high = total.astype(BF16).astype(F32)
    lanes = lax.broadcasted_iota(jnp.int32, (query.shape[0], 128), 1) % 4
    wide = jnp.where(lanes == 0, high, total - total_high)
    wide = jnp.where(lanes == 1, low, wide)
    wide = jnp.where(lanes == 2, total_high, wide)
    stats = jnp.transpose(wide)
    if not packed:
        weighted_ref, stats_ref = outs
        weighted_ref[...] = weighted.astype(BF16)
        stats_ref[...] = stats[: stats_ref.shape[0]].astype(BF16)
        return
    (payload_ref,) = outs
    upper = lax.broadcasted_iota(jnp.int32, (8, 128), 0) < 4
    figures = jnp.where(upper, stats[:8, :128], stats[:8, 128:])
    devices = payload_ref.shape[0]
    copies = devices // groups
    share = query.shape[0] // devices
    for device in range(devices):
        first = (device % copies * groups + device // copies) * share
        rows = weighted[first : first + share]
        payload_ref[device] = jnp.concatenate(
            [rows[:, :128], rows[:, 128:], figures], axis=0
        ).astype(BF16)


def body(
    entity_emb,
    relation_emb,
    in_weight,
    out_weight,
    loop_weight,
    rel_weight,
    loop_rel,
    edge_src,
    edge_dst,
    edge_rel,
    export_rows,
    query_head,
    query_rel,
):
    groups = lax.axis_size("ent")
    copies = lax.axis_size("rep")
    devices = groups * copies
    group = lax.axis_index("ent")
    member = lax.axis_index("rep")
    device = group * copies + member
    rows_dev, columns = entity_emb.shape
    queries = query_head.shape[0]
    batch_rows = queries // copies
    share = -(-batch_rows // groups)
    padded = share * devices

    blocks = edge_src.shape[0]
    relations = relation_emb.shape[0]
    rel_count = -(-relations // 256) * 256
    relation_t = jnp.pad(relation_emb, ((0, rel_count - relations), (0, 0))).T
    near_t = entity_emb.T
    ahead = min(AHEAD, blocks // STEP)

    slots = export_rows.shape[1]
    offered = pl.pallas_call(
        pick_kernel,
        out_shape=jax.ShapeDtypeStruct((slots, columns), BF16),
        in_specs=[SMEM, WHOLE, WHOLE],
        out_specs=WHOLE,
        compiler_params=pltpu.CompilerParams(vmem_limit_bytes=VMEM_LIMIT),
    )((member * rows_dev)[None], export_rows, entity_emb)
    pieces = lax.all_to_all(offered, "rep", 0, 0, tiled=True)
    mine = jnp.sum(
        pieces.reshape(copies, slots // copies, columns).astype(F32), axis=0
    ).astype(BF16)
    mine, near_t = lax.optimization_barrier((mine, near_t))
    spread = jnp.broadcast_to(mine[None], (devices,) + mine.shape)
    table = lax.all_to_all(spread, BOTH, 0, 0).reshape(groups * slots, columns)
    base = (device * blocks)[None]
    mixed, order = near_call(
        False, ahead, edge_src, edge_rel, near_t, relation_t, (base, query_head)
    )
    far_count = -(-(groups * slots) // CHUNK) * CHUNK
    far = jnp.pad(table, ((0, far_count - groups * slots), (0, 0)))
    far = far.reshape(far_count // CHUNK, CHUNK, columns)

    heads_row = jnp.pad(query_head, (0, padded - queries), constant_values=-1)[None]
    weights = (in_weight, out_weight, loop_weight, loop_rel[None])
    edges = (edge_src, edge_dst, edge_rel)
    half_rel = relations // 2
    hidden, heads = far_call(
        half_rel,
        False,
        ahead,
        (base, order),
        edges,
        entity_emb,
        far,
        weights,
        (heads_row,),
        (mixed,),
        jax.ShapeDtypeStruct((padded, columns), BF16),
    )
    heads, mixed = lax.optimization_barrier((heads, mixed))
    parts = lax.all_to_all(heads, BOTH, 0, 0, tiled=True).reshape(devices, share, columns)
    mixed = near_call(True, ahead, edge_src, edge_rel, near_t, relation_t, (mixed, order))
    own_heads = jnp.sum(parts.astype(F32), axis=0).astype(BF16)
    own_heads, mixed = lax.optimization_barrier((own_heads, mixed))
    head_rows = lax.all_to_all(
        jnp.broadcast_to(own_heads[None], (devices, share, columns)), BOTH, 0, 0
    ).reshape(padded, columns)[:queries]
    hidden, query_factor = far_call(
        half_rel,
        True,
        ahead,
        (base, order),
        edges,
        entity_emb,
        far,
        weights,
        (query_rel[None], relation_t, rel_weight),
        (mixed, hidden),
        jax.ShapeDtypeStruct((queries, columns), F32),
    )

    packed = share == 8 and share * devices == queries and (queries, columns) == (256, 256)
    score_type = jax.ShapeDtypeStruct((queries, rows_dev), F32)
    if packed:
        more = (jax.ShapeDtypeStruct((devices, 24, 128), BF16),)
    else:
        more = (
            jax.ShapeDtypeStruct((queries, columns), BF16),
            jax.ShapeDtypeStruct((16, queries), BF16),
        )
    scores, *parts = pl.pallas_call(
        functools.partial(score_kernel, packed, groups),
        out_shape=(score_type,) + more,
        compiler_params=pltpu.CompilerParams(vmem_limit_bytes=SCORE_LIMIT),
    )(head_rows, query_factor, hidden)
    if packed:
        received = lax.all_to_all(parts[0], BOTH, 0, 0).astype(F32)
        sums = jnp.concatenate([received[:, :8], received[:, 8:16]], axis=2)
        figures = jnp.concatenate([received[:, 16:20], received[:, 20:24]], axis=2)
    else:
        split = parts[0].reshape(copies, batch_rows, columns)
        split = jnp.pad(split, ((0, 0), (0, share * groups - batch_rows), (0, 0)))
        split = split.reshape(copies, groups, share, columns).transpose(1, 0, 2, 3)
        split = split.reshape(devices, share * columns)
        figures = parts[1][:4].reshape(1, 4 * queries)
        figures = jnp.broadcast_to(figures, (devices, 4 * queries))
        payload = jnp.concatenate([split, figures], axis=1).reshape(devices, -1, 128)
        received = lax.all_to_all(payload, BOTH, 0, 0).reshape(devices, -1).astype(F32)
        sums = received[:, : share * columns].reshape(devices, share, columns)
        figures = received[:, share * columns :].reshape(devices, 4, queries)
    tops = figures[:, 0] + figures[:, 1]
    totals = figures[:, 2] + figures[:, 3]
    row_top = jnp.max(tops, axis=0)
    scale = jnp.exp(tops - row_top)
    row_total = jnp.sum(totals * scale, axis=0)
    factor = jnp.pad(
        (scale / row_total).reshape(devices, copies, batch_rows),
        ((0, 0), (0, 0), (0, share * groups - batch_rows)),
    ).reshape(devices, -1)
    own_factor = lax.dynamic_slice_in_dim(
        factor, (member * groups + group) * share, share, 1
    )
    own_expected = jnp.sum(sums * own_factor[:, :, None], axis=0)
    expected_tail = lax.all_to_all(
        jnp.broadcast_to(own_expected[None], (groups, share, columns)), "ent", 0, 0
    ).reshape(groups * share, columns)[:batch_rows]
    log_probs = scores - (row_top + jnp.log(row_total))[:, None]
    return (log_probs, expected_tail)


def solution(mesh):
    placed = (
        P(("ent", "rep"), None),
        P(),
        P(),
        P(),
        P(),
        P(),
        P(),
        P(("ent", "rep"), None),
        P(("ent", "rep"), None),
        P(("ent", "rep"), None),
        P("ent", None),
        P(),
        P(),
    )
    return jax.shard_map(
        body,
        mesh=mesh,
        in_specs=placed,
        out_specs=(P(None, ("ent", "rep")), P("rep", None)),
        check_vma=False,
    )
```

```python
import functools

import jax
import jax.numpy as jnp
from jax import lax
from jax.experimental import pallas as pl
from jax.experimental.pallas import tpu as pltpu
from jax.sharding import PartitionSpec as P

BLK = 128
CHUNK = 1024
BF16 = jnp.bfloat16
F32 = jnp.float32
BOTH = ("ent", "rep")
NT = (((1,), (1,)), ((), ()))
TN = (((0,), (0,)), ((), ()))
VMEM_LIMIT = 56 * 2**20
STEP = 2
AHEAD = 6
SCORE_LIMIT = 24 * 2**20


def one_hot(index, rows):
    where = lax.broadcasted_iota(jnp.int16, (rows, index.shape[1]), 0) == index.astype(jnp.int16)
    return jnp.where(where, jnp.asarray(1, BF16), jnp.asarray(0, BF16))


def one_hot_wide(index, rows):
    where = lax.broadcasted_iota(jnp.int32, (rows, index.shape[1]), 0) == index
    return where.astype(F32).astype(BF16)


def is_outside(src, rows_dev):
    return jnp.where(src < rows_dev, 0.0, 1.0).astype(BF16)


def order_blocks(head_ref, first_block, blocks, order_ref):
    def mark(q, marks):
        block = lax.shift_right_arithmetic(head_ref[q], BLK.bit_length() - 1) - first_block
        inside = (block >= 0) & (block < blocks)
        return marks | jnp.where(inside, lax.shift_left(1, jnp.where(inside, block, 0)), 0)

    marks = lax.fori_loop(0, head_ref.shape[0], mark, jnp.int32(0), unroll=16)
    position = jnp.int32(0)
    for wanted in (1, 0):
        for b in range(blocks):
            taken = (lax.shift_right_logical(marks, b) & 1) == wanted
            order_ref[jnp.where(taken, position, blocks + 1)] = jnp.int32(b)
            position = position + taken.astype(jnp.int32)
        if wanted:
            found = position
    order_ref[blocks] = found


def middle_step(order_ref, blocks, ahead):
    return jnp.maximum((order_ref[blocks] + STEP - 1) // STEP, ahead)


def near_kernel(
    ahead,
    base_ref,
    head_ref,
    src_ref,
    rel_ref,
    near_ref,
    relation_ref,
    mixed_ref,
    order_ref,
    held_ref,
    sems,
):
    blocks = src_ref.shape[0]
    rows_dev = near_ref.shape[1]
    order_blocks(head_ref, base_ref[0], blocks, order_ref)
    count = middle_step(order_ref, blocks, ahead)

    def save(step, slot):
        return pltpu.make_async_copy(held_ref.at[slot], mixed_ref.at[step], sems.at[slot])

    def one_step(i, carry):
        slot = lax.rem(i, 2)

        @pl.when(i >= 2)
        def _():
            save(i - 2, slot).wait()

        for u in range(STEP):
            block = order_ref[i * STEP + u]
            src = src_ref[pl.ds(block, 1), :]
            rel = rel_ref[pl.ds(block, 1), :]
            gathered = jnp.dot(near_ref[...], one_hot(src, rows_dev), preferred_element_type=F32)
            relation = jnp.dot(
                relation_ref[...],
                one_hot(rel, relation_ref.shape[1]),
                preferred_element_type=F32,
            )
            is_far = is_outside(src, rows_dev)
            held_ref[slot, u] = (gathered.astype(BF16) + is_far) * relation.astype(BF16)
        save(i, slot).start()
        return carry

    lax.fori_loop(0, count, one_step, 0)
    for back in (2, 1):

        @pl.when(count >= back)
        def _():
            save(count - back, lax.rem(count - back, 2)).wait()


def owners(head_row, devices, rows_dev):
    limits = lax.broadcasted_iota(jnp.int32, (devices, head_row.shape[1]), 0) * rows_dev
    return jnp.sum((limits <= head_row).astype(F32), axis=0, keepdims=True) - 1.0


def ranks(owner_row):
    queries = owner_row.shape[1]
    across = jnp.broadcast_to(owner_row, (queries, queries))
    earlier = lax.broadcasted_iota(jnp.int32, (queries, queries), 0) < lax.broadcasted_iota(
        jnp.int32, (queries, queries), 1
    )
    same = (jnp.transpose(across) == across) & earlier
    return jnp.sum(same.astype(F32), axis=0, keepdims=True)


def far_kernel(
    half_rel,
    last,
    ahead,
    devices,
    base_ref,
    order_ref,
    src_ref,
    dst_ref,
    rel_ref,
    emb_ref,
    far_ref,
    in_ref,
    out_ref,
    loop_ref,
    loop_rel_ref,
    *rest,
):
    far_t_ref, gathered_ref, agg_ref, held_ref, own_ref, made_ref, sems, own_sems, out_sems = rest[-9:]
    if last:
        near_ref, query_rel_ref, relation_ref, rel_weight_ref, _ = rest[:5]
        hidden_ref, factor_ref = rest[5:7]
    else:
        head_ref, mixed_ref, hidden_ref, heads_ref, rank_ref, most_ref = rest[:6]
    blocks = src_ref.shape[0]
    rows_dev = blocks * BLK
    far_chunks = far_ref.shape[0]
    middle = middle_step(order_ref, blocks, ahead)
    start, stop = (middle, blocks // STEP) if last else (0, middle)

    def load(step, slot):
        return pltpu.make_async_copy(mixed_ref.at[step], held_ref.at[slot], sems.at[slot])

    def block_rows(step, u):
        return pl.ds(pl.multiple_of(order_ref[step * STEP + u] * BLK, BLK), BLK)

    def load_own(step, u):
        slot = lax.rem(step, 2)
        return pltpu.make_async_copy(
            emb_ref.at[block_rows(step, u)], own_ref.at[slot, u], own_sems.at[slot, u]
        )

    def give(step, u):
        rows = block_rows(step, u)
        return pltpu.make_async_copy(
            made_ref.at[rows], hidden_ref.at[rows], out_sems.at[step * STEP + u]
        )

    if not last:

        @pl.when(start < stop)
        def _():
            load(start, 0).start()

    def turn(j, carry):
        far_t_ref[j] = jnp.transpose(far_ref[j])
        return carry

    lax.fori_loop(0, far_chunks, turn, 0)
    if not last:
        made_ref[...] = jnp.zeros_like(made_ref)

    def look_up(src, u):
        if far_chunks == 1:
            return jnp.dot(
                far_t_ref[0], one_hot(src - rows_dev, CHUNK), preferred_element_type=F32
            )
        gathered_ref[u] = jnp.zeros(gathered_ref.shape[1:], F32)

        def one_chunk(j, carry):
            gathered_ref[u] += jnp.dot(
                far_t_ref[j],
                one_hot(src - rows_dev - j * CHUNK, CHUNK),
                preferred_element_type=F32,
            )
            return carry

        lax.fori_loop(0, far_chunks, one_chunk, 0)
        return gathered_ref[u]

    def finish(step, slot):
        own = own_ref[slot].reshape(STEP * BLK, own_ref.shape[-1])
        own = (own.astype(F32) * loop_rel_ref[...]).astype(BF16)
        preact = jnp.dot(agg_ref[0, slot], in_ref[...], preferred_element_type=F32)
        preact += jnp.dot(agg_ref[1, slot], out_ref[...], preferred_element_type=F32)
        preact += jnp.dot(own, loop_ref[...], preferred_element_type=F32)
        hidden = jnp.tanh(preact).astype(BF16)
        for u in range(STEP):
            made_ref[block_rows(step, u), :] = hidden[u * BLK : (u + 1) * BLK]

    def one_step(i, carry):
        slot = lax.rem(i, 2)
        step = start + i
        before = jnp.maximum(step - 1, start)

        @pl.when(i > 0)
        def _():
            for u in range(STEP):
                load_own(before, u).wait()

        for u in range(STEP):
            load_own(step, u).start()

        if not last:

            @pl.when(step + 1 < stop)
            def _():
                load(step + 1, 1 - slot).start()

            load(step, slot).wait()
        finish(before, lax.rem(step + 1, 2))
        rows = [pl.ds(order_ref[(start + i) * STEP + u], 1) for u in range(STEP)]
        srcs = [src_ref[row, :] for row in rows]
        found = [look_up(src, u) for u, src in enumerate(srcs)]
        composed = []
        for u, row in enumerate(rows):
            if last:
                near = jnp.dot(
                    near_ref[...], one_hot(srcs[u], rows_dev), preferred_element_type=F32
                )
                relation = jnp.dot(
                    relation_ref[...],
                    one_hot(rel_ref[row, :], relation_ref.shape[1]),
                    preferred_element_type=F32,
                )
                composed.append((found[u] + near).astype(BF16) * relation.astype(BF16))
            else:
                is_near = 1 - is_outside(srcs[u], rows_dev)
                composed.append((found[u].astype(BF16) + is_near) * held_ref[slot, u])
        for u, row in enumerate(rows):
            key = dst_ref[row, :] + jnp.where(rel_ref[row, :] >= half_rel, BLK, 0)
            selector = one_hot(key, 2 * BLK)
            counts = selector[:, :128]
            for lane in range(128, selector.shape[1], 128):
                counts = counts + selector[:, lane : lane + 128]
            counts = jnp.sum(counts.astype(F32), axis=1, keepdims=True)
            sums = lax.dot_general(selector, composed[u], NT, preferred_element_type=F32)
            agg = (sums * (1.0 / jnp.maximum(counts, 1.0))).astype(BF16)
            here = pl.ds(u * BLK, BLK)
            agg_ref[0, lax.rem(step, 2), here, :] = agg[:BLK]
            agg_ref[1, lax.rem(step, 2), here, :] = agg[BLK:]

        @pl.when(i > 0)
        def _():
            for u in range(STEP):
                give(before, u).start()

        return carry

    lax.fori_loop(0, stop - start, one_step, 0)

    @pl.when(start < stop)
    def _():
        for u in range(STEP):
            load_own(stop - 1, u).wait()
        finish(stop - 1, lax.rem(stop - 1, 2))
        for u in range(STEP):
            give(stop - 1, u).start()

    if last:
        picks = one_hot(query_rel_ref[...], relation_ref.shape[1])
        rows = lax.dot_general(
            picks, relation_ref[...], (((0,), (1,)), ((), ())), preferred_element_type=F32
        )
        factor_ref[...] = jnp.dot(
            rows.astype(BF16), rel_weight_ref[...], preferred_element_type=F32
        )
    else:
        picks = one_hot_wide(head_ref[...] - base_ref[0] * BLK, rows_dev)
        rows = lax.dot_general(picks, made_ref[...], TN, preferred_element_type=F32)
        rank = ranks(owners(head_ref[...], devices, rows_dev))
        slots = one_hot(rank.astype(jnp.int32), heads_ref.shape[0])
        heads_ref[...] = jnp.dot(slots, rows.astype(BF16), preferred_element_type=F32).astype(BF16)
        rank_ref[...] = rank.astype(jnp.int32)
        most_ref[0] = jnp.max(rank).astype(jnp.int32)

    def gave(step, carry):
        for u in range(STEP):
            give(step, u).wait()
        return carry

    lax.fori_loop(start, stop, gave, 0)


def pick_kernel(base_ref, index_ref, emb_ref, offered_ref):
    picks = one_hot(index_ref[...] - base_ref[0], emb_ref.shape[0])
    offered_ref[...] = lax.dot_general(
        picks, emb_ref[...], TN, preferred_element_type=F32
    ).astype(BF16)


SMEM = pl.BlockSpec(memory_space=pltpu.SMEM)
WHOLE = pl.BlockSpec(memory_space=pltpu.VMEM)
HBM = pl.BlockSpec(memory_space=pltpu.HBM)


def near_call(ahead, base, query_head, src, rel, near, relation):
    columns, edges = near.shape[0], src.shape[1]
    blocks = src.shape[0]
    count = STEP * ahead
    flops = 2 * count * edges * columns * (near.shape[1] + relation.shape[1])
    return pl.pallas_call(
        functools.partial(near_kernel, ahead),
        out_shape=(
            jax.ShapeDtypeStruct((blocks // STEP, STEP, columns, edges), BF16),
            jax.ShapeDtypeStruct((blocks + 2,), jnp.int32),
        ),
        in_specs=[SMEM] * 2 + [WHOLE] * 4,
        out_specs=(HBM, SMEM),
        scratch_shapes=[
            pltpu.VMEM((2, STEP, columns, edges), BF16),
            pltpu.SemaphoreType.DMA((2,)),
        ],
        compiler_params=pltpu.CompilerParams(vmem_limit_bytes=VMEM_LIMIT),
        cost_estimate=pl.CostEstimate(
            flops=flops, bytes_accessed=2 * count * edges * columns, transcendentals=0
        ),
    )(base, query_head, src, rel, near, relation)


def far_call(half_rel, last, ahead, devices, scalars, edges, emb, far, weights, more, kept, outs):
    rows_dev, columns = emb.shape
    blocks, width = edges[0].shape
    return pl.pallas_call(
        functools.partial(far_kernel, half_rel, last, ahead, devices),
        out_shape=(jax.ShapeDtypeStruct((rows_dev, columns), BF16),) + outs,
        in_specs=[SMEM] * 2 + [WHOLE] * 3 + [HBM] + [WHOLE] * (5 + len(more)) + [HBM],
        out_specs=(HBM, WHOLE) if last else (HBM, WHOLE, WHOLE, SMEM),
        input_output_aliases={11 + len(more): 0} if last else {},
        scratch_shapes=[
            pltpu.VMEM((far.shape[0], columns, CHUNK), BF16),
            pltpu.VMEM((STEP, columns, width if far.shape[0] > 1 else 128), F32),
            pltpu.VMEM((2, 2, STEP * BLK, columns), BF16),
            pltpu.VMEM((2, STEP, columns, 128 if last else width), BF16),
            pltpu.VMEM((2, STEP, BLK, columns), BF16),
            pltpu.VMEM((rows_dev, columns), BF16),
            pltpu.SemaphoreType.DMA((2,)),
            pltpu.SemaphoreType.DMA((2, STEP)),
            pltpu.SemaphoreType.DMA((blocks,)),
        ],
        compiler_params=pltpu.CompilerParams(vmem_limit_bytes=VMEM_LIMIT),
        cost_estimate=pl.CostEstimate(
            flops=blocks * width * columns * far.shape[0] * CHUNK,
            bytes_accessed=blocks * width * columns,
            transcendentals=0,
        ),
    )(*scalars, *edges, emb, far, *weights, *more, kept)


def score_kernel(
    packed,
    groups,
    devices,
    sent_ref,
    more_ref,
    rank_ref,
    head_ref,
    rel_ref,
    hidden_ref,
    scores_ref,
    *outs,
):
    slots = sent_ref.shape[0] // devices
    owner = owners(head_ref[...], devices, hidden_ref.shape[0]).astype(jnp.int32)
    place = jnp.where(rank_ref[...] < slots, owner * slots + rank_ref[...], -1)
    picks = one_hot(place, sent_ref.shape[0])
    heads = lax.dot_general(picks, sent_ref[...], TN, preferred_element_type=F32)
    heads = heads + more_ref[...].astype(F32)
    query = (heads * rel_ref[...]).astype(BF16)
    scores = lax.dot_general(query, hidden_ref[...], NT, preferred_element_type=F32)
    scores_ref[...] = scores
    top = jnp.max(scores, axis=1, keepdims=True)
    high = top.astype(BF16).astype(F32)
    low = (top - high).astype(BF16).astype(F32)
    top = high + low
    weights = jnp.exp(scores - top)
    total = jnp.sum(weights, axis=1, keepdims=True)
    weighted = jnp.dot(weights.astype(BF16), hidden_ref[...], preferred_element_type=F32)
    total_high = total.astype(BF16).astype(F32)
    lanes = lax.broadcasted_iota(jnp.int32, (query.shape[0], 128), 1) % 4
    wide = jnp.where(lanes == 0, high, total - total_high)
    wide = jnp.where(lanes == 1, low, wide)
    wide = jnp.where(lanes == 2, total_high, wide)
    stats = jnp.transpose(wide)
    if not packed:
        weighted_ref, stats_ref = outs
        weighted_ref[...] = weighted.astype(BF16)
        stats_ref[...] = stats[: stats_ref.shape[0]].astype(BF16)
        return
    (payload_ref,) = outs
    upper = lax.broadcasted_iota(jnp.int32, (8, 128), 0) < 4
    figures = jnp.where(upper, stats[:8, :128], stats[:8, 128:])
    copies = devices // groups
    share = query.shape[0] // devices
    for device in range(devices):
        first = (device % copies * groups + device // copies) * share
        rows = weighted[first : first + share]
        payload_ref[device] = jnp.concatenate(
            [rows[:, :128], rows[:, 128:], figures], axis=0
        ).astype(BF16)


def body(
    entity_emb,
    relation_emb,
    in_weight,
    out_weight,
    loop_weight,
    rel_weight,
    loop_rel,
    edge_src,
    edge_dst,
    edge_rel,
    export_rows,
    query_head,
    query_rel,
):
    groups = lax.axis_size("ent")
    copies = lax.axis_size("rep")
    devices = groups * copies
    group = lax.axis_index("ent")
    member = lax.axis_index("rep")
    device = group * copies + member
    rows_dev, columns = entity_emb.shape
    queries = query_head.shape[0]
    batch_rows = queries // copies
    share = -(-batch_rows // groups)
    padded = share * devices

    blocks = edge_src.shape[0]
    relations = relation_emb.shape[0]
    rel_count = -(-relations // 256) * 256
    relation_t = jnp.pad(relation_emb, ((0, rel_count - relations), (0, 0))).T
    near_t = entity_emb.T
    ahead = min(AHEAD, blocks // STEP)

    slots = export_rows.shape[1]
    offered = pl.pallas_call(
        pick_kernel,
        out_shape=jax.ShapeDtypeStruct((slots, columns), BF16),
        in_specs=[SMEM, WHOLE, WHOLE],
        out_specs=WHOLE,
        compiler_params=pltpu.CompilerParams(vmem_limit_bytes=VMEM_LIMIT),
    )((member * rows_dev)[None], export_rows, entity_emb)
    pieces = lax.all_to_all(offered, "rep", 0, 0, tiled=True)
    mine = jnp.sum(
        pieces.reshape(copies, slots // copies, columns).astype(F32), axis=0
    ).astype(BF16)
    mine, near_t = lax.optimization_barrier((mine, near_t))
    spread = jnp.broadcast_to(mine[None], (devices,) + mine.shape)
    table = lax.all_to_all(spread, BOTH, 0, 0).reshape(groups * slots, columns)
    base = (device * blocks)[None]
    mixed, order = near_call(
        ahead, base, query_head, edge_src, edge_rel, near_t, relation_t
    )
    far_count = -(-(groups * slots) // CHUNK) * CHUNK
    far = jnp.pad(table, ((0, far_count - groups * slots), (0, 0)))
    far = far.reshape(far_count // CHUNK, CHUNK, columns)

    head_row = query_head[None]
    weights = (in_weight, out_weight, loop_weight, loop_rel[None])
    edges = (edge_src, edge_dst, edge_rel)
    cap = min(queries, -(-3 * queries // (8 * devices)) * 8)
    hidden, heads, rank, most = far_call(
        relations // 2,
        False,
        ahead,
        devices,
        (base, order),
        edges,
        entity_emb,
        far,
        weights,
        (head_row,),
        mixed,
        (
            jax.ShapeDtypeStruct((-(-queries // cap) * cap, columns), BF16),
            jax.ShapeDtypeStruct((1, queries), jnp.int32),
            jax.ShapeDtypeStruct((1,), jnp.int32),
        ),
    )

    def send_round(turn):
        some = lax.dynamic_slice_in_dim(heads, turn * cap, cap, 0)
        spread = jnp.broadcast_to(some[None], (devices,) + some.shape)
        return lax.all_to_all(spread, BOTH, 0, 0).reshape(devices * cap, columns)

    def another_round(state):
        turn, more = state
        slot = rank[0] - turn * cap
        place = query_head // rows_dev * cap + slot
        rows = jnp.take(send_round(turn), jnp.clip(place, 0, devices * cap - 1), axis=0)
        inside = (slot >= 0) & (slot < cap)
        return turn + 1, jnp.where(inside[:, None], rows, more)

    sent = send_round(0)
    hidden, query_factor = far_call(
        relations // 2,
        True,
        ahead,
        devices,
        (base, order),
        edges,
        entity_emb,
        far,
        weights,
        (near_t, query_rel[None], relation_t, rel_weight),
        hidden,
        (jax.ShapeDtypeStruct((queries, columns), F32),),
    )
    _, more_heads = lax.while_loop(
        lambda state: state[0] * cap <= most[0],
        another_round,
        (jnp.int32(1), jnp.zeros((queries, columns), BF16)),
    )

    packed = share == 8 and share * devices == queries and (queries, columns) == (256, 256)
    score_type = jax.ShapeDtypeStruct((queries, rows_dev), F32)
    if packed:
        more = (jax.ShapeDtypeStruct((devices, 24, 128), BF16),)
    else:
        more = (
            jax.ShapeDtypeStruct((queries, columns), BF16),
            jax.ShapeDtypeStruct((16, queries), BF16),
        )
    scores, *parts = pl.pallas_call(
        functools.partial(score_kernel, packed, groups, devices),
        out_shape=(score_type,) + more,
        compiler_params=pltpu.CompilerParams(vmem_limit_bytes=SCORE_LIMIT),
    )(sent, more_heads, rank, head_row, query_factor, hidden)
    if packed:
        received = lax.all_to_all(parts[0], BOTH, 0, 0).astype(F32)
        sums = jnp.concatenate([received[:, :8], received[:, 8:16]], axis=2)
        figures = jnp.concatenate([received[:, 16:20], received[:, 20:24]], axis=2)
    else:
        split = parts[0].reshape(copies, batch_rows, columns)
        split = jnp.pad(split, ((0, 0), (0, share * groups - batch_rows), (0, 0)))
        split = split.reshape(copies, groups, share, columns).transpose(1, 0, 2, 3)
        split = split.reshape(devices, share * columns)
        figures = parts[1][:4].reshape(1, 4 * queries)
        figures = jnp.broadcast_to(figures, (devices, 4 * queries))
        payload = jnp.concatenate([split, figures], axis=1).reshape(devices, -1, 128)
        received = lax.all_to_all(payload, BOTH, 0, 0).reshape(devices, -1).astype(F32)
        sums = received[:, : share * columns].reshape(devices, share, columns)
        figures = received[:, share * columns :].reshape(devices, 4, queries)
    tops = figures[:, 0] + figures[:, 1]
    totals = figures[:, 2] + figures[:, 3]
    row_top = jnp.max(tops, axis=0)
    scale = jnp.exp(tops - row_top)
    row_total = jnp.sum(totals * scale, axis=0)
    factor = jnp.pad(
        (scale / row_total).reshape(devices, copies, batch_rows),
        ((0, 0), (0, 0), (0, share * groups - batch_rows)),
    ).reshape(devices, -1)
    own_factor = lax.dynamic_slice_in_dim(
        factor, (member * groups + group) * share, share, 1
    )
    own_expected = jnp.sum(sums * own_factor[:, :, None], axis=0)
    expected_tail = lax.all_to_all(
        jnp.broadcast_to(own_expected[None], (groups, share, columns)), "ent", 0, 0
    ).reshape(groups * share, columns)[:batch_rows]
    log_probs = scores - (row_top + jnp.log(row_total))[:, None]
    return (log_probs, expected_tail)


def solution(mesh):
    placed = (
        P(("ent", "rep"), None),
        P(),
        P(),
        P(),
        P(),
        P(),
        P(),
        P(("ent", "rep"), None),
        P(("ent", "rep"), None),
        P(("ent", "rep"), None),
        P("ent", None),
        P(),
        P(),
    )
    return jax.shard_map(
        body,
        mesh=mesh,
        in_specs=placed,
        out_specs=(P(None, ("ent", "rep")), P("rep", None)),
        check_vma=False,
    )
```

```python
import functools

import jax
import jax.numpy as jnp
from jax import lax
from jax.experimental import pallas as pl
from jax.experimental.pallas import tpu as pltpu
from jax.sharding import PartitionSpec as P

BLK = 128
CHUNK = 1024
LANES = 128
BF16 = jnp.bfloat16
F32 = jnp.float32
BOTH = ("ent", "rep")
NT = (((1,), (1,)), ((), ()))
TN = (((0,), (0,)), ((), ()))
VMEM_LIMIT = 56 * 2**20
STEP = 2
AHEAD = 6
SCORE_LIMIT = 24 * 2**20


def one_hot(index, rows):
    where = lax.broadcasted_iota(jnp.int16, (rows, index.shape[1]), 0) == index.astype(jnp.int16)
    return jnp.where(where, jnp.asarray(1, BF16), jnp.asarray(0, BF16))


def one_hot_wide(index, rows):
    where = lax.broadcasted_iota(jnp.int32, (rows, index.shape[1]), 0) == index
    return where.astype(F32).astype(BF16)


def is_outside(src, rows_dev):
    return jnp.where(src < rows_dev, 0.0, 1.0).astype(BF16)


def order_blocks(head_ref, first_block, blocks, order_ref):
    def mark(q, marks):
        block = lax.shift_right_arithmetic(head_ref[q], BLK.bit_length() - 1) - first_block
        inside = (block >= 0) & (block < blocks)
        return marks | jnp.where(inside, lax.shift_left(1, jnp.where(inside, block, 0)), 0)

    marks = lax.fori_loop(0, head_ref.shape[0], mark, jnp.int32(0), unroll=16)
    position = jnp.int32(0)
    for wanted in (1, 0):
        for b in range(blocks):
            taken = (lax.shift_right_logical(marks, b) & 1) == wanted
            order_ref[jnp.where(taken, position, blocks + 1)] = jnp.int32(b)
            position = position + taken.astype(jnp.int32)
        if wanted:
            found = position
    order_ref[blocks] = found


def middle_step(order_ref, blocks, ahead):
    return jnp.maximum((order_ref[blocks] + STEP - 1) // STEP, ahead)


def near_kernel(
    ahead,
    base_ref,
    head_ref,
    src_ref,
    rel_ref,
    near_ref,
    relation_ref,
    mixed_ref,
    order_ref,
    held_ref,
    sems,
):
    blocks = src_ref.shape[0]
    rows_dev = near_ref.shape[1]
    order_blocks(head_ref, base_ref[0], blocks, order_ref)
    count = middle_step(order_ref, blocks, ahead)

    def save(step, slot):
        return pltpu.make_async_copy(held_ref.at[slot], mixed_ref.at[step], sems.at[slot])

    def one_step(i, carry):
        slot = lax.rem(i, 2)

        @pl.when(i >= 2)
        def _():
            save(i - 2, slot).wait()

        for u in range(STEP):
            block = order_ref[i * STEP + u]
            src = src_ref[pl.ds(block, 1), :]
            rel = rel_ref[pl.ds(block, 1), :]
            gathered = jnp.dot(near_ref[...], one_hot(src, rows_dev), preferred_element_type=F32)
            relation = jnp.dot(
                relation_ref[...],
                one_hot(rel, relation_ref.shape[1]),
                preferred_element_type=F32,
            )
            is_far = is_outside(src, rows_dev)
            held_ref[slot, u] = (gathered.astype(BF16) + is_far) * relation.astype(BF16)
        save(i, slot).start()
        return carry

    lax.fori_loop(0, count, one_step, 0)
    for back in (2, 1):

        @pl.when(count >= back)
        def _():
            save(count - back, lax.rem(count - back, 2)).wait()


def owners(head_row, devices, rows_dev):
    limits = lax.broadcasted_iota(jnp.int32, (devices, head_row.shape[1]), 0) * rows_dev
    return jnp.sum((limits <= head_row).astype(F32), axis=0, keepdims=True) - 1.0


def ranks(owner_row):
    queries = owner_row.shape[1]
    across = jnp.broadcast_to(owner_row, (queries, queries))
    earlier = lax.broadcasted_iota(jnp.int32, (queries, queries), 0) < lax.broadcasted_iota(
        jnp.int32, (queries, queries), 1
    )
    same = (jnp.transpose(across) == across) & earlier
    return jnp.sum(same.astype(F32), axis=0, keepdims=True)


def far_kernel(
    half_rel,
    last,
    ahead,
    devices,
    base_ref,
    order_ref,
    src_ref,
    dst_ref,
    rel_ref,
    emb_ref,
    far_ref,
    in_ref,
    out_ref,
    loop_ref,
    loop_rel_ref,
    *rest,
):
    far_t_ref, gathered_ref, agg_ref, held_ref, own_ref, made_ref, sems, own_sems, out_sems = rest[-9:]
    if last:
        near_ref, query_rel_ref, relation_ref, rel_weight_ref, _ = rest[:5]
        hidden_ref, factor_ref = rest[5:7]
    else:
        head_ref, mixed_ref, hidden_ref, heads_ref, rank_ref, most_ref = rest[:6]
    blocks = src_ref.shape[0]
    rows_dev = blocks * BLK
    far_chunks = far_ref.shape[0]
    middle = middle_step(order_ref, blocks, ahead)
    start, stop = (middle, blocks // STEP) if last else (0, middle)

    def load(step, slot):
        return pltpu.make_async_copy(mixed_ref.at[step], held_ref.at[slot], sems.at[slot])

    def block_rows(step, u):
        return pl.ds(pl.multiple_of(order_ref[step * STEP + u] * BLK, BLK), BLK)

    def load_own(step, u):
        slot = lax.rem(step, 2)
        return pltpu.make_async_copy(
            emb_ref.at[block_rows(step, u)], own_ref.at[slot, u], own_sems.at[slot, u]
        )

    def give(step, u):
        rows = block_rows(step, u)
        return pltpu.make_async_copy(
            made_ref.at[rows], hidden_ref.at[rows], out_sems.at[step * STEP + u]
        )

    if not last:

        @pl.when(start < stop)
        def _():
            load(start, 0).start()

    def turn(j, carry):
        far_t_ref[j] = jnp.transpose(far_ref[j])
        return carry

    lax.fori_loop(0, far_chunks, turn, 0)
    if not last:
        made_ref[...] = jnp.zeros_like(made_ref)

    def look_up(src, u):
        if far_chunks == 1:
            return jnp.dot(
                far_t_ref[0], one_hot(src - rows_dev, CHUNK), preferred_element_type=F32
            )
        gathered_ref[u] = jnp.zeros(gathered_ref.shape[1:], F32)

        def one_chunk(j, carry):
            gathered_ref[u] += jnp.dot(
                far_t_ref[j],
                one_hot(src - rows_dev - j * CHUNK, CHUNK),
                preferred_element_type=F32,
            )
            return carry

        lax.fori_loop(0, far_chunks, one_chunk, 0)
        return gathered_ref[u]

    def finish(step, slot):
        own = own_ref[slot].reshape(STEP * BLK, own_ref.shape[-1])
        own = (own.astype(F32) * loop_rel_ref[...]).astype(BF16)
        preact = jnp.dot(agg_ref[0, slot], in_ref[...], preferred_element_type=F32)
        preact += jnp.dot(agg_ref[1, slot], out_ref[...], preferred_element_type=F32)
        preact += jnp.dot(own, loop_ref[...], preferred_element_type=F32)
        hidden = jnp.tanh(preact).astype(BF16)
        for u in range(STEP):
            made_ref[block_rows(step, u), :] = hidden[u * BLK : (u + 1) * BLK]

    def one_step(i, carry):
        slot = lax.rem(i, 2)
        step = start + i
        before = jnp.maximum(step - 1, start)

        @pl.when(i > 0)
        def _():
            for u in range(STEP):
                load_own(before, u).wait()

        for u in range(STEP):
            load_own(step, u).start()

        if not last:

            @pl.when(step + 1 < stop)
            def _():
                load(step + 1, 1 - slot).start()

            load(step, slot).wait()
        finish(before, lax.rem(step + 1, 2))
        rows = [pl.ds(order_ref[(start + i) * STEP + u], 1) for u in range(STEP)]
        srcs = [src_ref[row, :] for row in rows]
        found = [look_up(src, u) for u, src in enumerate(srcs)]
        composed = []
        for u, row in enumerate(rows):
            if last:
                near = jnp.dot(
                    near_ref[...], one_hot(srcs[u], rows_dev), preferred_element_type=F32
                )
                relation = jnp.dot(
                    relation_ref[...],
                    one_hot(rel_ref[row, :], relation_ref.shape[1]),
                    preferred_element_type=F32,
                )
                composed.append((found[u] + near).astype(BF16) * relation.astype(BF16))
            else:
                is_near = 1 - is_outside(srcs[u], rows_dev)
                composed.append((found[u].astype(BF16) + is_near) * held_ref[slot, u])
        for u, row in enumerate(rows):
            key = dst_ref[row, :] + jnp.where(rel_ref[row, :] >= half_rel, BLK, 0)
            selector = one_hot(key, 2 * BLK)
            counts = selector[:, :128]
            for lane in range(128, selector.shape[1], 128):
                counts = counts + selector[:, lane : lane + 128]
            counts = jnp.sum(counts.astype(F32), axis=1, keepdims=True)
            sums = lax.dot_general(selector, composed[u], NT, preferred_element_type=F32)
            agg = (sums * (1.0 / jnp.maximum(counts, 1.0))).astype(BF16)
            here = pl.ds(u * BLK, BLK)
            agg_ref[0, lax.rem(step, 2), here, :] = agg[:BLK]
            agg_ref[1, lax.rem(step, 2), here, :] = agg[BLK:]

        @pl.when(i > 0)
        def _():
            for u in range(STEP):
                give(before, u).start()

        return carry

    lax.fori_loop(0, stop - start, one_step, 0)

    @pl.when(start < stop)
    def _():
        for u in range(STEP):
            load_own(stop - 1, u).wait()
        finish(stop - 1, lax.rem(stop - 1, 2))
        for u in range(STEP):
            give(stop - 1, u).start()

    if last:
        picks = one_hot(query_rel_ref[...], relation_ref.shape[1])
        rows = lax.dot_general(
            picks, relation_ref[...], (((0,), (1,)), ((), ())), preferred_element_type=F32
        )
        factor_ref[...] = jnp.dot(
            rows.astype(BF16), rel_weight_ref[...], preferred_element_type=F32
        )
    else:
        picks = one_hot_wide(head_ref[...] - base_ref[0] * BLK, rows_dev)
        rows = lax.dot_general(picks, made_ref[...], TN, preferred_element_type=F32)
        rank = ranks(owners(head_ref[...], devices, rows_dev))
        slots = one_hot(rank.astype(jnp.int32), heads_ref.shape[0])
        heads_ref[...] = jnp.dot(slots, rows.astype(BF16), preferred_element_type=F32).astype(BF16)
        rank_ref[...] = rank.astype(jnp.int32)
        most_ref[0] = jnp.max(rank).astype(jnp.int32)

    def gave(step, carry):
        for u in range(STEP):
            give(step, u).wait()
        return carry

    lax.fori_loop(start, stop, gave, 0)


def pick_kernel(base_ref, index_ref, emb_ref, offered_ref):
    picks = one_hot(index_ref[...] - base_ref[0], emb_ref.shape[0])
    offered_ref[...] = lax.dot_general(
        picks, emb_ref[...], TN, preferred_element_type=F32
    ).astype(BF16)


SMEM = pl.BlockSpec(memory_space=pltpu.SMEM)
WHOLE = pl.BlockSpec(memory_space=pltpu.VMEM)
HBM = pl.BlockSpec(memory_space=pltpu.HBM)


def near_call(ahead, base, query_head, src, rel, near, relation):
    columns, edges = near.shape[0], src.shape[1]
    blocks = src.shape[0]
    count = STEP * ahead
    flops = 2 * count * edges * columns * (near.shape[1] + relation.shape[1])
    return pl.pallas_call(
        functools.partial(near_kernel, ahead),
        out_shape=(
            jax.ShapeDtypeStruct((blocks // STEP, STEP, columns, edges), BF16),
            jax.ShapeDtypeStruct((blocks + 2,), jnp.int32),
        ),
        in_specs=[SMEM] * 2 + [WHOLE] * 4,
        out_specs=(HBM, SMEM),
        scratch_shapes=[
            pltpu.VMEM((2, STEP, columns, edges), BF16),
            pltpu.SemaphoreType.DMA((2,)),
        ],
        compiler_params=pltpu.CompilerParams(vmem_limit_bytes=VMEM_LIMIT),
        cost_estimate=pl.CostEstimate(
            flops=flops, bytes_accessed=2 * count * edges * columns, transcendentals=0
        ),
    )(base, query_head, src, rel, near, relation)


def far_call(half_rel, last, ahead, devices, scalars, edges, emb, far, weights, more, kept, outs):
    rows_dev, columns = emb.shape
    blocks, width = edges[0].shape
    return pl.pallas_call(
        functools.partial(far_kernel, half_rel, last, ahead, devices),
        out_shape=(jax.ShapeDtypeStruct((rows_dev, columns), BF16),) + outs,
        in_specs=[SMEM] * 2 + [WHOLE] * 3 + [HBM] + [WHOLE] * (5 + len(more)) + [HBM],
        out_specs=(HBM, WHOLE) if last else (HBM, WHOLE, WHOLE, SMEM),
        input_output_aliases={11 + len(more): 0} if last else {},
        scratch_shapes=[
            pltpu.VMEM((far.shape[0], columns, CHUNK), BF16),
            pltpu.VMEM((STEP, columns, width if far.shape[0] > 1 else 128), F32),
            pltpu.VMEM((2, 2, STEP * BLK, columns), BF16),
            pltpu.VMEM((2, STEP, columns, 128 if last else width), BF16),
            pltpu.VMEM((2, STEP, BLK, columns), BF16),
            pltpu.VMEM((rows_dev, columns), BF16),
            pltpu.SemaphoreType.DMA((2,)),
            pltpu.SemaphoreType.DMA((2, STEP)),
            pltpu.SemaphoreType.DMA((blocks,)),
        ],
        compiler_params=pltpu.CompilerParams(vmem_limit_bytes=VMEM_LIMIT),
        cost_estimate=pl.CostEstimate(
            flops=blocks * width * columns * far.shape[0] * CHUNK,
            bytes_accessed=blocks * width * columns,
            transcendentals=0,
        ),
    )(*scalars, *edges, emb, far, *weights, *more, kept)


def score_kernel(
    devices,
    sent_ref,
    more_ref,
    rank_ref,
    head_ref,
    factor_hbm,
    hidden_hbm,
    scores_ref,
    payload_ref,
    factor_ref,
    hidden_ref,
    sems,
):
    copies = (
        pltpu.make_async_copy(factor_hbm, factor_ref, sems.at[0]),
        pltpu.make_async_copy(hidden_hbm, hidden_ref, sems.at[1]),
    )
    for copy in copies:
        copy.start()
    slots = sent_ref.shape[0] // devices
    owner = owners(head_ref[...], devices, hidden_ref.shape[0]).astype(jnp.int32)
    place = jnp.where(rank_ref[...] < slots, owner * slots + rank_ref[...], -1)
    picks = one_hot(place, sent_ref.shape[0])
    heads = lax.dot_general(picks, sent_ref[...], TN, preferred_element_type=F32)
    heads = heads + more_ref[...].astype(F32)
    for copy in copies:
        copy.wait()
    query = (heads * factor_ref[...]).astype(BF16)
    scores = lax.dot_general(query, hidden_ref[...], NT, preferred_element_type=F32)
    scores_ref[...] = scores
    top = jnp.max(scores, axis=1, keepdims=True)
    high = top.astype(BF16).astype(F32)
    low = (top - high).astype(BF16).astype(F32)
    top = high + low
    weights = jnp.exp(scores - top)
    total = jnp.sum(weights, axis=1, keepdims=True)
    weighted = jnp.dot(weights.astype(BF16), hidden_ref[...], preferred_element_type=F32)
    total_high = total.astype(BF16).astype(F32)
    lanes = lax.broadcasted_iota(jnp.int32, (query.shape[0], LANES), 1) % 4
    wide = jnp.where(lanes == 0, high, total - total_high)
    wide = jnp.where(lanes == 1, low, wide)
    wide = jnp.where(lanes == 2, total_high, wide)
    stats = jnp.transpose(wide)
    upper = lax.broadcasted_iota(jnp.int32, (8, LANES), 0) < 4
    figures = jnp.where(upper, stats[:8, :LANES], stats[:8, LANES:])
    share = query.shape[0] // payload_ref.shape[0]
    for peer in range(payload_ref.shape[0]):
        rows = weighted[peer * share : (peer + 1) * share]
        payload_ref[peer] = pack(rows[:, :LANES], rows[:, LANES:], figures)


def pack(left, right, figures):
    return jnp.concatenate([left, right, figures, figures], axis=0).astype(BF16)


def merge(data, first):
    share = (data.shape[1] - 16) // 2
    figures = data[:, 2 * share : 2 * share + 8]
    tops, totals, scales = [], [], []
    for half in (0, 4):
        each = figures[:, half : half + 1] + figures[:, half + 1 : half + 2]
        top = jnp.max(each, axis=0)
        scale = jnp.exp(each - top[None])
        total = figures[:, half + 2 : half + 3] + figures[:, half + 3 : half + 4]
        tops.append(top)
        totals.append(jnp.sum(total * scale, axis=0))
        scales.append(scale)
    left = right = 0.0
    for i in range(data.shape[0]):
        scale = jnp.where(first >= LANES, scales[1][i], scales[0][i])
        factor = column(scale, lax.rem(first, LANES), share)
        left += factor * data[i, :share]
        right += factor * data[i, share : 2 * share]
    return left, right, tops, totals


def column(row, first, rows):
    lanes = lax.broadcasted_iota(jnp.int32, (rows, LANES), 1)
    wanted = lax.broadcasted_iota(jnp.int32, (rows, LANES), 0) + first
    return jnp.sum(jnp.where(lanes == wanted, row, 0.0), axis=1, keepdims=True)


def merge_kernel(first_ref, received_ref, payload_ref):
    left, right, tops, totals = merge(received_ref[...].astype(F32), first_ref[0])
    row = lax.broadcasted_iota(jnp.int32, (8, LANES), 0)
    figures = jnp.zeros((8, LANES), F32)
    for half in range(2):
        for at, value in ((0, tops[half]), (2, totals[half])):
            high = value.astype(BF16).astype(F32)
            figures = jnp.where(row == 4 * half + at, high, figures)
            figures = jnp.where(row == 4 * half + at + 1, value - high, figures)
    block = pack(left, right, figures)
    for peer in range(payload_ref.shape[0]):
        payload_ref[peer] = block


def last_kernel(first_ref, received_ref, scores_ref, log_probs_ref, expected_ref):
    first = first_ref[0]
    left, right, tops, totals = merge(received_ref[...].astype(F32), first)
    for half in range(2):
        norm = column(tops[half] + jnp.log(totals[half]), 0, LANES)
        rows = pl.ds(half * LANES, LANES)
        log_probs_ref[rows, :] = scores_ref[rows, :] - norm
    total = jnp.where(first >= LANES, totals[1], totals[0])
    total = column(total, lax.rem(first, LANES), left.shape[0])
    expected_ref[:, :LANES] = left / total
    expected_ref[:, LANES:] = right / total


def body(
    entity_emb,
    relation_emb,
    in_weight,
    out_weight,
    loop_weight,
    rel_weight,
    loop_rel,
    edge_src,
    edge_dst,
    edge_rel,
    export_rows,
    query_head,
    query_rel,
):
    groups = lax.axis_size("ent")
    copies = lax.axis_size("rep")
    devices = groups * copies
    group = lax.axis_index("ent")
    member = lax.axis_index("rep")
    device = group * copies + member
    rows_dev, columns = entity_emb.shape
    queries = query_head.shape[0]

    blocks = edge_src.shape[0]
    relations = relation_emb.shape[0]
    ahead = min(AHEAD, blocks // STEP)

    slots = export_rows.shape[1]
    offered = pl.pallas_call(
        pick_kernel,
        out_shape=jax.ShapeDtypeStruct((slots, columns), BF16),
        in_specs=[SMEM, WHOLE, WHOLE],
        out_specs=WHOLE,
        compiler_params=pltpu.CompilerParams(vmem_limit_bytes=VMEM_LIMIT),
    )((member * rows_dev)[None], export_rows, entity_emb)
    offered, later_relation = lax.optimization_barrier((offered, relation_emb))
    rel_count = -(-relations // 256) * 256
    relation_t = jnp.pad(later_relation, ((0, rel_count - relations), (0, 0))).T
    near_t = entity_emb.T
    pieces = lax.all_to_all(offered, "rep", 0, 0, tiled=True)
    mine = jnp.sum(
        pieces.reshape(copies, slots // copies, columns).astype(F32), axis=0
    ).astype(BF16)
    mine, near_t = lax.optimization_barrier((mine, near_t))
    spread = jnp.broadcast_to(mine[None], (devices,) + mine.shape)
    table = lax.all_to_all(spread, BOTH, 0, 0).reshape(groups * slots, columns)
    base = (device * blocks)[None]
    mixed, order = near_call(
        ahead, base, query_head, edge_src, edge_rel, near_t, relation_t
    )
    far_count = -(-(groups * slots) // CHUNK) * CHUNK
    far = jnp.pad(table, ((0, far_count - groups * slots), (0, 0)))
    far = far.reshape(far_count // CHUNK, CHUNK, columns)

    head_row = query_head[None]
    weights = (in_weight, out_weight, loop_weight, loop_rel[None])
    edges = (edge_src, edge_dst, edge_rel)
    cap = min(queries, -(-3 * queries // (8 * devices)) * 8)
    hidden, heads, rank, most = far_call(
        relations // 2,
        False,
        ahead,
        devices,
        (base, order),
        edges,
        entity_emb,
        far,
        weights,
        (head_row,),
        mixed,
        (
            jax.ShapeDtypeStruct((-(-queries // cap) * cap, columns), BF16),
            jax.ShapeDtypeStruct((1, queries), jnp.int32),
            jax.ShapeDtypeStruct((1,), jnp.int32),
        ),
    )

    def send_round(turn):
        some = lax.dynamic_slice_in_dim(heads, turn * cap, cap, 0)
        spread = jnp.broadcast_to(some[None], (devices,) + some.shape)
        return lax.all_to_all(spread, BOTH, 0, 0).reshape(devices * cap, columns)

    def another_round(state):
        turn, more = state
        slot = rank[0] - turn * cap
        place = query_head // rows_dev * cap + slot
        rows = jnp.take(send_round(turn), jnp.clip(place, 0, devices * cap - 1), axis=0)
        inside = (slot >= 0) & (slot < cap)
        return turn + 1, jnp.where(inside[:, None], rows, more)

    sent = send_round(0)
    hidden, query_factor = far_call(
        relations // 2,
        True,
        ahead,
        devices,
        (base, order),
        edges,
        entity_emb,
        far,
        weights,
        (near_t, query_rel[None], relation_t, rel_weight),
        hidden,
        (jax.ShapeDtypeStruct((queries, columns), F32),),
    )
    _, more_heads = lax.while_loop(
        lambda state: state[0] * cap <= most[0],
        another_round,
        (jnp.int32(1), jnp.zeros((queries, columns), BF16)),
    )

    batch_rows = queries // copies
    first = (member * batch_rows)[None]
    part = (2 * batch_rows + 16, LANES)
    few = pltpu.CompilerParams(vmem_limit_bytes=SCORE_LIMIT)
    scores, payload = pl.pallas_call(
        functools.partial(score_kernel, devices),
        out_shape=(
            jax.ShapeDtypeStruct((queries, rows_dev), F32),
            jax.ShapeDtypeStruct((copies,) + part, BF16),
        ),
        in_specs=[WHOLE] * 4 + [HBM] * 2,
        out_specs=(WHOLE, WHOLE),
        scratch_shapes=[
            pltpu.VMEM((queries, columns), F32),
            pltpu.VMEM((rows_dev, columns), BF16),
            pltpu.SemaphoreType.DMA((2,)),
        ],
        compiler_params=few,
    )(sent, more_heads, rank, head_row, query_factor, hidden)
    payload = pl.pallas_call(
        merge_kernel,
        out_shape=jax.ShapeDtypeStruct((groups,) + part, BF16),
        in_specs=[SMEM, WHOLE],
        out_specs=WHOLE,
        compiler_params=few,
    )(first, lax.all_to_all(payload, "rep", 0, 0))
    log_probs, expected_tail = pl.pallas_call(
        last_kernel,
        out_shape=(
            jax.ShapeDtypeStruct((queries, rows_dev), F32),
            jax.ShapeDtypeStruct((batch_rows, columns), F32),
        ),
        in_specs=[SMEM, WHOLE, WHOLE],
        out_specs=(WHOLE, WHOLE),
        compiler_params=few,
    )(first, lax.all_to_all(payload, "ent", 0, 0), scores)
    return (log_probs, expected_tail)


def solution(mesh):
    placed = (
        P(("ent", "rep"), None),
        P(),
        P(),
        P(),
        P(),
        P(),
        P(),
        P(("ent", "rep"), None),
        P(("ent", "rep"), None),
        P(("ent", "rep"), None),
        P("ent", None),
        P(),
        P(),
    )
    return jax.shard_map(
        body,
        mesh=mesh,
        in_specs=placed,
        out_specs=(P(None, ("ent", "rep")), P("rep", None)),
        check_vma=False,
    )
```

```python
import functools

import jax
import jax.numpy as jnp
from jax import lax
from jax.experimental import pallas as pl
from jax.experimental.pallas import tpu as pltpu
from jax.sharding import PartitionSpec as P

BLK = 128
CHUNK = 1024
LANES = 128
BF16 = jnp.bfloat16
F32 = jnp.float32
BOTH = ("ent", "rep")
NT = (((1,), (1,)), ((), ()))
TN = (((0,), (0,)), ((), ()))
VMEM_LIMIT = 56 * 2**20
STEP = 2
AHEAD = 6
SCORE_LIMIT = 24 * 2**20
FAR_LIMIT = 56 * 2**20
FIRST_LIMIT = 56 * 2**20


def one_hot(index, rows):
    where = lax.broadcasted_iota(jnp.int16, (rows, index.shape[1]), 0) == index.astype(jnp.int16)
    return jnp.where(where, jnp.asarray(1, BF16), jnp.asarray(0, BF16))


def one_hot_wide(index, rows):
    where = lax.broadcasted_iota(jnp.int32, (rows, index.shape[1]), 0) == index
    return where.astype(F32).astype(BF16)


def is_outside(src, rows_dev):
    return jnp.where(src < rows_dev, 0.0, 1.0).astype(BF16)


def order_blocks(head_ref, first_block, blocks, order_ref):
    def mark(q, marks):
        block = lax.shift_right_arithmetic(head_ref[q], BLK.bit_length() - 1) - first_block
        inside = (block >= 0) & (block < blocks)
        return marks | jnp.where(inside, lax.shift_left(1, jnp.where(inside, block, 0)), 0)

    marks = lax.fori_loop(0, head_ref.shape[0], mark, jnp.int32(0), unroll=16)
    position = jnp.int32(0)
    for wanted in (1, 0):
        for b in range(blocks):
            taken = (lax.shift_right_logical(marks, b) & 1) == wanted
            order_ref[jnp.where(taken, position, blocks + 1)] = jnp.int32(b)
            position = position + taken.astype(jnp.int32)
        if wanted:
            found = position
    order_ref[blocks] = found


def middle_step(order_ref, blocks, ahead):
    return jnp.maximum((order_ref[blocks] + STEP - 1) // STEP, ahead)


def near_kernel(
    ahead,
    base_ref,
    head_ref,
    src_ref,
    rel_ref,
    near_ref,
    relation_ref,
    mixed_ref,
    order_ref,
    held_ref,
    sems,
):
    blocks = src_ref.shape[0]
    rows_dev = near_ref.shape[1]
    order_blocks(head_ref, base_ref[0], blocks, order_ref)
    count = middle_step(order_ref, blocks, ahead)

    def save(step, slot):
        return pltpu.make_async_copy(held_ref.at[slot], mixed_ref.at[step], sems.at[slot])

    def one_step(i, carry):
        slot = lax.rem(i, 2)

        @pl.when(i >= 2)
        def _():
            save(i - 2, slot).wait()

        for u in range(STEP):
            block = order_ref[i * STEP + u]
            src = src_ref[pl.ds(block, 1), :]
            rel = rel_ref[pl.ds(block, 1), :]
            gathered = jnp.dot(near_ref[...], one_hot(src, rows_dev), preferred_element_type=F32)
            relation = jnp.dot(
                relation_ref[...],
                one_hot(rel, relation_ref.shape[1]),
                preferred_element_type=F32,
            )
            is_far = is_outside(src, rows_dev)
            held_ref[slot, u] = (gathered.astype(BF16) + is_far) * relation.astype(BF16)
        save(i, slot).start()
        return carry

    lax.fori_loop(0, count, one_step, 0)
    for back in (2, 1):

        @pl.when(count >= back)
        def _():
            save(count - back, lax.rem(count - back, 2)).wait()


def owners(head_row, devices, rows_dev):
    limits = lax.broadcasted_iota(jnp.int32, (devices, head_row.shape[1]), 0) * rows_dev
    return jnp.sum((limits <= head_row).astype(F32), axis=0, keepdims=True) - 1.0


def ranks(owner_row):
    queries = owner_row.shape[1]
    across = jnp.broadcast_to(owner_row, (queries, queries))
    earlier = lax.broadcasted_iota(jnp.int32, (queries, queries), 0) < lax.broadcasted_iota(
        jnp.int32, (queries, queries), 1
    )
    same = (jnp.transpose(across) == across) & earlier
    return jnp.sum(same.astype(F32), axis=0, keepdims=True)


def far_kernel(
    half_rel,
    last,
    ahead,
    devices,
    base_ref,
    order_ref,
    src_ref,
    dst_ref,
    rel_ref,
    emb_ref,
    far_ref,
    in_ref,
    out_ref,
    loop_ref,
    loop_rel_ref,
    *rest,
):
    far_t_ref, gathered_ref, agg_ref, held_ref, own_ref, made_ref, sems, own_sems, out_sems = rest[-9:]
    if last:
        near_ref, query_rel_ref, relation_ref, rel_weight_ref, _ = rest[:5]
        hidden_ref, factor_ref = rest[5:7]
    else:
        head_ref, mixed_ref, hidden_ref, heads_ref, sent_ref, rank_ref, most_ref = rest[:7]
    blocks = src_ref.shape[0]
    rows_dev = blocks * BLK
    far_chunks = far_ref.shape[0]
    middle = middle_step(order_ref, blocks, ahead)
    start, stop = (middle, blocks // STEP) if last else (0, middle)

    def load(step, slot):
        return pltpu.make_async_copy(mixed_ref.at[step], held_ref.at[slot], sems.at[slot])

    def block_rows(step, u):
        return pl.ds(pl.multiple_of(order_ref[step * STEP + u] * BLK, BLK), BLK)

    def load_own(step, u):
        slot = lax.rem(step, 2)
        return pltpu.make_async_copy(
            emb_ref.at[block_rows(step, u)], own_ref.at[slot, u], own_sems.at[slot, u]
        )

    def give(step, u):
        rows = block_rows(step, u)
        return pltpu.make_async_copy(
            made_ref.at[rows], hidden_ref.at[rows], out_sems.at[step * STEP + u]
        )

    if not last:

        @pl.when(start < stop)
        def _():
            load(start, 0).start()

    def turn(j, carry):
        far_t_ref[j] = jnp.transpose(far_ref[j])
        return carry

    lax.fori_loop(0, far_chunks, turn, 0)
    if not last:
        made_ref[...] = jnp.zeros_like(made_ref)

    def look_up(src, u):
        if far_chunks == 1:
            return jnp.dot(
                far_t_ref[0], one_hot(src - rows_dev, CHUNK), preferred_element_type=F32
            )
        gathered_ref[u] = jnp.zeros(gathered_ref.shape[1:], F32)

        def one_chunk(j, carry):
            gathered_ref[u] += jnp.dot(
                far_t_ref[j],
                one_hot(src - rows_dev - j * CHUNK, CHUNK),
                preferred_element_type=F32,
            )
            return carry

        lax.fori_loop(0, far_chunks, one_chunk, 0)
        return gathered_ref[u]

    def finish(step, slot):
        own = own_ref[slot].reshape(STEP * BLK, own_ref.shape[-1])
        own = (own.astype(F32) * loop_rel_ref[...]).astype(BF16)
        preact = jnp.dot(agg_ref[0, slot], in_ref[...], preferred_element_type=F32)
        preact += jnp.dot(agg_ref[1, slot], out_ref[...], preferred_element_type=F32)
        preact += jnp.dot(own, loop_ref[...], preferred_element_type=F32)
        hidden = jnp.tanh(preact).astype(BF16)
        for u in range(STEP):
            made_ref[block_rows(step, u), :] = hidden[u * BLK : (u + 1) * BLK]

    def one_step(i, carry):
        slot = lax.rem(i, 2)
        step = start + i
        before = jnp.maximum(step - 1, start)

        @pl.when(i > 0)
        def _():
            for u in range(STEP):
                load_own(before, u).wait()

        for u in range(STEP):
            load_own(step, u).start()

        if not last:

            @pl.when(step + 1 < stop)
            def _():
                load(step + 1, 1 - slot).start()

            load(step, slot).wait()
        finish(before, lax.rem(step + 1, 2))
        rows = [pl.ds(order_ref[(start + i) * STEP + u], 1) for u in range(STEP)]
        srcs = [src_ref[row, :] for row in rows]
        found = [look_up(src, u) for u, src in enumerate(srcs)]
        composed = []
        for u, row in enumerate(rows):
            if last:
                near = jnp.dot(
                    near_ref[...], one_hot(srcs[u], rows_dev), preferred_element_type=F32
                )
                relation = jnp.dot(
                    relation_ref[...],
                    one_hot(rel_ref[row, :], relation_ref.shape[1]),
                    preferred_element_type=F32,
                )
                composed.append((found[u] + near).astype(BF16) * relation.astype(BF16))
            else:
                is_near = 1 - is_outside(srcs[u], rows_dev)
                composed.append((found[u].astype(BF16) + is_near) * held_ref[slot, u])
        for u, row in enumerate(rows):
            key = dst_ref[row, :] + jnp.where(rel_ref[row, :] >= half_rel, BLK, 0)
            selector = one_hot(key, 2 * BLK)
            counts = selector[:, :128]
            for lane in range(128, selector.shape[1], 128):
                counts = counts + selector[:, lane : lane + 128]
            counts = jnp.sum(counts.astype(F32), axis=1, keepdims=True)
            sums = lax.dot_general(selector, composed[u], NT, preferred_element_type=F32)
            agg = (sums * (1.0 / jnp.maximum(counts, 1.0))).astype(BF16)
            here = pl.ds(u * BLK, BLK)
            agg_ref[0, lax.rem(step, 2), here, :] = agg[:BLK]
            agg_ref[1, lax.rem(step, 2), here, :] = agg[BLK:]

        @pl.when(i > 0)
        def _():
            for u in range(STEP):
                give(before, u).start()

        return carry

    lax.fori_loop(0, stop - start, one_step, 0)

    @pl.when(start < stop)
    def _():
        for u in range(STEP):
            load_own(stop - 1, u).wait()
        finish(stop - 1, lax.rem(stop - 1, 2))
        for u in range(STEP):
            give(stop - 1, u).start()

    if last:
        picks = one_hot(query_rel_ref[...], relation_ref.shape[1])
        rows = lax.dot_general(
            picks, relation_ref[...], (((0,), (1,)), ((), ())), preferred_element_type=F32
        )
        factor_ref[...] = jnp.dot(
            rows.astype(BF16), rel_weight_ref[...], preferred_element_type=F32
        )
    else:
        picks = one_hot_wide(head_ref[...] - base_ref[0] * BLK, rows_dev)
        rows = lax.dot_general(picks, made_ref[...], TN, preferred_element_type=F32)
        rank = ranks(owners(head_ref[...], devices, rows_dev))
        slots = one_hot(rank.astype(jnp.int32), heads_ref.shape[0])
        packed = jnp.dot(slots, rows.astype(BF16), preferred_element_type=F32)
        heads_ref[...] = packed.astype(BF16)
        for peer in range(devices):
            sent_ref[peer] = packed[: sent_ref.shape[1]].astype(BF16)
        rank_ref[...] = rank.astype(jnp.int32)
        most_ref[0] = jnp.max(rank).astype(jnp.int32)

    def gave(step, carry):
        for u in range(STEP):
            give(step, u).wait()
        return carry

    lax.fori_loop(start, stop, gave, 0)


def pick_kernel(base_ref, index_ref, emb_ref, offered_ref):
    picks = one_hot(index_ref[...] - base_ref[0], emb_ref.shape[0])
    offered_ref[...] = lax.dot_general(
        picks, emb_ref[...], TN, preferred_element_type=F32
    ).astype(BF16)


SMEM = pl.BlockSpec(memory_space=pltpu.SMEM)
WHOLE = pl.BlockSpec(memory_space=pltpu.VMEM)
HBM = pl.BlockSpec(memory_space=pltpu.HBM)


def near_call(ahead, base, query_head, src, rel, near, relation):
    columns, edges = near.shape[0], src.shape[1]
    blocks = src.shape[0]
    count = STEP * ahead
    flops = 2 * count * edges * columns * (near.shape[1] + relation.shape[1])
    return pl.pallas_call(
        functools.partial(near_kernel, ahead),
        out_shape=(
            jax.ShapeDtypeStruct((blocks // STEP, STEP, columns, edges), BF16),
            jax.ShapeDtypeStruct((blocks + 2,), jnp.int32),
        ),
        in_specs=[SMEM] * 2 + [WHOLE] * 4,
        out_specs=(HBM, SMEM),
        scratch_shapes=[
            pltpu.VMEM((2, STEP, columns, edges), BF16),
            pltpu.SemaphoreType.DMA((2,)),
        ],
        compiler_params=pltpu.CompilerParams(vmem_limit_bytes=VMEM_LIMIT),
        cost_estimate=pl.CostEstimate(
            flops=flops, bytes_accessed=2 * count * edges * columns, transcendentals=0
        ),
    )(base, query_head, src, rel, near, relation)


def far_call(half_rel, last, ahead, devices, scalars, edges, emb, far, weights, more, kept, outs):
    rows_dev, columns = emb.shape
    blocks, width = edges[0].shape
    return pl.pallas_call(
        functools.partial(far_kernel, half_rel, last, ahead, devices),
        out_shape=(jax.ShapeDtypeStruct((rows_dev, columns), BF16),) + outs,
        in_specs=[SMEM] * 2 + [WHOLE] * 3 + [HBM] + [WHOLE] * (5 + len(more)) + [HBM],
        out_specs=(HBM, WHOLE) if last else (HBM, WHOLE, WHOLE, WHOLE, SMEM),
        input_output_aliases={11 + len(more): 0} if last else {},
        scratch_shapes=[
            pltpu.VMEM((far.shape[0], columns, CHUNK), BF16),
            pltpu.VMEM((STEP, columns, width if far.shape[0] > 1 else 128), F32),
            pltpu.VMEM((2, 2, STEP * BLK, columns), BF16),
            pltpu.VMEM((2, STEP, columns, 128 if last else width), BF16),
            pltpu.VMEM((2, STEP, BLK, columns), BF16),
            pltpu.VMEM((rows_dev, columns), BF16),
            pltpu.SemaphoreType.DMA((2,)),
            pltpu.SemaphoreType.DMA((2, STEP)),
            pltpu.SemaphoreType.DMA((blocks,)),
        ],
        compiler_params=pltpu.CompilerParams(vmem_limit_bytes=FAR_LIMIT),
        cost_estimate=pl.CostEstimate(
            flops=blocks * width * columns * far.shape[0] * CHUNK,
            bytes_accessed=blocks * width * columns,
            transcendentals=0,
        ),
    )(*scalars, *edges, emb, far, *weights, *more, kept)


def score_kernel(
    devices,
    sent_ref,
    more_ref,
    rank_ref,
    head_ref,
    factor_hbm,
    hidden_hbm,
    scores_ref,
    payload_ref,
    factor_ref,
    hidden_ref,
    sems,
):
    copies = (
        pltpu.make_async_copy(factor_hbm, factor_ref, sems.at[0]),
        pltpu.make_async_copy(hidden_hbm, hidden_ref, sems.at[1]),
    )
    for copy in copies:
        copy.start()
    slots = sent_ref.shape[0] // devices
    owner = owners(head_ref[...], devices, hidden_ref.shape[0]).astype(jnp.int32)
    place = jnp.where(rank_ref[...] < slots, owner * slots + rank_ref[...], -1)
    picks = one_hot(place, sent_ref.shape[0])
    heads = lax.dot_general(picks, sent_ref[...], TN, preferred_element_type=F32)
    heads = heads + more_ref[...].astype(F32)
    for copy in copies:
        copy.wait()
    query = (heads * factor_ref[...]).astype(BF16)
    scores = lax.dot_general(query, hidden_ref[...], NT, preferred_element_type=F32)
    scores_ref[...] = scores
    top = jnp.max(scores, axis=1, keepdims=True)
    high = top.astype(BF16).astype(F32)
    low = (top - high).astype(BF16).astype(F32)
    top = high + low
    weights = jnp.exp(scores - top)
    total = jnp.sum(weights, axis=1, keepdims=True)
    weighted = jnp.dot(weights.astype(BF16), hidden_ref[...], preferred_element_type=F32)
    total_high = total.astype(BF16).astype(F32)
    lanes = lax.broadcasted_iota(jnp.int32, (query.shape[0], LANES), 1) % 4
    wide = jnp.where(lanes == 0, high, total - total_high)
    wide = jnp.where(lanes == 1, low, wide)
    wide = jnp.where(lanes == 2, total_high, wide)
    stats = jnp.transpose(wide)
    upper = lax.broadcasted_iota(jnp.int32, (8, LANES), 0) < 4
    figures = jnp.where(upper, stats[:8, :LANES], stats[:8, LANES:])
    share = query.shape[0] // payload_ref.shape[0]
    for peer in range(payload_ref.shape[0]):
        rows = weighted[peer * share : (peer + 1) * share]
        payload_ref[peer] = pack(rows[:, :LANES], rows[:, LANES:], figures)


def pack(left, right, figures):
    return jnp.concatenate([left, right, figures, figures], axis=0).astype(BF16)


def merge(data, first):
    share = (data.shape[1] - 16) // 2
    figures = data[:, 2 * share : 2 * share + 8]
    tops, totals, scales = [], [], []
    for half in (0, 4):
        each = figures[:, half : half + 1] + figures[:, half + 1 : half + 2]
        top = jnp.max(each, axis=0)
        scale = jnp.exp(each - top[None])
        total = figures[:, half + 2 : half + 3] + figures[:, half + 3 : half + 4]
        tops.append(top)
        totals.append(jnp.sum(total * scale, axis=0))
        scales.append(scale)
    left = right = 0.0
    for i in range(data.shape[0]):
        scale = jnp.where(first >= LANES, scales[1][i], scales[0][i])
        factor = column(scale, lax.rem(first, LANES), share)
        left += factor * data[i, :share]
        right += factor * data[i, share : 2 * share]
    return left, right, tops, totals


def column(row, first, rows):
    lanes = lax.broadcasted_iota(jnp.int32, (rows, LANES), 1)
    wanted = lax.broadcasted_iota(jnp.int32, (rows, LANES), 0) + first
    return jnp.sum(jnp.where(lanes == wanted, row, 0.0), axis=1, keepdims=True)


def merge_kernel(first_ref, received_ref, payload_ref):
    left, right, tops, totals = merge(received_ref[...].astype(F32), first_ref[0])
    row = lax.broadcasted_iota(jnp.int32, (8, LANES), 0)
    figures = jnp.zeros((8, LANES), F32)
    for half in range(2):
        for at, value in ((0, tops[half]), (2, totals[half])):
            high = value.astype(BF16).astype(F32)
            figures = jnp.where(row == 4 * half + at, high, figures)
            figures = jnp.where(row == 4 * half + at + 1, value - high, figures)
    block = pack(left, right, figures)
    for peer in range(payload_ref.shape[0]):
        payload_ref[peer] = block


def last_kernel(first_ref, received_ref, scores_ref, log_probs_ref, expected_ref):
    first = first_ref[0]
    left, right, tops, totals = merge(received_ref[...].astype(F32), first)
    for half in range(2):
        norm = column(tops[half] + jnp.log(totals[half]), 0, LANES)
        rows = pl.ds(half * LANES, LANES)
        log_probs_ref[rows, :] = scores_ref[rows, :] - norm
    total = jnp.where(first >= LANES, totals[1], totals[0])
    total = column(total, lax.rem(first, LANES), left.shape[0])
    expected_ref[:, :LANES] = left / total
    expected_ref[:, LANES:] = right / total


def body(
    entity_emb,
    relation_emb,
    in_weight,
    out_weight,
    loop_weight,
    rel_weight,
    loop_rel,
    edge_src,
    edge_dst,
    edge_rel,
    export_rows,
    query_head,
    query_rel,
):
    groups = lax.axis_size("ent")
    copies = lax.axis_size("rep")
    devices = groups * copies
    group = lax.axis_index("ent")
    member = lax.axis_index("rep")
    device = group * copies + member
    rows_dev, columns = entity_emb.shape
    queries = query_head.shape[0]

    blocks = edge_src.shape[0]
    relations = relation_emb.shape[0]
    ahead = min(AHEAD, blocks // STEP)

    slots = export_rows.shape[1]
    offered = pl.pallas_call(
        pick_kernel,
        out_shape=jax.ShapeDtypeStruct((slots, columns), BF16),
        in_specs=[SMEM, WHOLE, WHOLE],
        out_specs=WHOLE,
        compiler_params=pltpu.CompilerParams(vmem_limit_bytes=VMEM_LIMIT),
    )((member * rows_dev)[None], export_rows, entity_emb)
    offered, later_relation = lax.optimization_barrier((offered, relation_emb))
    rel_count = -(-relations // 256) * 256
    relation_t = jnp.pad(later_relation, ((0, rel_count - relations), (0, 0))).T
    near_t = entity_emb.T
    pieces = lax.all_to_all(offered, "rep", 0, 0, tiled=True)
    mine = jnp.sum(
        pieces.reshape(copies, slots // copies, columns).astype(F32), axis=0
    ).astype(BF16)
    mine, near_t = lax.optimization_barrier((mine, near_t))
    spread = jnp.broadcast_to(mine[None], (devices,) + mine.shape)
    table = lax.all_to_all(spread, BOTH, 0, 0).reshape(groups * slots, columns)
    base = (device * blocks)[None]
    mixed, order = near_call(
        ahead, base, query_head, edge_src, edge_rel, near_t, relation_t
    )
    far_count = -(-(groups * slots) // CHUNK) * CHUNK
    far = jnp.pad(table, ((0, far_count - groups * slots), (0, 0)))
    far = far.reshape(far_count // CHUNK, CHUNK, columns)

    head_row = query_head[None]
    weights = (in_weight, out_weight, loop_weight, loop_rel[None])
    edges = (edge_src, edge_dst, edge_rel)
    cap = min(queries, -(-3 * queries // (8 * devices)) * 8)
    hidden, heads, spread, rank, most = far_call(
        relations // 2,
        False,
        ahead,
        devices,
        (base, order),
        edges,
        entity_emb,
        far,
        weights,
        (head_row,),
        mixed,
        (
            jax.ShapeDtypeStruct((-(-queries // cap) * cap, columns), BF16),
            jax.ShapeDtypeStruct((devices, cap, columns), BF16),
            jax.ShapeDtypeStruct((1, queries), jnp.int32),
            jax.ShapeDtypeStruct((1,), jnp.int32),
        ),
    )

    def send_round(turn):
        some = lax.dynamic_slice_in_dim(heads, turn * cap, cap, 0)
        spread = jnp.broadcast_to(some[None], (devices,) + some.shape)
        return lax.all_to_all(spread, BOTH, 0, 0).reshape(devices * cap, columns)

    def another_round(state):
        turn, more = state
        slot = rank[0] - turn * cap
        place = query_head // rows_dev * cap + slot
        rows = jnp.take(send_round(turn), jnp.clip(place, 0, devices * cap - 1), axis=0)
        inside = (slot >= 0) & (slot < cap)
        return turn + 1, jnp.where(inside[:, None], rows, more)

    sent = lax.all_to_all(spread, BOTH, 0, 0).reshape(devices * cap, columns)
    hidden, query_factor = far_call(
        relations // 2,
        True,
        ahead,
        devices,
        (base, order),
        edges,
        entity_emb,
        far,
        weights,
        (near_t, query_rel[None], relation_t, rel_weight),
        hidden,
        (jax.ShapeDtypeStruct((queries, columns), F32),),
    )
    _, more_heads = lax.while_loop(
        lambda state: state[0] * cap <= most[0],
        another_round,
        (jnp.int32(1), jnp.zeros((queries, columns), BF16)),
    )

    batch_rows = queries // copies
    first = (member * batch_rows)[None]
    part = (2 * batch_rows + 16, LANES)
    few = pltpu.CompilerParams(vmem_limit_bytes=SCORE_LIMIT)
    scores, payload = pl.pallas_call(
        functools.partial(score_kernel, devices),
        out_shape=(
            jax.ShapeDtypeStruct((queries, rows_dev), F32),
            jax.ShapeDtypeStruct((copies,) + part, BF16),
        ),
        in_specs=[WHOLE] * 4 + [HBM] * 2,
        out_specs=(WHOLE, WHOLE),
        scratch_shapes=[
            pltpu.VMEM((queries, columns), F32),
            pltpu.VMEM((rows_dev, columns), BF16),
            pltpu.SemaphoreType.DMA((2,)),
        ],
        compiler_params=pltpu.CompilerParams(vmem_limit_bytes=FIRST_LIMIT),
    )(sent, more_heads, rank, head_row, query_factor, hidden)
    payload = pl.pallas_call(
        merge_kernel,
        out_shape=jax.ShapeDtypeStruct((groups,) + part, BF16),
        in_specs=[SMEM, WHOLE],
        out_specs=WHOLE,
        compiler_params=few,
    )(first, lax.all_to_all(payload, "rep", 0, 0))
    log_probs, expected_tail = pl.pallas_call(
        last_kernel,
        out_shape=(
            jax.ShapeDtypeStruct((queries, rows_dev), F32),
            jax.ShapeDtypeStruct((batch_rows, columns), F32),
        ),
        in_specs=[SMEM, WHOLE, WHOLE],
        out_specs=(WHOLE, WHOLE),
        compiler_params=few,
    )(first, lax.all_to_all(payload, "ent", 0, 0), scores)
    return (log_probs, expected_tail)


def solution(mesh):
    placed = (
        P(("ent", "rep"), None),
        P(),
        P(),
        P(),
        P(),
        P(),
        P(),
        P(("ent", "rep"), None),
        P(("ent", "rep"), None),
        P(("ent", "rep"), None),
        P("ent", None),
        P(),
        P(),
    )
    return jax.shard_map(
        body,
        mesh=mesh,
        in_specs=placed,
        out_specs=(P(None, ("ent", "rep")), P("rep", None)),
        check_vma=False,
    )
```

```python
import functools

import jax
import jax.numpy as jnp
from jax import lax
from jax.experimental import pallas as pl
from jax.experimental.pallas import tpu as pltpu
from jax.sharding import PartitionSpec as P

BLK = 128
CHUNK = 1024
LANES = 128
BF16 = jnp.bfloat16
F32 = jnp.float32
BOTH = ("ent", "rep")
NT = (((1,), (1,)), ((), ()))
TN = (((0,), (0,)), ((), ()))
VMEM_LIMIT = 56 * 2**20
STEP = 2
AHEAD = 6
SCORE_LIMIT = 24 * 2**20
FAR_LIMIT = 56 * 2**20
FIRST_LIMIT = 24 * 2**20


def one_hot(index, rows):
    where = lax.broadcasted_iota(jnp.int16, (rows, index.shape[1]), 0) == index.astype(jnp.int16)
    return jnp.where(where, jnp.asarray(1, BF16), jnp.asarray(0, BF16))


def one_hot_wide(index, rows):
    where = lax.broadcasted_iota(jnp.int32, (rows, index.shape[1]), 0) == index
    return where.astype(F32).astype(BF16)


def is_outside(src, rows_dev):
    return jnp.where(src < rows_dev, 0.0, 1.0).astype(BF16)


def order_blocks(head_ref, first_block, blocks, order_ref):
    def mark(q, marks):
        block = lax.shift_right_arithmetic(head_ref[q], BLK.bit_length() - 1) - first_block
        inside = (block >= 0) & (block < blocks)
        return marks | jnp.where(inside, lax.shift_left(1, jnp.where(inside, block, 0)), 0)

    marks = lax.fori_loop(0, head_ref.shape[0], mark, jnp.int32(0), unroll=16)
    position = jnp.int32(0)
    for wanted in (1, 0):
        for b in range(blocks):
            taken = (lax.shift_right_logical(marks, b) & 1) == wanted
            order_ref[jnp.where(taken, position, blocks + 1)] = jnp.int32(b)
            position = position + taken.astype(jnp.int32)
        if wanted:
            found = position
    order_ref[blocks] = found


def middle_step(order_ref, blocks, ahead):
    return jnp.maximum((order_ref[blocks] + STEP - 1) // STEP, ahead)


def near_kernel(
    ahead,
    base_ref,
    head_ref,
    src_ref,
    rel_ref,
    near_ref,
    relation_ref,
    mixed_ref,
    order_ref,
    held_ref,
    sems,
):
    blocks = src_ref.shape[0]
    rows_dev = near_ref.shape[1]
    order_blocks(head_ref, base_ref[0], blocks, order_ref)
    count = middle_step(order_ref, blocks, ahead)

    def save(step, slot):
        return pltpu.make_async_copy(held_ref.at[slot], mixed_ref.at[step], sems.at[slot])

    def one_step(i, carry):
        slot = lax.rem(i, 2)

        @pl.when(i >= 2)
        def _():
            save(i - 2, slot).wait()

        for u in range(STEP):
            block = order_ref[i * STEP + u]
            src = src_ref[pl.ds(block, 1), :]
            rel = rel_ref[pl.ds(block, 1), :]
            gathered = jnp.dot(near_ref[...], one_hot(src, rows_dev), preferred_element_type=F32)
            relation = jnp.dot(
                relation_ref[...],
                one_hot(rel, relation_ref.shape[1]),
                preferred_element_type=F32,
            )
            is_far = is_outside(src, rows_dev)
            held_ref[slot, u] = (gathered.astype(BF16) + is_far) * relation.astype(BF16)
        save(i, slot).start()
        return carry

    lax.fori_loop(0, count, one_step, 0)
    for back in (2, 1):

        @pl.when(count >= back)
        def _():
            save(count - back, lax.rem(count - back, 2)).wait()


def owners(head_row, devices, rows_dev):
    limits = lax.broadcasted_iota(jnp.int32, (devices, head_row.shape[1]), 0) * rows_dev
    return jnp.sum((limits <= head_row).astype(F32), axis=0, keepdims=True) - 1.0


def ranks(owner_row):
    queries = owner_row.shape[1]
    across = jnp.broadcast_to(owner_row, (queries, queries))
    earlier = lax.broadcasted_iota(jnp.int32, (queries, queries), 0) < lax.broadcasted_iota(
        jnp.int32, (queries, queries), 1
    )
    same = (jnp.transpose(across) == across) & earlier
    return jnp.sum(same.astype(F32), axis=0, keepdims=True)


def far_kernel(
    half_rel,
    last,
    ahead,
    devices,
    base_ref,
    order_ref,
    *refs,
):
    if last:
        counts_ref, code_ref = refs[:2]
    else:
        src_ref, dst_ref, rel_ref = refs[:3]
    emb_ref, far_ref, in_ref, out_ref, loop_ref, loop_rel_ref, *rest = refs[2 if last else 3 :]
    far_t_ref, gathered_ref, agg_ref, held_ref, own_ref, made_ref, sems, own_sems, out_sems = rest[-9:]
    if last:
        near_ref, query_rel_ref, relation_ref, rel_weight_ref, _ = rest[:5]
        hidden_ref, factor_ref = rest[5:7]
    else:
        head_ref, mixed_ref, hidden_ref, heads_ref, sent_ref, rank_ref, most_ref = rest[:7]
    blocks, width = (code_ref if last else src_ref).shape
    third = width // 3
    rows_dev = blocks * BLK
    far_chunks = far_ref.shape[0]
    middle = middle_step(order_ref, blocks, ahead)
    start, stop = (middle, blocks // STEP) if last else (0, middle)

    def load(step, slot):
        return pltpu.make_async_copy(mixed_ref.at[step], held_ref.at[slot], sems.at[slot])

    def block_rows(step, u):
        return pl.ds(pl.multiple_of(order_ref[step * STEP + u] * BLK, BLK), BLK)

    def load_own(step, u):
        slot = lax.rem(step, 2)
        return pltpu.make_async_copy(
            emb_ref.at[block_rows(step, u)], own_ref.at[slot, u], own_sems.at[slot, u]
        )

    def give(step, u):
        rows = block_rows(step, u)
        return pltpu.make_async_copy(
            made_ref.at[rows], hidden_ref.at[rows], out_sems.at[step * STEP + u]
        )

    if not last:

        @pl.when(start < stop)
        def _():
            load(start, 0).start()

    def turn(j, carry):
        far_t_ref[j] = jnp.transpose(far_ref[j])
        return carry

    lax.fori_loop(0, far_chunks, turn, 0)
    if not last:
        made_ref[...] = jnp.zeros_like(made_ref)

    def edges_of(row):
        if last:
            code = code_ref[row, :]
            return code >> 16, (code >> 9) & (BLK - 1), code & 511
        return src_ref[row, :], dst_ref[row, :], rel_ref[row, :]

    def near_dot(src):
        return jnp.dot(near_ref[...], one_hot(src, rows_dev), preferred_element_type=F32)

    def look_up_sorted(src):
        near = near_dot(src[:, : 2 * third])
        far = look_up(src[:, third:], 0)
        both = near[:, third:] + far[:, :third]
        return jnp.concatenate([near[:, :third], both, far[:, third:]], axis=1)

    def look_up(src, u):
        if far_chunks == 1:
            return jnp.dot(
                far_t_ref[0], one_hot(src - rows_dev, CHUNK), preferred_element_type=F32
            )
        gathered_ref[u] = jnp.zeros(gathered_ref.shape[1:], F32)

        def one_chunk(j, carry):
            gathered_ref[u] += jnp.dot(
                far_t_ref[j],
                one_hot(src - rows_dev - j * CHUNK, CHUNK),
                preferred_element_type=F32,
            )
            return carry

        lax.fori_loop(0, far_chunks, one_chunk, 0)
        return gathered_ref[u]

    def finish(step, slot):
        own = own_ref[slot].reshape(STEP * BLK, own_ref.shape[-1])
        own = (own.astype(F32) * loop_rel_ref[...]).astype(BF16)
        preact = jnp.dot(agg_ref[0, slot], in_ref[...], preferred_element_type=F32)
        preact += jnp.dot(agg_ref[1, slot], out_ref[...], preferred_element_type=F32)
        preact += jnp.dot(own, loop_ref[...], preferred_element_type=F32)
        hidden = jnp.tanh(preact).astype(BF16)
        for u in range(STEP):
            made_ref[block_rows(step, u), :] = hidden[u * BLK : (u + 1) * BLK]

    def one_step(i, carry):
        slot = lax.rem(i, 2)
        step = start + i
        before = jnp.maximum(step - 1, start)

        @pl.when(i > 0)
        def _():
            for u in range(STEP):
                load_own(before, u).wait()

        for u in range(STEP):
            load_own(step, u).start()

        if not last:

            @pl.when(step + 1 < stop)
            def _():
                load(step + 1, 1 - slot).start()

            load(step, slot).wait()
        def work(is_sorted):
            finish(before, lax.rem(step + 1, 2))
            rows = [pl.ds(order_ref[step * STEP + u], 1) for u in range(STEP)]
            edges = [edges_of(row) for row in rows]
            if is_sorted:
                found = [look_up_sorted(src) for src, _, _ in edges]
            else:
                found = [look_up(src, u) for u, (src, _, _) in enumerate(edges)]
                if last:
                    found = [some + near_dot(src) for some, (src, _, _) in zip(found, edges)]
            composed = []
            for u, (src, _, rel) in enumerate(edges):
                if last:
                    relation = jnp.dot(
                        relation_ref[...],
                        one_hot(rel, relation_ref.shape[1]),
                        preferred_element_type=F32,
                    )
                    composed.append(found[u].astype(BF16) * relation.astype(BF16))
                else:
                    is_near = 1 - is_outside(src, rows_dev)
                    composed.append((found[u].astype(BF16) + is_near) * held_ref[slot, u])
            for u, (_, dst, rel) in enumerate(edges):
                key = dst + jnp.where(rel >= half_rel, BLK, 0)
                selector = one_hot(key, 2 * BLK)
                counts = selector[:, :128]
                for lane in range(128, selector.shape[1], 128):
                    counts = counts + selector[:, lane : lane + 128]
                counts = jnp.sum(counts.astype(F32), axis=1, keepdims=True)
                sums = lax.dot_general(selector, composed[u], NT, preferred_element_type=F32)
                agg = (sums * (1.0 / jnp.maximum(counts, 1.0))).astype(BF16)
                here = pl.ds(u * BLK, BLK)
                agg_ref[0, lax.rem(step, 2), here, :] = agg[:BLK]
                agg_ref[1, lax.rem(step, 2), here, :] = agg[BLK:]

        if last and far_chunks == 1 and width % 384 == 0:
            near_counts = [counts_ref[order_ref[step * STEP + u]] for u in range(STEP)]
            fits = [(count >= third) & (count <= 2 * third) for count in near_counts]
            all_fit = functools.reduce(jnp.logical_and, fits)
            pl.when(all_fit)(functools.partial(work, True))
            pl.when(jnp.logical_not(all_fit))(functools.partial(work, False))
        else:
            work(False)

        @pl.when(i > 0)
        def _():
            for u in range(STEP):
                give(before, u).start()

        return carry

    lax.fori_loop(0, stop - start, one_step, 0)

    @pl.when(start < stop)
    def _():
        for u in range(STEP):
            load_own(stop - 1, u).wait()
        finish(stop - 1, lax.rem(stop - 1, 2))
        for u in range(STEP):
            give(stop - 1, u).start()

    if last:
        picks = one_hot(query_rel_ref[...], relation_ref.shape[1])
        rows = lax.dot_general(
            picks, relation_ref[...], (((0,), (1,)), ((), ())), preferred_element_type=F32
        )
        factor_ref[...] = jnp.dot(
            rows.astype(BF16), rel_weight_ref[...], preferred_element_type=F32
        )
    else:
        picks = one_hot_wide(head_ref[...] - base_ref[0] * BLK, rows_dev)
        rows = lax.dot_general(picks, made_ref[...], TN, preferred_element_type=F32)
        rank = ranks(owners(head_ref[...], devices, rows_dev))
        slots = one_hot(rank.astype(jnp.int32), heads_ref.shape[0])
        packed = jnp.dot(slots, rows.astype(BF16), preferred_element_type=F32)
        heads_ref[...] = packed.astype(BF16)
        for peer in range(devices):
            sent_ref[peer] = packed[: sent_ref.shape[1]].astype(BF16)
        rank_ref[...] = rank.astype(jnp.int32)
        most_ref[0] = jnp.max(rank).astype(jnp.int32)

    def gave(step, carry):
        for u in range(STEP):
            give(step, u).wait()
        return carry

    lax.fori_loop(start, stop, gave, 0)


def pick_kernel(base_ref, index_ref, emb_ref, offered_ref):
    picks = one_hot(index_ref[...] - base_ref[0], emb_ref.shape[0])
    offered_ref[...] = lax.dot_general(
        picks, emb_ref[...], TN, preferred_element_type=F32
    ).astype(BF16)


SMEM = pl.BlockSpec(memory_space=pltpu.SMEM)
WHOLE = pl.BlockSpec(memory_space=pltpu.VMEM)
HBM = pl.BlockSpec(memory_space=pltpu.HBM)


def near_call(ahead, base, query_head, src, rel, near, relation):
    columns, edges = near.shape[0], src.shape[1]
    blocks = src.shape[0]
    count = STEP * ahead
    flops = 2 * count * edges * columns * (near.shape[1] + relation.shape[1])
    return pl.pallas_call(
        functools.partial(near_kernel, ahead),
        out_shape=(
            jax.ShapeDtypeStruct((blocks // STEP, STEP, columns, edges), BF16),
            jax.ShapeDtypeStruct((blocks + 2,), jnp.int32),
        ),
        in_specs=[SMEM] * 2 + [WHOLE] * 4,
        out_specs=(HBM, SMEM),
        scratch_shapes=[
            pltpu.VMEM((2, STEP, columns, edges), BF16),
            pltpu.SemaphoreType.DMA((2,)),
        ],
        compiler_params=pltpu.CompilerParams(vmem_limit_bytes=VMEM_LIMIT),
        cost_estimate=pl.CostEstimate(
            flops=flops, bytes_accessed=2 * count * edges * columns, transcendentals=0
        ),
    )(base, query_head, src, rel, near, relation)


def far_call(half_rel, last, ahead, devices, scalars, edges, emb, far, weights, more, kept, outs):
    rows_dev, columns = emb.shape
    blocks, width = edges[0].shape
    return pl.pallas_call(
        functools.partial(far_kernel, half_rel, last, ahead, devices),
        out_shape=(jax.ShapeDtypeStruct((rows_dev, columns), BF16),) + outs,
        in_specs=[SMEM] * len(scalars) + [WHOLE] * len(edges) + [HBM] + [WHOLE] * (5 + len(more)) + [HBM],
        out_specs=(HBM, WHOLE) if last else (HBM, WHOLE, WHOLE, WHOLE, SMEM),
        input_output_aliases={len(scalars) + len(edges) + 6 + len(more): 0} if last else {},
        scratch_shapes=[
            pltpu.VMEM((far.shape[0], columns, CHUNK), BF16),
            pltpu.VMEM((STEP, columns, width if far.shape[0] > 1 else 128), F32),
            pltpu.VMEM((2, 2, STEP * BLK, columns), BF16),
            pltpu.VMEM((2, STEP, columns, 128 if last else width), BF16),
            pltpu.VMEM((2, STEP, BLK, columns), BF16),
            pltpu.VMEM((rows_dev, columns), BF16),
            pltpu.SemaphoreType.DMA((2,)),
            pltpu.SemaphoreType.DMA((2, STEP)),
            pltpu.SemaphoreType.DMA((blocks,)),
        ],
        compiler_params=pltpu.CompilerParams(vmem_limit_bytes=FAR_LIMIT),
        cost_estimate=pl.CostEstimate(
            flops=blocks * width * columns * far.shape[0] * CHUNK,
            bytes_accessed=blocks * width * columns,
            transcendentals=0,
        ),
    )(*scalars, *edges, emb, far, *weights, *more, kept)


def score_kernel(
    devices,
    sent_ref,
    more_ref,
    rank_ref,
    head_ref,
    factor_hbm,
    hidden_hbm,
    scores_ref,
    payload_ref,
    factor_ref,
    hidden_ref,
    sems,
):
    copies = (
        pltpu.make_async_copy(factor_hbm, factor_ref, sems.at[0]),
        pltpu.make_async_copy(hidden_hbm, hidden_ref, sems.at[1]),
    )
    for copy in copies:
        copy.start()
    slots = sent_ref.shape[0] // devices
    owner = owners(head_ref[...], devices, hidden_ref.shape[0]).astype(jnp.int32)
    place = jnp.where(rank_ref[...] < slots, owner * slots + rank_ref[...], -1)
    picks = one_hot(place, sent_ref.shape[0])
    heads = lax.dot_general(picks, sent_ref[...], TN, preferred_element_type=F32)
    heads = heads + more_ref[...].astype(F32)
    for copy in copies:
        copy.wait()
    query = (heads * factor_ref[...]).astype(BF16)
    scores = lax.dot_general(query, hidden_ref[...], NT, preferred_element_type=F32)
    scores_ref[...] = scores
    top = jnp.max(scores, axis=1, keepdims=True)
    high = top.astype(BF16).astype(F32)
    low = (top - high).astype(BF16).astype(F32)
    top = high + low
    weights = jnp.exp(scores - top)
    total = jnp.sum(weights, axis=1, keepdims=True)
    weighted = jnp.dot(weights.astype(BF16), hidden_ref[...], preferred_element_type=F32)
    total_high = total.astype(BF16).astype(F32)
    lanes = lax.broadcasted_iota(jnp.int32, (query.shape[0], LANES), 1) % 4
    wide = jnp.where(lanes == 0, high, total - total_high)
    wide = jnp.where(lanes == 1, low, wide)
    wide = jnp.where(lanes == 2, total_high, wide)
    stats = jnp.transpose(wide)
    upper = lax.broadcasted_iota(jnp.int32, (8, LANES), 0) < 4
    figures = jnp.where(upper, stats[:8, :LANES], stats[:8, LANES:])
    share = query.shape[0] // payload_ref.shape[0]
    for peer in range(payload_ref.shape[0]):
        rows = weighted[peer * share : (peer + 1) * share]
        payload_ref[peer] = pack(rows[:, :LANES], rows[:, LANES:], figures)


def pack(left, right, figures):
    return jnp.concatenate([left, right, figures, figures], axis=0).astype(BF16)


def merge(data, first):
    share = (data.shape[1] - 16) // 2
    figures = data[:, 2 * share : 2 * share + 8]
    tops, totals, scales = [], [], []
    for half in (0, 4):
        each = figures[:, half : half + 1] + figures[:, half + 1 : half + 2]
        top = jnp.max(each, axis=0)
        scale = jnp.exp(each - top[None])
        total = figures[:, half + 2 : half + 3] + figures[:, half + 3 : half + 4]
        tops.append(top)
        totals.append(jnp.sum(total * scale, axis=0))
        scales.append(scale)
    left = right = 0.0
    for i in range(data.shape[0]):
        scale = jnp.where(first >= LANES, scales[1][i], scales[0][i])
        factor = column(scale, lax.rem(first, LANES), share)
        left += factor * data[i, :share]
        right += factor * data[i, share : 2 * share]
    return left, right, tops, totals


def column(row, first, rows):
    lanes = lax.broadcasted_iota(jnp.int32, (rows, LANES), 1)
    wanted = lax.broadcasted_iota(jnp.int32, (rows, LANES), 0) + first
    return jnp.sum(jnp.where(lanes == wanted, row, 0.0), axis=1, keepdims=True)


def merge_kernel(first_ref, received_ref, payload_ref):
    left, right, tops, totals = merge(received_ref[...].astype(F32), first_ref[0])
    row = lax.broadcasted_iota(jnp.int32, (8, LANES), 0)
    figures = jnp.zeros((8, LANES), F32)
    for half in range(2):
        for at, value in ((0, tops[half]), (2, totals[half])):
            high = value.astype(BF16).astype(F32)
            figures = jnp.where(row == 4 * half + at, high, figures)
            figures = jnp.where(row == 4 * half + at + 1, value - high, figures)
    block = pack(left, right, figures)
    for peer in range(payload_ref.shape[0]):
        payload_ref[peer] = block


def last_kernel(first_ref, received_ref, scores_ref, log_probs_ref, expected_ref):
    first = first_ref[0]
    left, right, tops, totals = merge(received_ref[...].astype(F32), first)
    for half in range(2):
        norm = column(tops[half] + jnp.log(totals[half]), 0, LANES)
        rows = pl.ds(half * LANES, LANES)
        log_probs_ref[rows, :] = scores_ref[rows, :] - norm
    total = jnp.where(first >= LANES, totals[1], totals[0])
    total = column(total, lax.rem(first, LANES), left.shape[0])
    expected_ref[:, :LANES] = left / total
    expected_ref[:, LANES:] = right / total


def body(
    entity_emb,
    relation_emb,
    in_weight,
    out_weight,
    loop_weight,
    rel_weight,
    loop_rel,
    edge_src,
    edge_dst,
    edge_rel,
    export_rows,
    query_head,
    query_rel,
):
    groups = lax.axis_size("ent")
    copies = lax.axis_size("rep")
    devices = groups * copies
    group = lax.axis_index("ent")
    member = lax.axis_index("rep")
    device = group * copies + member
    rows_dev, columns = entity_emb.shape
    queries = query_head.shape[0]

    blocks = edge_src.shape[0]
    relations = relation_emb.shape[0]
    ahead = min(AHEAD, blocks // STEP)

    slots = export_rows.shape[1]
    offered = pl.pallas_call(
        pick_kernel,
        out_shape=jax.ShapeDtypeStruct((slots, columns), BF16),
        in_specs=[SMEM, WHOLE, WHOLE],
        out_specs=WHOLE,
        compiler_params=pltpu.CompilerParams(vmem_limit_bytes=VMEM_LIMIT),
    )((member * rows_dev)[None], export_rows, entity_emb)
    offered, later_relation, later_src = lax.optimization_barrier(
        (offered, relation_emb, edge_src)
    )
    code = (later_src << 16) | (edge_dst << 9) | edge_rel
    near_counts = jnp.sum((later_src < rows_dev).astype(jnp.int32), axis=1)
    rel_count = -(-relations // 256) * 256
    relation_t = jnp.pad(later_relation, ((0, rel_count - relations), (0, 0))).T
    near_t = entity_emb.T
    pieces = lax.all_to_all(offered, "rep", 0, 0, tiled=True)
    mine = jnp.sum(
        pieces.reshape(copies, slots // copies, columns).astype(F32), axis=0
    ).astype(BF16)
    mine, near_t, code, near_counts = lax.optimization_barrier((mine, near_t, code, near_counts))
    code = lax.sort(code, dimension=1)
    spread = jnp.broadcast_to(mine[None], (devices,) + mine.shape)
    table = lax.all_to_all(spread, BOTH, 0, 0).reshape(groups * slots, columns)
    base = (device * blocks)[None]
    mixed, order = near_call(
        ahead, base, query_head, edge_src, edge_rel, near_t, relation_t
    )
    mixed, code = lax.optimization_barrier((mixed, code))
    far_count = -(-(groups * slots) // CHUNK) * CHUNK
    far = jnp.pad(table, ((0, far_count - groups * slots), (0, 0)))
    far = far.reshape(far_count // CHUNK, CHUNK, columns)

    head_row = query_head[None]
    weights = (in_weight, out_weight, loop_weight, loop_rel[None])
    edges = (edge_src, edge_dst, edge_rel)
    cap = min(queries, -(-3 * queries // (8 * devices)) * 8)
    hidden, heads, spread, rank, most = far_call(
        relations // 2,
        False,
        ahead,
        devices,
        (base, order),
        edges,
        entity_emb,
        far,
        weights,
        (head_row,),
        mixed,
        (
            jax.ShapeDtypeStruct((-(-queries // cap) * cap, columns), BF16),
            jax.ShapeDtypeStruct((devices, cap, columns), BF16),
            jax.ShapeDtypeStruct((1, queries), jnp.int32),
            jax.ShapeDtypeStruct((1,), jnp.int32),
        ),
    )

    def send_round(turn):
        some = lax.dynamic_slice_in_dim(heads, turn * cap, cap, 0)
        spread = jnp.broadcast_to(some[None], (devices,) + some.shape)
        return lax.all_to_all(spread, BOTH, 0, 0).reshape(devices * cap, columns)

    def another_round(state):
        turn, more = state
        slot = rank[0] - turn * cap
        place = query_head // rows_dev * cap + slot
        rows = jnp.take(send_round(turn), jnp.clip(place, 0, devices * cap - 1), axis=0)
        inside = (slot >= 0) & (slot < cap)
        return turn + 1, jnp.where(inside[:, None], rows, more)

    sent = lax.all_to_all(spread, BOTH, 0, 0).reshape(devices * cap, columns)
    hidden, query_factor = far_call(
        relations // 2,
        True,
        ahead,
        devices,
        (base, order, near_counts),
        (code,),
        entity_emb,
        far,
        weights,
        (near_t, query_rel[None], relation_t, rel_weight),
        hidden,
        (jax.ShapeDtypeStruct((queries, columns), F32),),
    )
    _, more_heads = lax.while_loop(
        lambda state: state[0] * cap <= most[0],
        another_round,
        (jnp.int32(1), jnp.zeros((queries, columns), BF16)),
    )

    batch_rows = queries // copies
    first = (member * batch_rows)[None]
    part = (2 * batch_rows + 16, LANES)
    few = pltpu.CompilerParams(vmem_limit_bytes=SCORE_LIMIT)
    scores, payload = pl.pallas_call(
        functools.partial(score_kernel, devices),
        out_shape=(
            jax.ShapeDtypeStruct((queries, rows_dev), F32),
            jax.ShapeDtypeStruct((copies,) + part, BF16),
        ),
        in_specs=[WHOLE] * 4 + [HBM] * 2,
        out_specs=(WHOLE, WHOLE),
        scratch_shapes=[
            pltpu.VMEM((queries, columns), F32),
            pltpu.VMEM((rows_dev, columns), BF16),
            pltpu.SemaphoreType.DMA((2,)),
        ],
        compiler_params=pltpu.CompilerParams(vmem_limit_bytes=FIRST_LIMIT),
    )(sent, more_heads, rank, head_row, query_factor, hidden)
    payload = pl.pallas_call(
        merge_kernel,
        out_shape=jax.ShapeDtypeStruct((groups,) + part, BF16),
        in_specs=[SMEM, WHOLE],
        out_specs=WHOLE,
        compiler_params=few,
    )(first, lax.all_to_all(payload, "rep", 0, 0))
    log_probs, expected_tail = pl.pallas_call(
        last_kernel,
        out_shape=(
            jax.ShapeDtypeStruct((queries, rows_dev), F32),
            jax.ShapeDtypeStruct((batch_rows, columns), F32),
        ),
        in_specs=[SMEM, WHOLE, WHOLE],
        out_specs=(WHOLE, WHOLE),
        compiler_params=few,
    )(first, lax.all_to_all(payload, "ent", 0, 0), scores)
    return (log_probs, expected_tail)


def solution(mesh):
    placed = (
        P(("ent", "rep"), None),
        P(),
        P(),
        P(),
        P(),
        P(),
        P(),
        P(("ent", "rep"), None),
        P(("ent", "rep"), None),
        P(("ent", "rep"), None),
        P("ent", None),
        P(),
        P(),
    )
    return jax.shard_map(
        body,
        mesh=mesh,
        in_specs=placed,
        out_specs=(P(None, ("ent", "rep")), P("rep", None)),
        check_vma=False,
    )
```

```python
import functools

import jax
import jax.numpy as jnp
from jax import lax
from jax.experimental import pallas as pl
from jax.experimental.pallas import tpu as pltpu
from jax.sharding import PartitionSpec as P

BLK = 128
CHUNK = 1024
LANES = 128
BF16 = jnp.bfloat16
F32 = jnp.float32
BOTH = ("ent", "rep")
NT = (((1,), (1,)), ((), ()))
TN = (((0,), (0,)), ((), ()))
VMEM_LIMIT = 56 * 2**20
STEP = 2
AHEAD = 6
SCORE_LIMIT = 24 * 2**20
FAR_LIMIT = 56 * 2**20
FIRST_LIMIT = 24 * 2**20


def one_hot(index, rows):
    where = lax.broadcasted_iota(jnp.int16, (rows, index.shape[1]), 0) == index.astype(jnp.int16)
    return jnp.where(where, jnp.asarray(1, BF16), jnp.asarray(0, BF16))


def one_hot_wide(index, rows):
    where = lax.broadcasted_iota(jnp.int32, (rows, index.shape[1]), 0) == index
    return where.astype(F32).astype(BF16)


def is_outside(src, rows_dev):
    return jnp.where(src < rows_dev, 0.0, 1.0).astype(BF16)


def order_blocks(head_ref, first_block, blocks, order_ref):
    def mark(q, marks):
        block = lax.shift_right_arithmetic(head_ref[q], BLK.bit_length() - 1) - first_block
        inside = (block >= 0) & (block < blocks)
        return marks | jnp.where(inside, lax.shift_left(1, jnp.where(inside, block, 0)), 0)

    marks = lax.fori_loop(0, head_ref.shape[0], mark, jnp.int32(0), unroll=16)
    position = jnp.int32(0)
    for wanted in (1, 0):
        for b in range(blocks):
            taken = (lax.shift_right_logical(marks, b) & 1) == wanted
            order_ref[jnp.where(taken, position, blocks + 1)] = jnp.int32(b)
            position = position + taken.astype(jnp.int32)
        if wanted:
            found = position
    order_ref[blocks] = found


def middle_step(order_ref, blocks, ahead):
    return jnp.maximum((order_ref[blocks] + STEP - 1) // STEP, ahead)


def near_kernel(
    ahead,
    base_ref,
    head_ref,
    src_ref,
    rel_ref,
    near_ref,
    relation_ref,
    mixed_ref,
    order_ref,
    held_ref,
    sems,
):
    blocks = src_ref.shape[0]
    rows_dev = near_ref.shape[1]
    order_blocks(head_ref, base_ref[0], blocks, order_ref)
    count = middle_step(order_ref, blocks, ahead)

    def save(step, slot):
        return pltpu.make_async_copy(held_ref.at[slot], mixed_ref.at[step], sems.at[slot])

    def one_step(i, carry):
        slot = lax.rem(i, 2)

        @pl.when(i >= 2)
        def _():
            save(i - 2, slot).wait()

        for u in range(STEP):
            block = order_ref[i * STEP + u]
            src = src_ref[pl.ds(block, 1), :]
            rel = rel_ref[pl.ds(block, 1), :]
            gathered = jnp.dot(near_ref[...], one_hot(src, rows_dev), preferred_element_type=F32)
            relation = jnp.dot(
                relation_ref[...],
                one_hot(rel, relation_ref.shape[1]),
                preferred_element_type=F32,
            )
            is_far = is_outside(src, rows_dev)
            held_ref[slot, u] = (gathered.astype(BF16) + is_far) * relation.astype(BF16)
        save(i, slot).start()
        return carry

    lax.fori_loop(0, count, one_step, 0)
    for back in (2, 1):

        @pl.when(count >= back)
        def _():
            save(count - back, lax.rem(count - back, 2)).wait()


def owners(head_row, devices, rows_dev):
    limits = lax.broadcasted_iota(jnp.int32, (devices, head_row.shape[1]), 0) * rows_dev
    return jnp.sum((limits <= head_row).astype(F32), axis=0, keepdims=True) - 1.0


def ranks(owner_row):
    queries = owner_row.shape[1]
    across = jnp.broadcast_to(owner_row, (queries, queries))
    earlier = lax.broadcasted_iota(jnp.int32, (queries, queries), 0) < lax.broadcasted_iota(
        jnp.int32, (queries, queries), 1
    )
    same = (jnp.transpose(across) == across) & earlier
    return jnp.sum(same.astype(F32), axis=0, keepdims=True)


def far_kernel(
    half_rel,
    last,
    ahead,
    devices,
    base_ref,
    order_ref,
    src_ref,
    dst_ref,
    rel_ref,
    emb_ref,
    far_ref,
    in_ref,
    out_ref,
    loop_ref,
    loop_rel_ref,
    *rest,
):
    far_t_ref, gathered_ref, agg_ref, held_ref, own_ref, made_ref, sems, own_sems, out_sems = rest[-9:]
    if last:
        near_ref, query_rel_ref, relation_ref, rel_weight_ref, _ = rest[:5]
        hidden_ref, factor_ref = rest[5:7]
    else:
        head_ref, mixed_ref, hidden_ref, heads_ref, sent_ref, rank_ref, most_ref = rest[:7]
    blocks = src_ref.shape[0]
    rows_dev = blocks * BLK
    far_chunks = far_ref.shape[0]
    middle = middle_step(order_ref, blocks, ahead)
    start, stop = (middle, blocks // STEP) if last else (0, middle)

    def load(step, slot):
        return pltpu.make_async_copy(mixed_ref.at[step], held_ref.at[slot], sems.at[slot])

    def block_rows(step, u):
        return pl.ds(pl.multiple_of(order_ref[step * STEP + u] * BLK, BLK), BLK)

    def load_own(step, u):
        slot = lax.rem(step, 2)
        return pltpu.make_async_copy(
            emb_ref.at[block_rows(step, u)], own_ref.at[slot, u], own_sems.at[slot, u]
        )

    def give(step, u):
        rows = block_rows(step, u)
        return pltpu.make_async_copy(
            made_ref.at[rows], hidden_ref.at[rows], out_sems.at[step * STEP + u]
        )

    if not last:

        @pl.when(start < stop)
        def _():
            load(start, 0).start()

    def turn(j, carry):
        far_t_ref[j] = jnp.transpose(far_ref[j])
        return carry

    lax.fori_loop(0, far_chunks, turn, 0)
    if not last:
        made_ref[...] = jnp.zeros_like(made_ref)

    def look_up(src, u):
        if far_chunks == 1:
            return jnp.dot(
                far_t_ref[0], one_hot(src - rows_dev, CHUNK), preferred_element_type=F32
            )
        gathered_ref[u] = jnp.zeros(gathered_ref.shape[1:], F32)

        def one_chunk(j, carry):
            gathered_ref[u] += jnp.dot(
                far_t_ref[j],
                one_hot(src - rows_dev - j * CHUNK, CHUNK),
                preferred_element_type=F32,
            )
            return carry

        lax.fori_loop(0, far_chunks, one_chunk, 0)
        return gathered_ref[u]

    def finish(step, slot):
        own = own_ref[slot].reshape(STEP * BLK, own_ref.shape[-1])
        own = (own.astype(F32) * loop_rel_ref[...]).astype(BF16)
        preact = jnp.dot(agg_ref[0, slot], in_ref[...], preferred_element_type=F32)
        preact += jnp.dot(agg_ref[1, slot], out_ref[...], preferred_element_type=F32)
        preact += jnp.dot(own, loop_ref[...], preferred_element_type=F32)
        hidden = jnp.tanh(preact).astype(BF16)
        for u in range(STEP):
            made_ref[block_rows(step, u), :] = hidden[u * BLK : (u + 1) * BLK]

    def one_step(i, carry):
        slot = lax.rem(i, 2)
        step = start + i
        before = jnp.maximum(step - 1, start)

        @pl.when(i > 0)
        def _():
            for u in range(STEP):
                load_own(before, u).wait()

        for u in range(STEP):
            load_own(step, u).start()

        if not last:

            @pl.when(step + 1 < stop)
            def _():
                load(step + 1, 1 - slot).start()

            load(step, slot).wait()
        finish(before, lax.rem(step + 1, 2))
        rows = [pl.ds(order_ref[(start + i) * STEP + u], 1) for u in range(STEP)]
        srcs = [src_ref[row, :] for row in rows]
        found = [look_up(src, u) for u, src in enumerate(srcs)]
        composed = []
        for u, row in enumerate(rows):
            if last:
                near = jnp.dot(
                    near_ref[...], one_hot(srcs[u], rows_dev), preferred_element_type=F32
                )
                relation = jnp.dot(
                    relation_ref[...],
                    one_hot(rel_ref[row, :], relation_ref.shape[1]),
                    preferred_element_type=F32,
                )
                composed.append((found[u] + near).astype(BF16) * relation.astype(BF16))
            else:
                is_near = 1 - is_outside(srcs[u], rows_dev)
                composed.append((found[u].astype(BF16) + is_near) * held_ref[slot, u])
        for u, row in enumerate(rows):
            key = dst_ref[row, :] + jnp.where(rel_ref[row, :] >= half_rel, BLK, 0)
            selector = one_hot(key, 2 * BLK)
            counts = selector[:, :128]
            for lane in range(128, selector.shape[1], 128):
                counts = counts + selector[:, lane : lane + 128]
            counts = jnp.sum(counts.astype(F32), axis=1, keepdims=True)
            sums = lax.dot_general(selector, composed[u], NT, preferred_element_type=F32)
            agg = (sums * (1.0 / jnp.maximum(counts, 1.0))).astype(BF16)
            here = pl.ds(u * BLK, BLK)
            agg_ref[0, lax.rem(step, 2), here, :] = agg[:BLK]
            agg_ref[1, lax.rem(step, 2), here, :] = agg[BLK:]

        @pl.when(i > 0)
        def _():
            for u in range(STEP):
                give(before, u).start()

        return carry

    lax.fori_loop(0, stop - start, one_step, 0)

    @pl.when(start < stop)
    def _():
        for u in range(STEP):
            load_own(stop - 1, u).wait()
        finish(stop - 1, lax.rem(stop - 1, 2))
        for u in range(STEP):
            give(stop - 1, u).start()

    if last:
        picks = one_hot(query_rel_ref[...], relation_ref.shape[1])
        rows = lax.dot_general(
            picks, relation_ref[...], (((0,), (1,)), ((), ())), preferred_element_type=F32
        )
        factor_ref[...] = jnp.dot(
            rows.astype(BF16), rel_weight_ref[...], preferred_element_type=F32
        )
    else:
        picks = one_hot_wide(head_ref[...] - base_ref[0] * BLK, rows_dev)
        rows = lax.dot_general(picks, made_ref[...], TN, preferred_element_type=F32)
        rank = ranks(owners(head_ref[...], devices, rows_dev))
        slots = one_hot(rank.astype(jnp.int32), heads_ref.shape[0])
        packed = jnp.dot(slots, rows.astype(BF16), preferred_element_type=F32)
        heads_ref[...] = packed.astype(BF16)
        for peer in range(devices):
            sent_ref[peer] = packed[: sent_ref.shape[1]].astype(BF16)
        rank_ref[...] = rank.astype(jnp.int32)
        most_ref[0] = jnp.max(rank).astype(jnp.int32)

    def gave(step, carry):
        for u in range(STEP):
            give(step, u).wait()
        return carry

    lax.fori_loop(start, stop, gave, 0)


def pick_kernel(bit, member_ref, index_ref, emb_ref, kept_ref, sent_ref):
    rows_dev = emb_ref.shape[0]
    picks = one_hot(index_ref[...] - member_ref[0] * rows_dev, rows_dev)
    rows = lax.dot_general(picks, emb_ref[...], TN, preferred_element_type=F32)
    half = kept_ref.shape[0]
    upper = member_ref[0] & bit > 0
    kept_ref[...] = jnp.where(upper, rows[half:], rows[:half]).astype(BF16)
    sent_ref[...] = jnp.where(upper, rows[:half], rows[half:]).astype(BF16)


SMEM = pl.BlockSpec(memory_space=pltpu.SMEM)
WHOLE = pl.BlockSpec(memory_space=pltpu.VMEM)
HBM = pl.BlockSpec(memory_space=pltpu.HBM)


def near_call(ahead, base, query_head, src, rel, near, relation):
    columns, edges = near.shape[0], src.shape[1]
    blocks = src.shape[0]
    count = STEP * ahead
    flops = 2 * count * edges * columns * (near.shape[1] + relation.shape[1])
    return pl.pallas_call(
        functools.partial(near_kernel, ahead),
        out_shape=(
            jax.ShapeDtypeStruct((blocks // STEP, STEP, columns, edges), BF16),
            jax.ShapeDtypeStruct((blocks + 2,), jnp.int32),
        ),
        in_specs=[SMEM] * 2 + [WHOLE] * 4,
        out_specs=(HBM, SMEM),
        scratch_shapes=[
            pltpu.VMEM((2, STEP, columns, edges), BF16),
            pltpu.SemaphoreType.DMA((2,)),
        ],
        compiler_params=pltpu.CompilerParams(vmem_limit_bytes=VMEM_LIMIT),
        cost_estimate=pl.CostEstimate(
            flops=flops, bytes_accessed=2 * count * edges * columns, transcendentals=0
        ),
    )(base, query_head, src, rel, near, relation)


def far_call(half_rel, last, ahead, devices, scalars, edges, emb, far, weights, more, kept, outs):
    rows_dev, columns = emb.shape
    blocks, width = edges[0].shape
    return pl.pallas_call(
        functools.partial(far_kernel, half_rel, last, ahead, devices),
        out_shape=(jax.ShapeDtypeStruct((rows_dev, columns), BF16),) + outs,
        in_specs=[SMEM] * 2 + [WHOLE] * 3 + [HBM] + [WHOLE] * (5 + len(more)) + [HBM],
        out_specs=(HBM, WHOLE) if last else (HBM, WHOLE, WHOLE, WHOLE, SMEM),
        input_output_aliases={11 + len(more): 0} if last else {},
        scratch_shapes=[
            pltpu.VMEM((far.shape[0], columns, CHUNK), BF16),
            pltpu.VMEM((STEP, columns, width if far.shape[0] > 1 else 128), F32),
            pltpu.VMEM((2, 2, STEP * BLK, columns), BF16),
            pltpu.VMEM((2, STEP, columns, 128 if last else width), BF16),
            pltpu.VMEM((2, STEP, BLK, columns), BF16),
            pltpu.VMEM((rows_dev, columns), BF16),
            pltpu.SemaphoreType.DMA((2,)),
            pltpu.SemaphoreType.DMA((2, STEP)),
            pltpu.SemaphoreType.DMA((blocks,)),
        ],
        compiler_params=pltpu.CompilerParams(vmem_limit_bytes=FAR_LIMIT),
        cost_estimate=pl.CostEstimate(
            flops=blocks * width * columns * far.shape[0] * CHUNK,
            bytes_accessed=blocks * width * columns,
            transcendentals=0,
        ),
    )(*scalars, *edges, emb, far, *weights, *more, kept)


def score_kernel(
    devices,
    sent_ref,
    more_ref,
    rank_ref,
    head_ref,
    factor_hbm,
    hidden_hbm,
    scores_ref,
    payload_ref,
    factor_ref,
    hidden_ref,
    sems,
):
    copies = (
        pltpu.make_async_copy(factor_hbm, factor_ref, sems.at[0]),
        pltpu.make_async_copy(hidden_hbm, hidden_ref, sems.at[1]),
    )
    for copy in copies:
        copy.start()
    slots = sent_ref.shape[0] // devices
    owner = owners(head_ref[...], devices, hidden_ref.shape[0]).astype(jnp.int32)
    place = jnp.where(rank_ref[...] < slots, owner * slots + rank_ref[...], -1)
    picks = one_hot(place, sent_ref.shape[0])
    heads = lax.dot_general(picks, sent_ref[...], TN, preferred_element_type=F32)
    heads = heads + more_ref[...].astype(F32)
    for copy in copies:
        copy.wait()
    query = (heads * factor_ref[...]).astype(BF16)
    scores = lax.dot_general(query, hidden_ref[...], NT, preferred_element_type=F32)
    scores_ref[...] = scores
    top = jnp.max(scores, axis=1, keepdims=True)
    high = top.astype(BF16).astype(F32)
    low = (top - high).astype(BF16).astype(F32)
    top = high + low
    weights = jnp.exp(scores - top)
    total = jnp.sum(weights, axis=1, keepdims=True)
    weighted = jnp.dot(weights.astype(BF16), hidden_ref[...], preferred_element_type=F32)
    total_high = total.astype(BF16).astype(F32)
    lanes = lax.broadcasted_iota(jnp.int32, (query.shape[0], LANES), 1) % 4
    wide = jnp.where(lanes == 0, high, total - total_high)
    wide = jnp.where(lanes == 1, low, wide)
    wide = jnp.where(lanes == 2, total_high, wide)
    stats = jnp.transpose(wide)
    upper = lax.broadcasted_iota(jnp.int32, (8, LANES), 0) < 4
    figures = jnp.where(upper, stats[:8, :LANES], stats[:8, LANES:])
    share = query.shape[0] // payload_ref.shape[0]
    for peer in range(payload_ref.shape[0]):
        rows = weighted[peer * share : (peer + 1) * share]
        payload_ref[peer] = pack(rows[:, :LANES], rows[:, LANES:], figures)


def pack(left, right, figures):
    return jnp.concatenate([left, right, figures, figures], axis=0).astype(BF16)


def merge(data, first):
    share = (data.shape[1] - 16) // 2
    figures = data[:, 2 * share : 2 * share + 8]
    tops, totals, scales = [], [], []
    for half in (0, 4):
        each = figures[:, half : half + 1] + figures[:, half + 1 : half + 2]
        top = jnp.max(each, axis=0)
        scale = jnp.exp(each - top[None])
        total = figures[:, half + 2 : half + 3] + figures[:, half + 3 : half + 4]
        tops.append(top)
        totals.append(jnp.sum(total * scale, axis=0))
        scales.append(scale)
    left = right = 0.0
    for i in range(data.shape[0]):
        scale = jnp.where(first >= LANES, scales[1][i], scales[0][i])
        factor = column(scale, lax.rem(first, LANES), share)
        left += factor * data[i, :share]
        right += factor * data[i, share : 2 * share]
    return left, right, tops, totals


def column(row, first, rows):
    lanes = lax.broadcasted_iota(jnp.int32, (rows, LANES), 1)
    wanted = lax.broadcasted_iota(jnp.int32, (rows, LANES), 0) + first
    return jnp.sum(jnp.where(lanes == wanted, row, 0.0), axis=1, keepdims=True)


def merge_kernel(first_ref, received_ref, payload_ref):
    left, right, tops, totals = merge(received_ref[...].astype(F32), first_ref[0])
    row = lax.broadcasted_iota(jnp.int32, (8, LANES), 0)
    figures = jnp.zeros((8, LANES), F32)
    for half in range(2):
        for at, value in ((0, tops[half]), (2, totals[half])):
            high = value.astype(BF16).astype(F32)
            figures = jnp.where(row == 4 * half + at, high, figures)
            figures = jnp.where(row == 4 * half + at + 1, value - high, figures)
    block = pack(left, right, figures)
    for peer in range(payload_ref.shape[0]):
        payload_ref[peer] = block


def last_kernel(first_ref, received_ref, scores_ref, log_probs_ref, expected_ref):
    first = first_ref[0]
    left, right, tops, totals = merge(received_ref[...].astype(F32), first)
    for half in range(2):
        norm = column(tops[half] + jnp.log(totals[half]), 0, LANES)
        rows = pl.ds(half * LANES, LANES)
        log_probs_ref[rows, :] = scores_ref[rows, :] - norm
    total = jnp.where(first >= LANES, totals[1], totals[0])
    total = column(total, lax.rem(first, LANES), left.shape[0])
    expected_ref[:, :LANES] = left / total
    expected_ref[:, LANES:] = right / total


def body(
    entity_emb,
    relation_emb,
    in_weight,
    out_weight,
    loop_weight,
    rel_weight,
    loop_rel,
    edge_src,
    edge_dst,
    edge_rel,
    export_rows,
    query_head,
    query_rel,
):
    groups = lax.axis_size("ent")
    copies = lax.axis_size("rep")
    devices = groups * copies
    group = lax.axis_index("ent")
    member = lax.axis_index("rep")
    device = group * copies + member
    rows_dev, columns = entity_emb.shape
    queries = query_head.shape[0]

    blocks = edge_src.shape[0]
    relations = relation_emb.shape[0]
    ahead = min(AHEAD, blocks // STEP)

    slots = export_rows.shape[1]
    bit = copies // 2
    half = slots // 2
    half_type = jax.ShapeDtypeStruct((half, columns), BF16)
    kept, gone = pl.pallas_call(
        functools.partial(pick_kernel, bit),
        out_shape=(half_type, half_type),
        in_specs=[SMEM, WHOLE, WHOLE],
        out_specs=(WHOLE, WHOLE),
        compiler_params=pltpu.CompilerParams(vmem_limit_bytes=VMEM_LIMIT),
    )(member[None], export_rows, entity_emb)
    gone, later_relation = lax.optimization_barrier((gone, relation_emb))
    rel_count = -(-relations // 256) * 256
    relation_t = jnp.pad(later_relation, ((0, rel_count - relations), (0, 0))).T
    near_t = entity_emb.T
    while True:
        pairs = [(one, one ^ bit) for one in range(copies)]
        mine = kept + lax.ppermute(gone, "rep", pairs)
        bit //= 2
        if bit == 0:
            break
        half //= 2
        upper = (member & bit > 0).astype(jnp.int32)
        kept = lax.dynamic_slice_in_dim(mine, upper * half, half, 0)
        gone = lax.dynamic_slice_in_dim(mine, (1 - upper) * half, half, 0)
    mine, near_t = lax.optimization_barrier((mine, near_t))
    spread = jnp.broadcast_to(mine[None], (devices,) + mine.shape)
    table = lax.all_to_all(spread, BOTH, 0, 0).reshape(groups * slots, columns)
    base = (device * blocks)[None]
    mixed, order = near_call(
        ahead, base, query_head, edge_src, edge_rel, near_t, relation_t
    )
    far_count = -(-(groups * slots) // CHUNK) * CHUNK
    far = jnp.pad(table, ((0, far_count - groups * slots), (0, 0)))
    far = far.reshape(far_count // CHUNK, CHUNK, columns)

    head_row = query_head[None]
    weights = (in_weight, out_weight, loop_weight, loop_rel[None])
    edges = (edge_src, edge_dst, edge_rel)
    cap = min(queries, -(-3 * queries // (8 * devices)) * 8)
    hidden, heads, spread, rank, most = far_call(
        relations // 2,
        False,
        ahead,
        devices,
        (base, order),
        edges,
        entity_emb,
        far,
        weights,
        (head_row,),
        mixed,
        (
            jax.ShapeDtypeStruct((-(-queries // cap) * cap, columns), BF16),
            jax.ShapeDtypeStruct((devices, cap, columns), BF16),
            jax.ShapeDtypeStruct((1, queries), jnp.int32),
            jax.ShapeDtypeStruct((1,), jnp.int32),
        ),
    )

    def send_round(turn):
        some = lax.dynamic_slice_in_dim(heads, turn * cap, cap, 0)
        spread = jnp.broadcast_to(some[None], (devices,) + some.shape)
        return lax.all_to_all(spread, BOTH, 0, 0).reshape(devices * cap, columns)

    def another_round(state):
        turn, more = state
        slot = rank[0] - turn * cap
        place = query_head // rows_dev * cap + slot
        rows = jnp.take(send_round(turn), jnp.clip(place, 0, devices * cap - 1), axis=0)
        inside = (slot >= 0) & (slot < cap)
        return turn + 1, jnp.where(inside[:, None], rows, more)

    sent = lax.all_to_all(spread, BOTH, 0, 0).reshape(devices * cap, columns)
    hidden, query_factor = far_call(
        relations // 2,
        True,
        ahead,
        devices,
        (base, order),
        edges,
        entity_emb,
        far,
        weights,
        (near_t, query_rel[None], relation_t, rel_weight),
        hidden,
        (jax.ShapeDtypeStruct((queries, columns), F32),),
    )
    _, more_heads = lax.while_loop(
        lambda state: state[0] * cap <= most[0],
        another_round,
        (jnp.int32(1), jnp.zeros((queries, columns), BF16)),
    )

    batch_rows = queries // copies
    first = (member * batch_rows)[None]
    part = (2 * batch_rows + 16, LANES)
    few = pltpu.CompilerParams(vmem_limit_bytes=SCORE_LIMIT)
    scores, payload = pl.pallas_call(
        functools.partial(score_kernel, devices),
        out_shape=(
            jax.ShapeDtypeStruct((queries, rows_dev), F32),
            jax.ShapeDtypeStruct((copies,) + part, BF16),
        ),
        in_specs=[WHOLE] * 4 + [HBM] * 2,
        out_specs=(WHOLE, WHOLE),
        scratch_shapes=[
            pltpu.VMEM((queries, columns), F32),
            pltpu.VMEM((rows_dev, columns), BF16),
            pltpu.SemaphoreType.DMA((2,)),
        ],
        compiler_params=pltpu.CompilerParams(vmem_limit_bytes=FIRST_LIMIT),
    )(sent, more_heads, rank, head_row, query_factor, hidden)
    payload = pl.pallas_call(
        merge_kernel,
        out_shape=jax.ShapeDtypeStruct((groups,) + part, BF16),
        in_specs=[SMEM, WHOLE],
        out_specs=WHOLE,
        compiler_params=few,
    )(first, lax.all_to_all(payload, "rep", 0, 0))
    log_probs, expected_tail = pl.pallas_call(
        last_kernel,
        out_shape=(
            jax.ShapeDtypeStruct((queries, rows_dev), F32),
            jax.ShapeDtypeStruct((batch_rows, columns), F32),
        ),
        in_specs=[SMEM, WHOLE, WHOLE],
        out_specs=(WHOLE, WHOLE),
        compiler_params=few,
    )(first, lax.all_to_all(payload, "ent", 0, 0), scores)
    return (log_probs, expected_tail)


def solution(mesh):
    placed = (
        P(("ent", "rep"), None),
        P(),
        P(),
        P(),
        P(),
        P(),
        P(),
        P(("ent", "rep"), None),
        P(("ent", "rep"), None),
        P(("ent", "rep"), None),
        P("ent", None),
        P(),
        P(),
    )
    return jax.shard_map(
        body,
        mesh=mesh,
        in_specs=placed,
        out_specs=(P(None, ("ent", "rep")), P("rep", None)),
        check_vma=False,
    )
```

```python
import functools

import jax
import jax.numpy as jnp
from jax import lax
from jax.experimental import pallas as pl
from jax.experimental.pallas import tpu as pltpu
from jax.sharding import PartitionSpec as P

BLK = 128
CHUNK = 1024
NARROW = 768
LANES = 128
BF16 = jnp.bfloat16
F32 = jnp.float32
BOTH = ("ent", "rep")
NT = (((1,), (1,)), ((), ()))
TN = (((0,), (0,)), ((), ()))
VMEM_LIMIT = 56 * 2**20
STEP = 2
AHEAD = 6
SCORE_LIMIT = 24 * 2**20


def one_hot(index, rows):
    where = lax.broadcasted_iota(jnp.int16, (rows, index.shape[1]), 0) == index.astype(jnp.int16)
    return jnp.where(where, jnp.asarray(1, BF16), jnp.asarray(0, BF16))


def one_hot_wide(index, rows):
    where = lax.broadcasted_iota(jnp.int32, (rows, index.shape[1]), 0) == index
    return where.astype(F32).astype(BF16)


def is_outside(src, rows_dev):
    return jnp.where(src < rows_dev, 0.0, 1.0).astype(BF16)


def border_place(slot):
    shard = (slot >> 7) & 7
    low = slot & 63
    place = jnp.where((slot & 64) == 0, shard * 64, 512 + (shard ^ 4) * 64) + low
    return jnp.where(slot < 0, -1, (slot >> 10) * CHUNK + place)


def reordered(rows):
    first = [rows[shard * 128 : shard * 128 + 64] for shard in range(8)]
    second = [rows[shard * 128 + 64 : shard * 128 + 128] for shard in (4, 5, 6, 7, 0, 1, 2, 3)]
    return jnp.concatenate(first + second, axis=0)


def order_blocks(head_ref, first_block, blocks, order_ref):
    def mark(q, marks):
        block = lax.shift_right_arithmetic(head_ref[q], BLK.bit_length() - 1) - first_block
        inside = (block >= 0) & (block < blocks)
        return marks | jnp.where(inside, lax.shift_left(1, jnp.where(inside, block, 0)), 0)

    marks = lax.fori_loop(0, head_ref.shape[0], mark, jnp.int32(0), unroll=16)
    position = jnp.int32(0)
    for wanted in (1, 0):
        for b in range(blocks):
            taken = (lax.shift_right_logical(marks, b) & 1) == wanted
            order_ref[jnp.where(taken, position, blocks + 1)] = jnp.int32(b)
            position = position + taken.astype(jnp.int32)
        if wanted:
            found = position
    order_ref[blocks] = found


def middle_step(order_ref, blocks, ahead):
    return jnp.maximum((order_ref[blocks] + STEP - 1) // STEP, ahead)


def near_kernel(
    ahead,
    base_ref,
    head_ref,
    src_ref,
    rel_ref,
    near_ref,
    relation_ref,
    mixed_ref,
    order_ref,
    wide_ref,
    held_ref,
    sems,
):
    blocks = src_ref.shape[0]
    rows_dev = near_ref.shape[1]
    order_blocks(head_ref, base_ref[0], blocks, order_ref)
    places = border_place(src_ref[...] - rows_dev)
    wide_ref[0] = jnp.max((places >= NARROW).astype(F32)).astype(jnp.int32)
    count = middle_step(order_ref, blocks, ahead)

    def save(step, slot):
        return pltpu.make_async_copy(held_ref.at[slot], mixed_ref.at[step], sems.at[slot])

    def one_step(i, carry):
        slot = lax.rem(i, 2)

        @pl.when(i >= 2)
        def _():
            save(i - 2, slot).wait()

        for u in range(STEP):
            block = order_ref[i * STEP + u]
            src = src_ref[pl.ds(block, 1), :]
            rel = rel_ref[pl.ds(block, 1), :]
            gathered = jnp.dot(near_ref[...], one_hot(src, rows_dev), preferred_element_type=F32)
            relation = jnp.dot(
                relation_ref[...],
                one_hot(rel, relation_ref.shape[1]),
                preferred_element_type=F32,
            )
            is_far = is_outside(src, rows_dev)
            held_ref[slot, u] = (gathered.astype(BF16) + is_far) * relation.astype(BF16)
        save(i, slot).start()
        return carry

    lax.fori_loop(0, count, one_step, 0)
    for back in (2, 1):

        @pl.when(count >= back)
        def _():
            save(count - back, lax.rem(count - back, 2)).wait()


def owners(head_row, devices, rows_dev):
    limits = lax.broadcasted_iota(jnp.int32, (devices, head_row.shape[1]), 0) * rows_dev
    return jnp.sum((limits <= head_row).astype(F32), axis=0, keepdims=True) - 1.0


def ranks(owner_row):
    queries = owner_row.shape[1]
    across = jnp.broadcast_to(owner_row, (queries, queries))
    earlier = lax.broadcasted_iota(jnp.int32, (queries, queries), 0) < lax.broadcasted_iota(
        jnp.int32, (queries, queries), 1
    )
    same = (jnp.transpose(across) == across) & earlier
    return jnp.sum(same.astype(F32), axis=0, keepdims=True)


def far_kernel(
    half_rel,
    last,
    ahead,
    devices,
    base_ref,
    order_ref,
    wide_ref,
    src_ref,
    dst_ref,
    rel_ref,
    emb_ref,
    far_ref,
    in_ref,
    out_ref,
    loop_ref,
    loop_rel_ref,
    *rest,
):
    far_t_ref, gathered_ref, agg_ref, held_ref, own_ref, made_ref, sems, own_sems, out_sems = rest[-9:]
    if last:
        near_ref, relation_ref, _, hidden_ref = rest[:4]
    else:
        head_ref, query_rel_ref, relation_ref, rel_weight_ref, mixed_ref = rest[:5]
        hidden_ref, heads_ref, factor_ref, rank_ref, most_ref = rest[5:10]
    blocks = src_ref.shape[0]
    rows_dev = blocks * BLK
    far_chunks = far_ref.shape[0]
    middle = middle_step(order_ref, blocks, ahead)
    start, stop = (middle, blocks // STEP) if last else (0, middle)

    def load(step, slot):
        return pltpu.make_async_copy(mixed_ref.at[step], held_ref.at[slot], sems.at[slot])

    def block_rows(step, u):
        return pl.ds(pl.multiple_of(order_ref[step * STEP + u] * BLK, BLK), BLK)

    def load_own(step, u):
        slot = lax.rem(step, 2)
        return pltpu.make_async_copy(
            emb_ref.at[block_rows(step, u)], own_ref.at[slot, u], own_sems.at[slot, u]
        )

    def give(step, u):
        rows = block_rows(step, u)
        return pltpu.make_async_copy(
            made_ref.at[rows], hidden_ref.at[rows], out_sems.at[step * STEP + u]
        )

    if not last:

        @pl.when(start < stop)
        def _():
            load(start, 0).start()

    def turn(j, carry):
        far_t_ref[j] = jnp.transpose(reordered(far_ref[j]))
        return carry

    lax.fori_loop(0, far_chunks, turn, 0)
    if not last:
        made_ref[...] = jnp.zeros_like(made_ref)

    def look_up(src, u, depth):
        place = border_place(src - rows_dev)
        if far_chunks == 1:
            return jnp.dot(
                far_t_ref[0, :, :depth], one_hot(place, depth), preferred_element_type=F32
            )
        gathered_ref[u] = jnp.zeros(gathered_ref.shape[1:], F32)

        def one_chunk(j, carry):
            gathered_ref[u] += jnp.dot(
                far_t_ref[j], one_hot(place - j * CHUNK, CHUNK), preferred_element_type=F32
            )
            return carry

        lax.fori_loop(0, far_chunks, one_chunk, 0)
        return gathered_ref[u]

    def finish(step, slot):
        own = own_ref[slot].reshape(STEP * BLK, own_ref.shape[-1])
        own = (own.astype(F32) * loop_rel_ref[...]).astype(BF16)
        preact = jnp.dot(agg_ref[0, slot], in_ref[...], preferred_element_type=F32)
        preact += jnp.dot(agg_ref[1, slot], out_ref[...], preferred_element_type=F32)
        preact += jnp.dot(own, loop_ref[...], preferred_element_type=F32)
        hidden = jnp.tanh(preact).astype(BF16)
        for u in range(STEP):
            made_ref[block_rows(step, u), :] = hidden[u * BLK : (u + 1) * BLK]

    def one_step(i, carry):
        slot = lax.rem(i, 2)
        step = start + i
        before = jnp.maximum(step - 1, start)

        @pl.when(i > 0)
        def _():
            for u in range(STEP):
                load_own(before, u).wait()

        for u in range(STEP):
            load_own(step, u).start()

        if not last:

            @pl.when(step + 1 < stop)
            def _():
                load(step + 1, 1 - slot).start()

            load(step, slot).wait()
        def work(depth):
            finish(before, lax.rem(step + 1, 2))
            rows = [pl.ds(order_ref[(start + i) * STEP + u], 1) for u in range(STEP)]
            srcs = [src_ref[row, :] for row in rows]
            found = [look_up(src, u, depth) for u, src in enumerate(srcs)]
            composed = []
            for u, row in enumerate(rows):
                if last:
                    near = jnp.dot(
                        near_ref[...], one_hot(srcs[u], rows_dev), preferred_element_type=F32
                    )
                    relation = jnp.dot(
                        relation_ref[...],
                        one_hot(rel_ref[row, :], relation_ref.shape[1]),
                        preferred_element_type=F32,
                    )
                    composed.append((found[u] + near).astype(BF16) * relation.astype(BF16))
                else:
                    is_near = 1 - is_outside(srcs[u], rows_dev)
                    composed.append((found[u].astype(BF16) + is_near) * held_ref[slot, u])
            for u, row in enumerate(rows):
                key = dst_ref[row, :] + jnp.where(rel_ref[row, :] >= half_rel, BLK, 0)
                selector = one_hot(key, 2 * BLK)
                counts = selector[:, :128]
                for lane in range(128, selector.shape[1], 128):
                    counts = counts + selector[:, lane : lane + 128]
                counts = jnp.sum(counts.astype(F32), axis=1, keepdims=True)
                sums = lax.dot_general(selector, composed[u], NT, preferred_element_type=F32)
                agg = (sums * (1.0 / jnp.maximum(counts, 1.0))).astype(BF16)
                here = pl.ds(u * BLK, BLK)
                agg_ref[0, lax.rem(step, 2), here, :] = agg[:BLK]
                agg_ref[1, lax.rem(step, 2), here, :] = agg[BLK:]

        if far_chunks == 1:
            pl.when(wide_ref[0] == 0)(functools.partial(work, NARROW))
            pl.when(wide_ref[0] != 0)(functools.partial(work, CHUNK))
        else:
            work(CHUNK)

        @pl.when(i > 0)
        def _():
            for u in range(STEP):
                give(before, u).start()

        return carry

    lax.fori_loop(0, stop - start, one_step, 0)

    @pl.when(start < stop)
    def _():
        for u in range(STEP):
            load_own(stop - 1, u).wait()
        finish(stop - 1, lax.rem(stop - 1, 2))
        for u in range(STEP):
            give(stop - 1, u).start()

    if not last:
        picks = one_hot(query_rel_ref[...], relation_ref.shape[1])
        rows = lax.dot_general(
            picks, relation_ref[...], (((0,), (1,)), ((), ())), preferred_element_type=F32
        )
        factor_ref[...] = jnp.dot(
            rows.astype(BF16), rel_weight_ref[...], preferred_element_type=F32
        )
        picks = one_hot_wide(head_ref[...] - base_ref[0] * BLK, rows_dev)
        rows = lax.dot_general(picks, made_ref[...], TN, preferred_element_type=F32)
        rank = ranks(owners(head_ref[...], devices, rows_dev))
        slots = one_hot(rank.astype(jnp.int32), heads_ref.shape[0])
        heads_ref[...] = jnp.dot(slots, rows.astype(BF16), preferred_element_type=F32).astype(BF16)
        rank_ref[...] = rank.astype(jnp.int32)
        most_ref[0] = jnp.max(rank).astype(jnp.int32)

    def gave(step, carry):
        for u in range(STEP):
            give(step, u).wait()
        return carry

    lax.fori_loop(start, stop, gave, 0)


def pick_kernel(base_ref, index_ref, emb_ref, offered_ref):
    picks = one_hot(index_ref[...] - base_ref[0], emb_ref.shape[0])
    offered_ref[...] = lax.dot_general(
        picks, emb_ref[...], TN, preferred_element_type=F32
    ).astype(BF16)


SMEM = pl.BlockSpec(memory_space=pltpu.SMEM)
WHOLE = pl.BlockSpec(memory_space=pltpu.VMEM)
HBM = pl.BlockSpec(memory_space=pltpu.HBM)


def near_call(ahead, base, query_head, src, rel, near, relation):
    columns, edges = near.shape[0], src.shape[1]
    blocks = src.shape[0]
    count = STEP * ahead
    flops = 2 * count * edges * columns * (near.shape[1] + relation.shape[1])
    return pl.pallas_call(
        functools.partial(near_kernel, ahead),
        out_shape=(
            jax.ShapeDtypeStruct((blocks // STEP, STEP, columns, edges), BF16),
            jax.ShapeDtypeStruct((blocks + 2,), jnp.int32),
            jax.ShapeDtypeStruct((1,), jnp.int32),
        ),
        in_specs=[SMEM] * 2 + [WHOLE] * 4,
        out_specs=(HBM, SMEM, SMEM),
        scratch_shapes=[
            pltpu.VMEM((2, STEP, columns, edges), BF16),
            pltpu.SemaphoreType.DMA((2,)),
        ],
        compiler_params=pltpu.CompilerParams(vmem_limit_bytes=VMEM_LIMIT),
        cost_estimate=pl.CostEstimate(
            flops=flops, bytes_accessed=2 * count * edges * columns, transcendentals=0
        ),
    )(base, query_head, src, rel, near, relation)


def far_call(half_rel, last, ahead, devices, scalars, edges, emb, far, weights, more, kept, outs):
    rows_dev, columns = emb.shape
    blocks, width = edges[0].shape
    return pl.pallas_call(
        functools.partial(far_kernel, half_rel, last, ahead, devices),
        out_shape=(jax.ShapeDtypeStruct((rows_dev, columns), BF16),) + outs,
        in_specs=[SMEM] * 3 + [WHOLE] * 3 + [HBM] + [WHOLE] * (5 + len(more)) + [HBM],
        out_specs=(HBM,) if last else (HBM, WHOLE, WHOLE, WHOLE, SMEM),
        input_output_aliases={12 + len(more): 0} if last else {},
        scratch_shapes=[
            pltpu.VMEM((far.shape[0], columns, CHUNK), BF16),
            pltpu.VMEM((STEP, columns, width if far.shape[0] > 1 else 128), F32),
            pltpu.VMEM((2, 2, STEP * BLK, columns), BF16),
            pltpu.VMEM((2, STEP, columns, 128 if last else width), BF16),
            pltpu.VMEM((2, STEP, BLK, columns), BF16),
            pltpu.VMEM((rows_dev, columns), BF16),
            pltpu.SemaphoreType.DMA((2,)),
            pltpu.SemaphoreType.DMA((2, STEP)),
            pltpu.SemaphoreType.DMA((blocks,)),
        ],
        compiler_params=pltpu.CompilerParams(vmem_limit_bytes=VMEM_LIMIT),
        cost_estimate=pl.CostEstimate(
            flops=blocks * width * columns * far.shape[0] * CHUNK,
            bytes_accessed=blocks * width * columns,
            transcendentals=0,
        ),
    )(*scalars, *edges, emb, far, *weights, *more, kept)


def score_kernel(
    devices,
    sent_ref,
    more_ref,
    rank_ref,
    head_ref,
    factor_hbm,
    hidden_hbm,
    scores_ref,
    payload_ref,
    factor_ref,
    hidden_ref,
    sems,
):
    copies = (
        pltpu.make_async_copy(factor_hbm, factor_ref, sems.at[0]),
        pltpu.make_async_copy(hidden_hbm, hidden_ref, sems.at[1]),
    )
    for copy in copies:
        copy.start()
    slots = sent_ref.shape[0] // devices
    owner = owners(head_ref[...], devices, hidden_ref.shape[0]).astype(jnp.int32)
    place = jnp.where(rank_ref[...] < slots, owner * slots + rank_ref[...], -1)
    picks = one_hot(place, sent_ref.shape[0])
    heads = lax.dot_general(picks, sent_ref[...], TN, preferred_element_type=F32)
    heads = heads + more_ref[...].astype(F32)
    for copy in copies:
        copy.wait()
    query = (heads * factor_ref[...]).astype(BF16)
    scores = lax.dot_general(query, hidden_ref[...], NT, preferred_element_type=F32)
    scores_ref[...] = scores
    top = jnp.max(scores, axis=1, keepdims=True)
    high = top.astype(BF16).astype(F32)
    low = (top - high).astype(BF16).astype(F32)
    top = high + low
    weights = jnp.exp(scores - top)
    total = jnp.sum(weights, axis=1, keepdims=True)
    weighted = jnp.dot(weights.astype(BF16), hidden_ref[...], preferred_element_type=F32)
    total_high = total.astype(BF16).astype(F32)
    lanes = lax.broadcasted_iota(jnp.int32, (query.shape[0], LANES), 1) % 4
    wide = jnp.where(lanes == 0, high, total - total_high)
    wide = jnp.where(lanes == 1, low, wide)
    wide = jnp.where(lanes == 2, total_high, wide)
    stats = jnp.transpose(wide)
    upper = lax.broadcasted_iota(jnp.int32, (8, LANES), 0) < 4
    figures = jnp.where(upper, stats[:8, :LANES], stats[:8, LANES:])
    share = query.shape[0] // payload_ref.shape[0]
    for peer in range(payload_ref.shape[0]):
        rows = weighted[peer * share : (peer + 1) * share]
        payload_ref[peer] = pack(rows[:, :LANES], rows[:, LANES:], figures)


def pack(left, right, figures):
    return jnp.concatenate([left, right, figures, figures], axis=0).astype(BF16)


def merge(data, first):
    share = (data.shape[1] - 16) // 2
    figures = data[:, 2 * share : 2 * share + 8]
    tops, totals, scales = [], [], []
    for half in (0, 4):
        each = figures[:, half : half + 1] + figures[:, half + 1 : half + 2]
        top = jnp.max(each, axis=0)
        scale = jnp.exp(each - top[None])
        total = figures[:, half + 2 : half + 3] + figures[:, half + 3 : half + 4]
        tops.append(top)
        totals.append(jnp.sum(total * scale, axis=0))
        scales.append(scale)
    left = right = 0.0
    for i in range(data.shape[0]):
        scale = jnp.where(first >= LANES, scales[1][i], scales[0][i])
        factor = column(scale, lax.rem(first, LANES), share)
        left += factor * data[i, :share]
        right += factor * data[i, share : 2 * share]
    return left, right, tops, totals


def column(row, first, rows):
    lanes = lax.broadcasted_iota(jnp.int32, (rows, LANES), 1)
    wanted = lax.broadcasted_iota(jnp.int32, (rows, LANES), 0) + first
    return jnp.sum(jnp.where(lanes == wanted, row, 0.0), axis=1, keepdims=True)


def merge_kernel(first_ref, received_ref, payload_ref):
    left, right, tops, totals = merge(received_ref[...].astype(F32), first_ref[0])
    row = lax.broadcasted_iota(jnp.int32, (8, LANES), 0)
    figures = jnp.zeros((8, LANES), F32)
    for half in range(2):
        for at, value in ((0, tops[half]), (2, totals[half])):
            high = value.astype(BF16).astype(F32)
            figures = jnp.where(row == 4 * half + at, high, figures)
            figures = jnp.where(row == 4 * half + at + 1, value - high, figures)
    block = pack(left, right, figures)
    for peer in range(payload_ref.shape[0]):
        payload_ref[peer] = block


def last_kernel(first_ref, received_ref, scores_ref, log_probs_ref, expected_ref):
    first = first_ref[0]
    left, right, tops, totals = merge(received_ref[...].astype(F32), first)
    for half in range(2):
        norm = column(tops[half] + jnp.log(totals[half]), 0, LANES)
        rows = pl.ds(half * LANES, LANES)
        log_probs_ref[rows, :] = scores_ref[rows, :] - norm
    total = jnp.where(first >= LANES, totals[1], totals[0])
    total = column(total, lax.rem(first, LANES), left.shape[0])
    expected_ref[:, :LANES] = left / total
    expected_ref[:, LANES:] = right / total


def body(
    entity_emb,
    relation_emb,
    in_weight,
    out_weight,
    loop_weight,
    rel_weight,
    loop_rel,
    edge_src,
    edge_dst,
    edge_rel,
    export_rows,
    query_head,
    query_rel,
):
    groups = lax.axis_size("ent")
    copies = lax.axis_size("rep")
    devices = groups * copies
    group = lax.axis_index("ent")
    member = lax.axis_index("rep")
    device = group * copies + member
    rows_dev, columns = entity_emb.shape
    queries = query_head.shape[0]

    blocks = edge_src.shape[0]
    relations = relation_emb.shape[0]
    ahead = min(AHEAD, blocks // STEP)

    slots = export_rows.shape[1]
    offered = pl.pallas_call(
        pick_kernel,
        out_shape=jax.ShapeDtypeStruct((slots, columns), BF16),
        in_specs=[SMEM, WHOLE, WHOLE],
        out_specs=WHOLE,
        compiler_params=pltpu.CompilerParams(vmem_limit_bytes=VMEM_LIMIT),
    )((member * rows_dev)[None], export_rows, entity_emb)
    offered, later_relation = lax.optimization_barrier((offered, relation_emb))
    rel_count = -(-relations // 256) * 256
    relation_t = jnp.pad(later_relation, ((0, rel_count - relations), (0, 0))).T
    near_t = entity_emb.T
    pieces = lax.all_to_all(offered, "rep", 0, 0, tiled=True)
    mine = jnp.sum(
        pieces.reshape(copies, slots // copies, columns).astype(F32), axis=0
    ).astype(BF16)
    mine, near_t = lax.optimization_barrier((mine, near_t))
    spread = jnp.broadcast_to(mine[None], (devices,) + mine.shape)
    table = lax.all_to_all(spread, BOTH, 0, 0).reshape(groups * slots, columns)
    base = (device * blocks)[None]
    mixed, order, wide = near_call(
        ahead, base, query_head, edge_src, edge_rel, near_t, relation_t
    )
    far_count = -(-(groups * slots) // CHUNK) * CHUNK
    far = jnp.pad(table, ((0, far_count - groups * slots), (0, 0)))
    far = far.reshape(far_count // CHUNK, CHUNK, columns)

    head_row = query_head[None]
    weights = (in_weight, out_weight, loop_weight, loop_rel[None])
    edges = (edge_src, edge_dst, edge_rel)
    cap = min(queries, -(-3 * queries // (8 * devices)) * 8)
    hidden, heads, query_factor, rank, most = far_call(
        relations // 2,
        False,
        ahead,
        devices,
        (base, order, wide),
        edges,
        entity_emb,
        far,
        weights,
        (head_row, query_rel[None], relation_t, rel_weight),
        mixed,
        (
            jax.ShapeDtypeStruct((-(-queries // cap) * cap, columns), BF16),
            jax.ShapeDtypeStruct((queries, columns), F32),
            jax.ShapeDtypeStruct((1, queries), jnp.int32),
            jax.ShapeDtypeStruct((1,), jnp.int32),
        ),
    )

    def send_round(turn):
        some = lax.dynamic_slice_in_dim(heads, turn * cap, cap, 0)
        spread = jnp.broadcast_to(some[None], (devices,) + some.shape)
        return lax.all_to_all(spread, BOTH, 0, 0).reshape(devices * cap, columns)

    def another_round(state):
        turn, more = state
        slot = rank[0] - turn * cap
        place = query_head // rows_dev * cap + slot
        rows = jnp.take(send_round(turn), jnp.clip(place, 0, devices * cap - 1), axis=0)
        inside = (slot >= 0) & (slot < cap)
        return turn + 1, jnp.where(inside[:, None], rows, more)

    sent = send_round(0)
    (hidden,) = far_call(
        relations // 2,
        True,
        ahead,
        devices,
        (base, order, wide),
        edges,
        entity_emb,
        far,
        weights,
        (near_t, relation_t),
        hidden,
        (),
    )
    _, more_heads = lax.while_loop(
        lambda state: state[0] * cap <= most[0],
        another_round,
        (jnp.int32(1), jnp.zeros((queries, columns), BF16)),
    )

    batch_rows = queries // copies
    first = (member * batch_rows)[None]
    part = (2 * batch_rows + 16, LANES)
    few = pltpu.CompilerParams(vmem_limit_bytes=SCORE_LIMIT)
    scores, payload = pl.pallas_call(
        functools.partial(score_kernel, devices),
        out_shape=(
            jax.ShapeDtypeStruct((queries, rows_dev), F32),
            jax.ShapeDtypeStruct((copies,) + part, BF16),
        ),
        in_specs=[WHOLE] * 4 + [HBM] * 2,
        out_specs=(WHOLE, WHOLE),
        scratch_shapes=[
            pltpu.VMEM((queries, columns), F32),
            pltpu.VMEM((rows_dev, columns), BF16),
            pltpu.SemaphoreType.DMA((2,)),
        ],
        compiler_params=few,
    )(sent, more_heads, rank, head_row, query_factor, hidden)
    payload = pl.pallas_call(
        merge_kernel,
        out_shape=jax.ShapeDtypeStruct((groups,) + part, BF16),
        in_specs=[SMEM, WHOLE],
        out_specs=WHOLE,
        compiler_params=few,
    )(first, lax.all_to_all(payload, "rep", 0, 0))
    log_probs, expected_tail = pl.pallas_call(
        last_kernel,
        out_shape=(
            jax.ShapeDtypeStruct((queries, rows_dev), F32),
            jax.ShapeDtypeStruct((batch_rows, columns), F32),
        ),
        in_specs=[SMEM, WHOLE, WHOLE],
        out_specs=(WHOLE, WHOLE),
        compiler_params=few,
    )(first, lax.all_to_all(payload, "ent", 0, 0), scores)
    return (log_probs, expected_tail)


def solution(mesh):
    placed = (
        P(("ent", "rep"), None),
        P(),
        P(),
        P(),
        P(),
        P(),
        P(),
        P(("ent", "rep"), None),
        P(("ent", "rep"), None),
        P(("ent", "rep"), None),
        P("ent", None),
        P(),
        P(),
    )
    return jax.shard_map(
        body,
        mesh=mesh,
        in_specs=placed,
        out_specs=(P(None, ("ent", "rep")), P("rep", None)),
        check_vma=False,
    )
```

```python
import functools

import jax
import jax.numpy as jnp
from jax import lax
from jax.experimental import pallas as pl
from jax.experimental.pallas import tpu as pltpu
from jax.sharding import PartitionSpec as P

BLK = 128
CHUNK = 1024
LANES = 128
BF16 = jnp.bfloat16
F32 = jnp.float32
BOTH = ("ent", "rep")
NT = (((1,), (1,)), ((), ()))
TN = (((0,), (0,)), ((), ()))
VMEM_LIMIT = 56 * 2**20
STEP = 2
AHEAD = 6
SCORE_LIMIT = 24 * 2**20


def one_hot(index, rows):
    where = lax.broadcasted_iota(jnp.int16, (rows, index.shape[1]), 0) == index.astype(jnp.int16)
    return jnp.where(where, jnp.asarray(1, BF16), jnp.asarray(0, BF16))


def one_hot_wide(index, rows):
    where = lax.broadcasted_iota(jnp.int32, (rows, index.shape[1]), 0) == index
    return where.astype(F32).astype(BF16)


def is_outside(src, rows_dev):
    return jnp.where(src < rows_dev, 0.0, 1.0).astype(BF16)


def order_blocks(head_ref, first_block, blocks, order_ref):
    def mark(q, marks):
        block = lax.shift_right_arithmetic(head_ref[q], BLK.bit_length() - 1) - first_block
        inside = (block >= 0) & (block < blocks)
        return marks | jnp.where(inside, lax.shift_left(1, jnp.where(inside, block, 0)), 0)

    marks = lax.fori_loop(0, head_ref.shape[0], mark, jnp.int32(0), unroll=16)
    position = jnp.int32(0)
    for wanted in (1, 0):
        for b in range(blocks):
            taken = (lax.shift_right_logical(marks, b) & 1) == wanted
            order_ref[jnp.where(taken, position, blocks + 1)] = jnp.int32(b)
            position = position + taken.astype(jnp.int32)
        if wanted:
            found = position
    order_ref[blocks] = found


def middle_step(order_ref, blocks, ahead):
    return jnp.maximum((order_ref[blocks] + STEP - 1) // STEP, ahead)


def near_kernel(
    ahead,
    base_ref,
    head_ref,
    src_ref,
    rel_ref,
    near_ref,
    relation_ref,
    mixed_ref,
    order_ref,
    held_ref,
    sems,
):
    blocks = src_ref.shape[0]
    rows_dev = near_ref.shape[1]
    order_blocks(head_ref, base_ref[0], blocks, order_ref)
    count = middle_step(order_ref, blocks, ahead)

    def save(step, slot):
        return pltpu.make_async_copy(held_ref.at[slot], mixed_ref.at[step], sems.at[slot])

    def one_step(i, carry):
        slot = lax.rem(i, 2)

        @pl.when(i >= 2)
        def _():
            save(i - 2, slot).wait()

        for u in range(STEP):
            block = order_ref[i * STEP + u]
            src = src_ref[pl.ds(block, 1), :]
            rel = rel_ref[pl.ds(block, 1), :]
            gathered = jnp.dot(near_ref[...], one_hot(src, rows_dev), preferred_element_type=F32)
            relation = jnp.dot(
                relation_ref[...],
                one_hot(rel, relation_ref.shape[1]),
                preferred_element_type=F32,
            )
            is_far = is_outside(src, rows_dev)
            held_ref[slot, u] = (gathered.astype(BF16) + is_far) * relation.astype(BF16)
        save(i, slot).start()
        return carry

    lax.fori_loop(0, count, one_step, 0)
    for back in (2, 1):

        @pl.when(count >= back)
        def _():
            save(count - back, lax.rem(count - back, 2)).wait()


def owners(head_row, devices, rows_dev):
    limits = lax.broadcasted_iota(jnp.int32, (devices, head_row.shape[1]), 0) * rows_dev
    return jnp.sum((limits <= head_row).astype(F32), axis=0, keepdims=True) - 1.0


def ranks(owner_row):
    queries = owner_row.shape[1]
    across = jnp.broadcast_to(owner_row, (queries, queries))
    earlier = lax.broadcasted_iota(jnp.int32, (queries, queries), 0) < lax.broadcasted_iota(
        jnp.int32, (queries, queries), 1
    )
    same = (jnp.transpose(across) == across) & earlier
    return jnp.sum(same.astype(F32), axis=0, keepdims=True)


def far_kernel(
    half_rel,
    last,
    ahead,
    devices,
    base_ref,
    order_ref,
    src_ref,
    dst_ref,
    rel_ref,
    emb_ref,
    far_ref,
    in_ref,
    out_ref,
    loop_ref,
    loop_rel_ref,
    *rest,
):
    far_t_ref, gathered_ref, agg_ref, held_ref, own_ref, made_ref, sems, own_sems, out_sems = rest[-9:]
    if last:
        near_ref, relation_ref, _, hidden_ref = rest[:4]
    else:
        head_ref, query_rel_ref, relation_ref, rel_weight_ref, mixed_ref = rest[:5]
        hidden_ref, heads_ref, factor_ref, rank_ref, most_ref = rest[5:10]
    blocks = src_ref.shape[0]
    rows_dev = blocks * BLK
    far_chunks = far_ref.shape[0]
    middle = middle_step(order_ref, blocks, ahead)
    start, stop = (middle, blocks // STEP) if last else (0, middle)

    def load(step, slot):
        return pltpu.make_async_copy(mixed_ref.at[step], held_ref.at[slot], sems.at[slot])

    def block_rows(step, u):
        return pl.ds(pl.multiple_of(order_ref[step * STEP + u] * BLK, BLK), BLK)

    def load_own(step, u):
        slot = lax.rem(step, 2)
        return pltpu.make_async_copy(
            emb_ref.at[block_rows(step, u)], own_ref.at[slot, u], own_sems.at[slot, u]
        )

    def give(step, u):
        rows = block_rows(step, u)
        return pltpu.make_async_copy(
            made_ref.at[rows], hidden_ref.at[rows], out_sems.at[step * STEP + u]
        )

    if not last:

        @pl.when(start < stop)
        def _():
            load(start, 0).start()

    def turn(j, carry):
        far_t_ref[j] = jnp.transpose(far_ref[j])
        return carry

    lax.fori_loop(0, far_chunks, turn, 0)
    if not last:
        made_ref[...] = jnp.zeros_like(made_ref)

    def look_up(src, u):
        if far_chunks == 1:
            return jnp.dot(
                far_t_ref[0], one_hot(src - rows_dev, CHUNK), preferred_element_type=F32
            )
        gathered_ref[u] = jnp.zeros(gathered_ref.shape[1:], F32)

        def one_chunk(j, carry):
            gathered_ref[u] += jnp.dot(
                far_t_ref[j],
                one_hot(src - rows_dev - j * CHUNK, CHUNK),
                preferred_element_type=F32,
            )
            return carry

        lax.fori_loop(0, far_chunks, one_chunk, 0)
        return gathered_ref[u]

    def finish(step, slot):
        own = own_ref[slot].reshape(STEP * BLK, own_ref.shape[-1])
        own = (own.astype(F32) * loop_rel_ref[...]).astype(BF16)
        preact = jnp.dot(agg_ref[0, slot], in_ref[...], preferred_element_type=F32)
        preact += jnp.dot(agg_ref[1, slot], out_ref[...], preferred_element_type=F32)
        preact += jnp.dot(own, loop_ref[...], preferred_element_type=F32)
        hidden = jnp.tanh(preact).astype(BF16)
        for u in range(STEP):
            made_ref[block_rows(step, u), :] = hidden[u * BLK : (u + 1) * BLK]

    def one_step(i, carry):
        slot = lax.rem(i, 2)
        step = start + i
        before = jnp.maximum(step - 1, start)

        @pl.when(i > 0)
        def _():
            for u in range(STEP):
                load_own(before, u).wait()

        for u in range(STEP):
            load_own(step, u).start()

        if not last:

            @pl.when(step + 1 < stop)
            def _():
                load(step + 1, 1 - slot).start()

            load(step, slot).wait()
        finish(before, lax.rem(step + 1, 2))
        rows = [pl.ds(order_ref[(start + i) * STEP + u], 1) for u in range(STEP)]
        srcs = [src_ref[row, :] for row in rows]
        found = [look_up(src, u) for u, src in enumerate(srcs)]
        composed = []
        for u, row in enumerate(rows):
            if last:
                near = jnp.dot(
                    near_ref[...], one_hot(srcs[u], rows_dev), preferred_element_type=F32
                )
                relation = jnp.dot(
                    relation_ref[...],
                    one_hot(rel_ref[row, :], relation_ref.shape[1]),
                    preferred_element_type=F32,
                )
                composed.append((found[u] + near).astype(BF16) * relation.astype(BF16))
            else:
                is_near = 1 - is_outside(srcs[u], rows_dev)
                composed.append((found[u].astype(BF16) + is_near) * held_ref[slot, u])
        for u, row in enumerate(rows):
            key = dst_ref[row, :] + jnp.where(rel_ref[row, :] >= half_rel, BLK, 0)
            selector = one_hot(key, 2 * BLK)
            counts = selector[:, :128]
            for lane in range(128, selector.shape[1], 128):
                counts = counts + selector[:, lane : lane + 128]
            counts = jnp.sum(counts.astype(F32), axis=1, keepdims=True)
            sums = lax.dot_general(selector, composed[u], NT, preferred_element_type=F32)
            agg = (sums * (1.0 / jnp.maximum(counts, 1.0))).astype(BF16)
            here = pl.ds(u * BLK, BLK)
            agg_ref[0, lax.rem(step, 2), here, :] = agg[:BLK]
            agg_ref[1, lax.rem(step, 2), here, :] = agg[BLK:]

        @pl.when(i > 0)
        def _():
            for u in range(STEP):
                give(before, u).start()

        return carry

    lax.fori_loop(0, stop - start, one_step, 0)

    @pl.when(start < stop)
    def _():
        for u in range(STEP):
            load_own(stop - 1, u).wait()
        finish(stop - 1, lax.rem(stop - 1, 2))
        for u in range(STEP):
            give(stop - 1, u).start()

    if not last:
        picks = one_hot(query_rel_ref[...], relation_ref.shape[1])
        rows = lax.dot_general(
            picks, relation_ref[...], (((0,), (1,)), ((), ())), preferred_element_type=F32
        )
        factor_ref[...] = jnp.dot(
            rows.astype(BF16), rel_weight_ref[...], preferred_element_type=F32
        )
        picks = one_hot_wide(head_ref[...] - base_ref[0] * BLK, rows_dev)
        rows = lax.dot_general(picks, made_ref[...], TN, preferred_element_type=F32)
        rank = ranks(owners(head_ref[...], devices, rows_dev))
        slots = one_hot(rank.astype(jnp.int32), heads_ref.shape[0])
        heads_ref[...] = jnp.dot(slots, rows.astype(BF16), preferred_element_type=F32).astype(BF16)
        rank_ref[...] = rank.astype(jnp.int32)
        most_ref[0] = jnp.max(rank).astype(jnp.int32)

    def gave(step, carry):
        for u in range(STEP):
            give(step, u).wait()
        return carry

    lax.fori_loop(start, stop, gave, 0)


def pick_kernel(base_ref, index_ref, emb_ref, offered_ref):
    picks = one_hot(index_ref[...] - base_ref[0], emb_ref.shape[0])
    offered_ref[...] = lax.dot_general(
        picks, emb_ref[...], TN, preferred_element_type=F32
    ).astype(BF16)


SMEM = pl.BlockSpec(memory_space=pltpu.SMEM)
WHOLE = pl.BlockSpec(memory_space=pltpu.VMEM)
HBM = pl.BlockSpec(memory_space=pltpu.HBM)


def near_call(ahead, base, query_head, src, rel, near, relation):
    columns, edges = near.shape[0], src.shape[1]
    blocks = src.shape[0]
    count = STEP * ahead
    flops = 2 * count * edges * columns * (near.shape[1] + relation.shape[1])
    return pl.pallas_call(
        functools.partial(near_kernel, ahead),
        out_shape=(
            jax.ShapeDtypeStruct((blocks // STEP, STEP, columns, edges), BF16),
            jax.ShapeDtypeStruct((blocks + 2,), jnp.int32),
        ),
        in_specs=[SMEM] * 2 + [WHOLE] * 4,
        out_specs=(HBM, SMEM),
        scratch_shapes=[
            pltpu.VMEM((2, STEP, columns, edges), BF16),
            pltpu.SemaphoreType.DMA((2,)),
        ],
        compiler_params=pltpu.CompilerParams(vmem_limit_bytes=VMEM_LIMIT),
        cost_estimate=pl.CostEstimate(
            flops=flops, bytes_accessed=2 * count * edges * columns, transcendentals=0
        ),
    )(base, query_head, src, rel, near, relation)


def far_call(half_rel, last, ahead, devices, scalars, edges, emb, far, weights, more, kept, outs):
    rows_dev, columns = emb.shape
    blocks, width = edges[0].shape
    return pl.pallas_call(
        functools.partial(far_kernel, half_rel, last, ahead, devices),
        out_shape=(jax.ShapeDtypeStruct((rows_dev, columns), BF16),) + outs,
        in_specs=[SMEM] * 2 + [WHOLE] * 3 + [HBM] + [WHOLE] * (5 + len(more)) + [HBM],
        out_specs=(HBM,) if last else (HBM, WHOLE, WHOLE, WHOLE, SMEM),
        input_output_aliases={11 + len(more): 0} if last else {},
        scratch_shapes=[
            pltpu.VMEM((far.shape[0], columns, CHUNK), BF16),
            pltpu.VMEM((STEP, columns, width if far.shape[0] > 1 else 128), F32),
            pltpu.VMEM((2, 2, STEP * BLK, columns), BF16),
            pltpu.VMEM((2, STEP, columns, 128 if last else width), BF16),
            pltpu.VMEM((2, STEP, BLK, columns), BF16),
            pltpu.VMEM((rows_dev, columns), BF16),
            pltpu.SemaphoreType.DMA((2,)),
            pltpu.SemaphoreType.DMA((2, STEP)),
            pltpu.SemaphoreType.DMA((blocks,)),
        ],
        compiler_params=pltpu.CompilerParams(vmem_limit_bytes=VMEM_LIMIT),
        cost_estimate=pl.CostEstimate(
            flops=blocks * width * columns * far.shape[0] * CHUNK,
            bytes_accessed=blocks * width * columns,
            transcendentals=0,
        ),
    )(*scalars, *edges, emb, far, *weights, *more, kept)


def score_kernel(
    devices,
    sent_ref,
    more_ref,
    rank_ref,
    head_ref,
    factor_hbm,
    hidden_hbm,
    scores_ref,
    payload_ref,
    factor_ref,
    hidden_ref,
    sems,
):
    copies = (
        pltpu.make_async_copy(factor_hbm, factor_ref, sems.at[0]),
        pltpu.make_async_copy(hidden_hbm, hidden_ref, sems.at[1]),
    )
    for copy in copies:
        copy.start()
    slots = sent_ref.shape[0] // devices
    owner = owners(head_ref[...], devices, hidden_ref.shape[0]).astype(jnp.int32)
    place = jnp.where(rank_ref[...] < slots, owner * slots + rank_ref[...], -1)
    picks = one_hot(place, sent_ref.shape[0])
    heads = lax.dot_general(picks, sent_ref[...], TN, preferred_element_type=F32)
    heads = heads + more_ref[...].astype(F32)
    for copy in copies:
        copy.wait()
    query = (heads * factor_ref[...]).astype(BF16)
    scores = lax.dot_general(query, hidden_ref[...], NT, preferred_element_type=F32)
    scores_ref[...] = scores
    top = jnp.max(scores, axis=1, keepdims=True)
    high = top.astype(BF16).astype(F32)
    low = (top - high).astype(BF16).astype(F32)
    top = high + low
    weights = jnp.exp(scores - top)
    total = jnp.sum(weights, axis=1, keepdims=True)
    weighted = jnp.dot(weights.astype(BF16), hidden_ref[...], preferred_element_type=F32)
    total_high = total.astype(BF16).astype(F32)
    lanes = lax.broadcasted_iota(jnp.int32, (query.shape[0], LANES), 1) % 4
    wide = jnp.where(lanes == 0, high, total - total_high)
    wide = jnp.where(lanes == 1, low, wide)
    wide = jnp.where(lanes == 2, total_high, wide)
    stats = jnp.transpose(wide)
    upper = lax.broadcasted_iota(jnp.int32, (8, LANES), 0) < 4
    figures = jnp.where(upper, stats[:8, :LANES], stats[:8, LANES:])
    share = query.shape[0] // payload_ref.shape[0]
    for peer in range(payload_ref.shape[0]):
        rows = weighted[peer * share : (peer + 1) * share]
        payload_ref[peer] = pack(rows[:, :LANES], rows[:, LANES:], figures)


def pack(left, right, figures):
    return jnp.concatenate([left, right, figures, figures], axis=0).astype(BF16)


def merge(data, first):
    share = (data.shape[1] - 16) // 2
    figures = data[:, 2 * share : 2 * share + 8]
    tops, totals, scales = [], [], []
    for half in (0, 4):
        each = figures[:, half : half + 1] + figures[:, half + 1 : half + 2]
        top = jnp.max(each, axis=0)
        scale = jnp.exp(each - top[None])
        total = figures[:, half + 2 : half + 3] + figures[:, half + 3 : half + 4]
        tops.append(top)
        totals.append(jnp.sum(total * scale, axis=0))
        scales.append(scale)
    left = right = 0.0
    for i in range(data.shape[0]):
        scale = jnp.where(first >= LANES, scales[1][i], scales[0][i])
        factor = column(scale, lax.rem(first, LANES), share)
        left += factor * data[i, :share]
        right += factor * data[i, share : 2 * share]
    return left, right, tops, totals


def column(row, first, rows):
    lanes = lax.broadcasted_iota(jnp.int32, (rows, LANES), 1)
    wanted = lax.broadcasted_iota(jnp.int32, (rows, LANES), 0) + first
    return jnp.sum(jnp.where(lanes == wanted, row, 0.0), axis=1, keepdims=True)


def merge_kernel(first_ref, received_ref, payload_ref):
    left, right, tops, totals = merge(received_ref[...].astype(F32), first_ref[0])
    row = lax.broadcasted_iota(jnp.int32, (8, LANES), 0)
    figures = jnp.zeros((8, LANES), F32)
    for half in range(2):
        for at, value in ((0, tops[half]), (2, totals[half])):
            high = value.astype(BF16).astype(F32)
            figures = jnp.where(row == 4 * half + at, high, figures)
            figures = jnp.where(row == 4 * half + at + 1, value - high, figures)
    block = pack(left, right, figures)
    for peer in range(payload_ref.shape[0]):
        payload_ref[peer] = block


def last_kernel(first_ref, received_ref, scores_ref, log_probs_ref, expected_ref):
    first = first_ref[0]
    left, right, tops, totals = merge(received_ref[...].astype(F32), first)
    for half in range(2):
        norm = column(tops[half] + jnp.log(totals[half]), 0, LANES)
        rows = pl.ds(half * LANES, LANES)
        log_probs_ref[rows, :] = scores_ref[rows, :] - norm
    total = jnp.where(first >= LANES, totals[1], totals[0])
    total = column(total, lax.rem(first, LANES), left.shape[0])
    expected_ref[:, :LANES] = left / total
    expected_ref[:, LANES:] = right / total


def body(
    entity_emb,
    relation_emb,
    in_weight,
    out_weight,
    loop_weight,
    rel_weight,
    loop_rel,
    edge_src,
    edge_dst,
    edge_rel,
    export_rows,
    query_head,
    query_rel,
):
    groups = lax.axis_size("ent")
    copies = lax.axis_size("rep")
    devices = groups * copies
    group = lax.axis_index("ent")
    member = lax.axis_index("rep")
    device = group * copies + member
    rows_dev, columns = entity_emb.shape
    queries = query_head.shape[0]

    blocks = edge_src.shape[0]
    relations = relation_emb.shape[0]
    ahead = min(AHEAD, blocks // STEP)

    slots = export_rows.shape[1]
    offered = pl.pallas_call(
        pick_kernel,
        out_shape=jax.ShapeDtypeStruct((slots, columns), BF16),
        in_specs=[SMEM, WHOLE, WHOLE],
        out_specs=WHOLE,
        compiler_params=pltpu.CompilerParams(vmem_limit_bytes=VMEM_LIMIT),
    )((member * rows_dev)[None], export_rows, entity_emb)
    offered, later_relation = lax.optimization_barrier((offered, relation_emb))
    rel_count = -(-relations // 256) * 256
    relation_t = jnp.pad(later_relation, ((0, rel_count - relations), (0, 0))).T
    near_t = entity_emb.T
    pieces = lax.all_to_all(offered, "rep", 0, 0, tiled=True)
    mine = jnp.sum(
        pieces.reshape(copies, slots // copies, columns).astype(F32), axis=0
    ).astype(BF16)
    mine, near_t = lax.optimization_barrier((mine, near_t))
    spread = jnp.broadcast_to(mine[None], (devices,) + mine.shape)
    table = lax.all_to_all(spread, BOTH, 0, 0).reshape(groups * slots, columns)
    base = (device * blocks)[None]
    mixed, order = near_call(
        ahead, base, query_head, edge_src, edge_rel, near_t, relation_t
    )
    far_count = -(-(groups * slots) // CHUNK) * CHUNK
    far = jnp.pad(table, ((0, far_count - groups * slots), (0, 0)))
    far = far.reshape(far_count // CHUNK, CHUNK, columns)

    head_row = query_head[None]
    weights = (in_weight, out_weight, loop_weight, loop_rel[None])
    edges = (edge_src, edge_dst, edge_rel)
    cap = min(queries, -(-3 * queries // (8 * devices)) * 8)
    hidden, heads, query_factor, rank, most = far_call(
        relations // 2,
        False,
        ahead,
        devices,
        (base, order),
        edges,
        entity_emb,
        far,
        weights,
        (head_row, query_rel[None], relation_t, rel_weight),
        mixed,
        (
            jax.ShapeDtypeStruct((-(-queries // cap) * cap, columns), BF16),
            jax.ShapeDtypeStruct((queries, columns), F32),
            jax.ShapeDtypeStruct((1, queries), jnp.int32),
            jax.ShapeDtypeStruct((1,), jnp.int32),
        ),
    )

    def send_round(turn):
        some = lax.dynamic_slice_in_dim(heads, turn * cap, cap, 0)
        spread = jnp.broadcast_to(some[None], (devices,) + some.shape)
        return lax.all_to_all(spread, BOTH, 0, 0).reshape(devices * cap, columns)

    def another_round(state):
        turn, more = state
        slot = rank[0] - turn * cap
        place = query_head // rows_dev * cap + slot
        rows = jnp.take(send_round(turn), jnp.clip(place, 0, devices * cap - 1), axis=0)
        inside = (slot >= 0) & (slot < cap)
        return turn + 1, jnp.where(inside[:, None], rows, more)

    sent = send_round(0)
    (hidden,) = far_call(
        relations // 2,
        True,
        ahead,
        devices,
        (base, order),
        edges,
        entity_emb,
        far,
        weights,
        (near_t, relation_t),
        hidden,
        (),
    )
    _, more_heads = lax.while_loop(
        lambda state: state[0] * cap <= most[0],
        another_round,
        (jnp.int32(1), jnp.zeros((queries, columns), BF16)),
    )

    batch_rows = queries // copies
    first = (member * batch_rows)[None]
    part = (2 * batch_rows + 16, LANES)
    few = pltpu.CompilerParams(vmem_limit_bytes=SCORE_LIMIT)
    scores, payload = pl.pallas_call(
        functools.partial(score_kernel, devices),
        out_shape=(
            jax.ShapeDtypeStruct((queries, rows_dev), F32),
            jax.ShapeDtypeStruct((copies,) + part, BF16),
        ),
        in_specs=[WHOLE] * 4 + [HBM] * 2,
        out_specs=(WHOLE, WHOLE),
        scratch_shapes=[
            pltpu.VMEM((queries, columns), F32),
            pltpu.VMEM((rows_dev, columns), BF16),
            pltpu.SemaphoreType.DMA((2,)),
        ],
        compiler_params=few,
    )(sent, more_heads, rank, head_row, query_factor, hidden)
    payload = pl.pallas_call(
        merge_kernel,
        out_shape=jax.ShapeDtypeStruct((groups,) + part, BF16),
        in_specs=[SMEM, WHOLE],
        out_specs=WHOLE,
        compiler_params=few,
    )(first, lax.all_to_all(payload, "rep", 0, 0))
    log_probs, expected_tail = pl.pallas_call(
        last_kernel,
        out_shape=(
            jax.ShapeDtypeStruct((queries, rows_dev), F32),
            jax.ShapeDtypeStruct((batch_rows, columns), F32),
        ),
        in_specs=[SMEM, WHOLE, WHOLE],
        out_specs=(WHOLE, WHOLE),
        compiler_params=few,
    )(first, lax.all_to_all(payload, "ent", 0, 0), scores)
    return (log_probs, expected_tail)


def solution(mesh):
    placed = (
        P(("ent", "rep"), None),
        P(),
        P(),
        P(),
        P(),
        P(),
        P(),
        P(("ent", "rep"), None),
        P(("ent", "rep"), None),
        P(("ent", "rep"), None),
        P("ent", None),
        P(),
        P(),
    )
    return jax.shard_map(
        body,
        mesh=mesh,
        in_specs=placed,
        out_specs=(P(None, ("ent", "rep")), P("rep", None)),
        check_vma=False,
    )
```

```python
import functools

import jax
import jax.numpy as jnp
from jax import lax
from jax.experimental import pallas as pl
from jax.experimental.pallas import tpu as pltpu
from jax.sharding import PartitionSpec as P

BLK = 128
CHUNK = 1024
LANES = 128
BF16 = jnp.bfloat16
F32 = jnp.float32
BOTH = ("ent", "rep")
NT = (((1,), (1,)), ((), ()))
TN = (((0,), (0,)), ((), ()))
VMEM_LIMIT = 56 * 2**20
STEP = 2
AHEAD = 6
SCORE_LIMIT = 24 * 2**20


def one_hot(index, rows):
    where = lax.broadcasted_iota(jnp.int16, (rows, index.shape[1]), 0) == index.astype(jnp.int16)
    return jnp.where(where, jnp.asarray(1, BF16), jnp.asarray(0, BF16))


def one_hot_wide(index, rows):
    where = lax.broadcasted_iota(jnp.int32, (rows, index.shape[1]), 0) == index
    return where.astype(F32).astype(BF16)


def is_outside(src, rows_dev):
    return jnp.where(src < rows_dev, 0.0, 1.0).astype(BF16)


def order_blocks(head_ref, first_block, blocks, order_ref):
    def mark(q, marks):
        block = lax.shift_right_arithmetic(head_ref[q], BLK.bit_length() - 1) - first_block
        inside = (block >= 0) & (block < blocks)
        return marks | jnp.where(inside, lax.shift_left(1, jnp.where(inside, block, 0)), 0)

    marks = lax.fori_loop(0, head_ref.shape[0], mark, jnp.int32(0), unroll=16)
    position = jnp.int32(0)
    for wanted in (1, 0):
        for b in range(blocks):
            taken = (lax.shift_right_logical(marks, b) & 1) == wanted
            order_ref[jnp.where(taken, position, blocks + 1)] = jnp.int32(b)
            position = position + taken.astype(jnp.int32)
        if wanted:
            found = position
    order_ref[blocks] = found


def middle_step(order_ref, blocks, ahead):
    return jnp.maximum((order_ref[blocks] + STEP - 1) // STEP, ahead)


def near_kernel(
    ahead,
    base_ref,
    head_ref,
    src_ref,
    rel_ref,
    near_ref,
    relation_ref,
    mixed_ref,
    order_ref,
    held_ref,
    sems,
):
    blocks = src_ref.shape[0]
    rows_dev = near_ref.shape[1]
    order_blocks(head_ref, base_ref[0], blocks, order_ref)
    count = middle_step(order_ref, blocks, ahead)

    def save(step, slot):
        return pltpu.make_async_copy(held_ref.at[slot], mixed_ref.at[step], sems.at[slot])

    def one_step(i, carry):
        slot = lax.rem(i, 2)

        @pl.when(i >= 2)
        def _():
            save(i - 2, slot).wait()

        for u in range(STEP):
            block = order_ref[i * STEP + u]
            src = src_ref[pl.ds(block, 1), :]
            rel = rel_ref[pl.ds(block, 1), :]
            gathered = jnp.dot(near_ref[...], one_hot(src, rows_dev), preferred_element_type=F32)
            relation = jnp.dot(
                relation_ref[...],
                one_hot(rel, relation_ref.shape[1]),
                preferred_element_type=F32,
            )
            is_far = is_outside(src, rows_dev)
            held_ref[slot, u] = (gathered.astype(BF16) + is_far) * relation.astype(BF16)
        save(i, slot).start()
        return carry

    lax.fori_loop(0, count, one_step, 0)
    for back in (2, 1):

        @pl.when(count >= back)
        def _():
            save(count - back, lax.rem(count - back, 2)).wait()


def owners(head_row, devices, rows_dev):
    limits = lax.broadcasted_iota(jnp.int32, (devices, head_row.shape[1]), 0) * rows_dev
    return jnp.sum((limits <= head_row).astype(F32), axis=0, keepdims=True) - 1.0


def ranks(owner_row):
    queries = owner_row.shape[1]
    across = jnp.broadcast_to(owner_row, (queries, queries))
    earlier = lax.broadcasted_iota(jnp.int32, (queries, queries), 0) < lax.broadcasted_iota(
        jnp.int32, (queries, queries), 1
    )
    same = (jnp.transpose(across) == across) & earlier
    return jnp.sum(same.astype(F32), axis=0, keepdims=True)


def far_kernel(
    half_rel,
    last,
    ahead,
    devices,
    base_ref,
    order_ref,
    src_ref,
    dst_ref,
    rel_ref,
    emb_ref,
    far_ref,
    in_ref,
    out_ref,
    loop_ref,
    loop_rel_ref,
    *rest,
):
    far_t_ref, gathered_ref, agg_ref, held_ref, own_ref, made_ref, sems, own_sems, out_sems = rest[-9:]
    if last:
        near_ref, relation_ref, _, hidden_ref = rest[:4]
    else:
        head_ref, query_rel_ref, relation_ref, rel_weight_ref, mixed_ref = rest[:5]
        hidden_ref, heads_ref, factor_ref, rank_ref, most_ref = rest[5:10]
    blocks = src_ref.shape[0]
    rows_dev = blocks * BLK
    far_chunks = far_ref.shape[0]
    middle = middle_step(order_ref, blocks, ahead)
    start, stop = (middle, blocks // STEP) if last else (0, middle)

    def load(step, slot):
        return pltpu.make_async_copy(mixed_ref.at[step], held_ref.at[slot], sems.at[slot])

    def block_rows(step, u):
        return pl.ds(pl.multiple_of(order_ref[step * STEP + u] * BLK, BLK), BLK)

    def load_own(step, u):
        slot = lax.rem(step, 2)
        return pltpu.make_async_copy(
            emb_ref.at[block_rows(step, u)], own_ref.at[slot, u], own_sems.at[slot, u]
        )

    def give(step, u):
        rows = block_rows(step, u)
        return pltpu.make_async_copy(
            made_ref.at[rows], hidden_ref.at[rows], out_sems.at[step * STEP + u]
        )

    if not last:

        @pl.when(start < stop)
        def _():
            load(start, 0).start()

    def turn(j, carry):
        far_t_ref[j] = jnp.transpose(far_ref[j])
        return carry

    lax.fori_loop(0, far_chunks, turn, 0)
    if not last:
        made_ref[...] = jnp.zeros_like(made_ref)

    def look_up(src, u):
        if far_chunks == 1:
            return jnp.dot(
                far_t_ref[0], one_hot(src - rows_dev, CHUNK), preferred_element_type=F32
            )
        gathered_ref[u] = jnp.zeros(gathered_ref.shape[1:], F32)

        def one_chunk(j, carry):
            gathered_ref[u] += jnp.dot(
                far_t_ref[j],
                one_hot(src - rows_dev - j * CHUNK, CHUNK),
                preferred_element_type=F32,
            )
            return carry

        lax.fori_loop(0, far_chunks, one_chunk, 0)
        return gathered_ref[u]

    def finish(step, slot):
        own = own_ref[slot].reshape(STEP * BLK, own_ref.shape[-1])
        own = (own.astype(F32) * loop_rel_ref[...]).astype(BF16)
        preact = jnp.dot(agg_ref[0, slot], in_ref[...], preferred_element_type=F32)
        preact += jnp.dot(agg_ref[1, slot], out_ref[...], preferred_element_type=F32)
        preact += jnp.dot(own, loop_ref[...], preferred_element_type=F32)
        hidden = jnp.tanh(preact).astype(BF16)
        for u in range(STEP):
            made_ref[block_rows(step, u), :] = hidden[u * BLK : (u + 1) * BLK]

    def one_step(i, carry):
        slot = lax.rem(i, 2)
        step = start + i
        before = jnp.maximum(step - 1, start)

        @pl.when(i > 0)
        def _():
            for u in range(STEP):
                load_own(before, u).wait()

        for u in range(STEP):
            load_own(step, u).start()

        if not last:

            @pl.when(step + 1 < stop)
            def _():
                load(step + 1, 1 - slot).start()

            load(step, slot).wait()
        finish(before, lax.rem(step + 1, 2))
        rows = [pl.ds(order_ref[(start + i) * STEP + u], 1) for u in range(STEP)]
        srcs = [src_ref[row, :] for row in rows]
        found = [look_up(src, u) for u, src in enumerate(srcs)]
        composed = []
        for u, row in enumerate(rows):
            if last:
                near = jnp.dot(
                    near_ref[...], one_hot(srcs[u], rows_dev), preferred_element_type=F32
                )
                relation = jnp.dot(
                    relation_ref[...],
                    one_hot(rel_ref[row, :], relation_ref.shape[1]),
                    preferred_element_type=F32,
                )
                composed.append((found[u] + near).astype(BF16) * relation.astype(BF16))
            else:
                is_near = 1 - is_outside(srcs[u], rows_dev)
                composed.append((found[u].astype(BF16) + is_near) * held_ref[slot, u])
        for u, row in enumerate(rows):
            key = dst_ref[row, :] + jnp.where(rel_ref[row, :] >= half_rel, BLK, 0)
            selector = one_hot(key, 2 * BLK)
            counts = selector[:, :128]
            for lane in range(128, selector.shape[1], 128):
                counts = counts + selector[:, lane : lane + 128]
            counts = jnp.sum(counts.astype(F32), axis=1, keepdims=True)
            sums = lax.dot_general(selector, composed[u], NT, preferred_element_type=F32)
            agg = (sums * (1.0 / jnp.maximum(counts, 1.0))).astype(BF16)
            here = pl.ds(u * BLK, BLK)
            agg_ref[0, lax.rem(step, 2), here, :] = agg[:BLK]
            agg_ref[1, lax.rem(step, 2), here, :] = agg[BLK:]

        @pl.when(i > 0)
        def _():
            for u in range(STEP):
                give(before, u).start()

        return carry

    lax.fori_loop(0, stop - start, one_step, 0)

    @pl.when(start < stop)
    def _():
        for u in range(STEP):
            load_own(stop - 1, u).wait()
        finish(stop - 1, lax.rem(stop - 1, 2))
        for u in range(STEP):
            give(stop - 1, u).start()

    if not last:
        picks = one_hot(query_rel_ref[...], relation_ref.shape[1])
        rows = lax.dot_general(
            picks, relation_ref[...], (((0,), (1,)), ((), ())), preferred_element_type=F32
        )
        factor_ref[...] = jnp.dot(
            rows.astype(BF16), rel_weight_ref[...], preferred_element_type=F32
        )
        picks = one_hot_wide(head_ref[...] - base_ref[0] * BLK, rows_dev)
        rows = lax.dot_general(picks, made_ref[...], TN, preferred_element_type=F32)
        rank = ranks(owners(head_ref[...], devices, rows_dev))
        slots = one_hot(rank.astype(jnp.int32), heads_ref.shape[0])
        heads_ref[...] = jnp.dot(slots, rows.astype(BF16), preferred_element_type=F32).astype(BF16)
        rank_ref[...] = rank.astype(jnp.int32)
        most_ref[0] = jnp.max(rank).astype(jnp.int32)

    def gave(step, carry):
        for u in range(STEP):
            give(step, u).wait()
        return carry

    lax.fori_loop(start, stop, gave, 0)


def pick_kernel(base_ref, index_ref, emb_ref, offered_ref):
    picks = one_hot(index_ref[...] - base_ref[0], emb_ref.shape[0])
    offered_ref[...] = lax.dot_general(
        picks, emb_ref[...], TN, preferred_element_type=F32
    ).astype(BF16)


SMEM = pl.BlockSpec(memory_space=pltpu.SMEM)
WHOLE = pl.BlockSpec(memory_space=pltpu.VMEM)
HBM = pl.BlockSpec(memory_space=pltpu.HBM)


def near_call(ahead, base, query_head, src, rel, near, relation):
    columns, edges = near.shape[0], src.shape[1]
    blocks = src.shape[0]
    count = STEP * ahead
    flops = 2 * count * edges * columns * (near.shape[1] + relation.shape[1])
    return pl.pallas_call(
        functools.partial(near_kernel, ahead),
        out_shape=(
            jax.ShapeDtypeStruct((blocks // STEP, STEP, columns, edges), BF16),
            jax.ShapeDtypeStruct((blocks + 2,), jnp.int32),
        ),
        in_specs=[SMEM] * 2 + [WHOLE] * 4,
        out_specs=(HBM, SMEM),
        scratch_shapes=[
            pltpu.VMEM((2, STEP, columns, edges), BF16),
            pltpu.SemaphoreType.DMA((2,)),
        ],
        compiler_params=pltpu.CompilerParams(vmem_limit_bytes=VMEM_LIMIT),
        cost_estimate=pl.CostEstimate(
            flops=flops, bytes_accessed=2 * count * edges * columns, transcendentals=0
        ),
    )(base, query_head, src, rel, near, relation)


def far_call(half_rel, last, ahead, devices, scalars, edges, emb, far, weights, more, kept, outs):
    rows_dev, columns = emb.shape
    blocks, width = edges[0].shape
    return pl.pallas_call(
        functools.partial(far_kernel, half_rel, last, ahead, devices),
        out_shape=(jax.ShapeDtypeStruct((rows_dev, columns), BF16),) + outs,
        in_specs=[SMEM] * 2 + [WHOLE] * 3 + [HBM] + [WHOLE] * (5 + len(more)) + [HBM],
        out_specs=(HBM,) if last else (HBM, WHOLE, WHOLE, WHOLE, SMEM),
        input_output_aliases={11 + len(more): 0} if last else {},
        scratch_shapes=[
            pltpu.VMEM((far.shape[0], columns, CHUNK), BF16),
            pltpu.VMEM((STEP, columns, width if far.shape[0] > 1 else 128), F32),
            pltpu.VMEM((2, 2, STEP * BLK, columns), BF16),
            pltpu.VMEM((2, STEP, columns, 128 if last else width), BF16),
            pltpu.VMEM((2, STEP, BLK, columns), BF16),
            pltpu.VMEM((rows_dev, columns), BF16),
            pltpu.SemaphoreType.DMA((2,)),
            pltpu.SemaphoreType.DMA((2, STEP)),
            pltpu.SemaphoreType.DMA((blocks,)),
        ],
        compiler_params=pltpu.CompilerParams(vmem_limit_bytes=VMEM_LIMIT),
        cost_estimate=pl.CostEstimate(
            flops=blocks * width * columns * far.shape[0] * CHUNK,
            bytes_accessed=blocks * width * columns,
            transcendentals=0,
        ),
    )(*scalars, *edges, emb, far, *weights, *more, kept)


def score_kernel(
    devices,
    sent_ref,
    more_ref,
    rank_ref,
    head_ref,
    factor_hbm,
    hidden_hbm,
    scores_ref,
    payload_ref,
    factor_ref,
    hidden_ref,
    sems,
):
    copies = (
        pltpu.make_async_copy(factor_hbm, factor_ref, sems.at[0]),
        pltpu.make_async_copy(hidden_hbm, hidden_ref, sems.at[1]),
    )
    for copy in copies:
        copy.start()
    slots = sent_ref.shape[0] // devices
    owner = owners(head_ref[...], devices, hidden_ref.shape[0]).astype(jnp.int32)
    place = jnp.where(rank_ref[...] < slots, owner * slots + rank_ref[...], -1)
    picks = one_hot(place, sent_ref.shape[0])
    heads = lax.dot_general(picks, sent_ref[...], TN, preferred_element_type=F32)
    heads = heads + more_ref[...].astype(F32)
    for copy in copies:
        copy.wait()
    query = (heads * factor_ref[...]).astype(BF16)
    scores = lax.dot_general(query, hidden_ref[...], NT, preferred_element_type=F32)
    scores_ref[...] = scores
    top = jnp.max(scores, axis=1, keepdims=True)
    high = top.astype(BF16).astype(F32)
    low = (top - high).astype(BF16).astype(F32)
    top = high + low
    weights = jnp.exp(scores - top)
    total = jnp.sum(weights, axis=1, keepdims=True)
    weighted = jnp.dot(weights.astype(BF16), hidden_ref[...], preferred_element_type=F32)
    total_high = total.astype(BF16).astype(F32)
    lanes = lax.broadcasted_iota(jnp.int32, (query.shape[0], LANES), 1) % 4
    wide = jnp.where(lanes == 0, high, total - total_high)
    wide = jnp.where(lanes == 1, low, wide)
    wide = jnp.where(lanes == 2, total_high, wide)
    stats = jnp.transpose(wide)
    upper = lax.broadcasted_iota(jnp.int32, (8, LANES), 0) < 4
    figures = jnp.where(upper, stats[:8, :LANES], stats[:8, LANES:])
    share = query.shape[0] // payload_ref.shape[0]
    for peer in range(payload_ref.shape[0]):
        rows = weighted[peer * share : (peer + 1) * share]
        payload_ref[peer] = pack(rows[:, :LANES], rows[:, LANES:], figures)


def pack(left, right, figures):
    return jnp.concatenate([left, right, figures, figures], axis=0).astype(BF16)


def merge(data, first):
    share = (data.shape[1] - 16) // 2
    figures = data[:, 2 * share : 2 * share + 8]
    tops, totals, scales = [], [], []
    for half in (0, 4):
        each = figures[:, half : half + 1] + figures[:, half + 1 : half + 2]
        top = jnp.max(each, axis=0)
        scale = jnp.exp(each - top[None])
        total = figures[:, half + 2 : half + 3] + figures[:, half + 3 : half + 4]
        tops.append(top)
        totals.append(jnp.sum(total * scale, axis=0))
        scales.append(scale)
    left = right = 0.0
    for i in range(data.shape[0]):
        scale = jnp.where(first >= LANES, scales[1][i], scales[0][i])
        factor = column(scale, lax.rem(first, LANES), share)
        left += factor * data[i, :share]
        right += factor * data[i, share : 2 * share]
    return left, right, tops, totals


def column(row, first, rows):
    lanes = lax.broadcasted_iota(jnp.int32, (rows, LANES), 1)
    wanted = lax.broadcasted_iota(jnp.int32, (rows, LANES), 0) + first
    return jnp.sum(jnp.where(lanes == wanted, row, 0.0), axis=1, keepdims=True)


def merge_kernel(first_ref, received_ref, payload_ref):
    left, right, tops, totals = merge(received_ref[...].astype(F32), first_ref[0])
    row = lax.broadcasted_iota(jnp.int32, (8, LANES), 0)
    figures = jnp.zeros((8, LANES), F32)
    for half in range(2):
        for at, value in ((0, tops[half]), (2, totals[half])):
            high = value.astype(BF16).astype(F32)
            figures = jnp.where(row == 4 * half + at, high, figures)
            figures = jnp.where(row == 4 * half + at + 1, value - high, figures)
    block = pack(left, right, figures)
    for peer in range(payload_ref.shape[0]):
        payload_ref[peer] = block


def last_kernel(
    first_ref, received_ref, scores_ref, log_probs_ref, expected_ref, made_ref, sems
):
    first = first_ref[0]
    left, right, tops, totals = merge(received_ref[...].astype(F32), first)
    copies = []
    for half in range(2):
        norm = column(tops[half] + jnp.log(totals[half]), 0, LANES)
        rows = pl.ds(half * LANES, LANES)
        made_ref[rows, :] = scores_ref[rows, :] - norm
        copies.append(
            pltpu.make_async_copy(made_ref.at[rows], log_probs_ref.at[rows], sems.at[half])
        )
        copies[half].start()
    total = jnp.where(first >= LANES, totals[1], totals[0])
    total = column(total, lax.rem(first, LANES), left.shape[0])
    expected_ref[:, :LANES] = left / total
    expected_ref[:, LANES:] = right / total
    for copy in copies:
        copy.wait()


def body(
    entity_emb,
    relation_emb,
    in_weight,
    out_weight,
    loop_weight,
    rel_weight,
    loop_rel,
    edge_src,
    edge_dst,
    edge_rel,
    export_rows,
    query_head,
    query_rel,
):
    groups = lax.axis_size("ent")
    copies = lax.axis_size("rep")
    devices = groups * copies
    group = lax.axis_index("ent")
    member = lax.axis_index("rep")
    device = group * copies + member
    rows_dev, columns = entity_emb.shape
    queries = query_head.shape[0]

    blocks = edge_src.shape[0]
    relations = relation_emb.shape[0]
    ahead = min(AHEAD, blocks // STEP)

    slots = export_rows.shape[1]
    offered = pl.pallas_call(
        pick_kernel,
        out_shape=jax.ShapeDtypeStruct((slots, columns), BF16),
        in_specs=[SMEM, WHOLE, WHOLE],
        out_specs=WHOLE,
        compiler_params=pltpu.CompilerParams(vmem_limit_bytes=VMEM_LIMIT),
    )((member * rows_dev)[None], export_rows, entity_emb)
    offered, later_relation = lax.optimization_barrier((offered, relation_emb))
    rel_count = -(-relations // 256) * 256
    relation_t = jnp.pad(later_relation, ((0, rel_count - relations), (0, 0))).T
    near_t = entity_emb.T
    pieces = lax.all_to_all(offered, "rep", 0, 0, tiled=True)
    mine = jnp.sum(
        pieces.reshape(copies, slots // copies, columns).astype(F32), axis=0
    ).astype(BF16)
    mine, near_t = lax.optimization_barrier((mine, near_t))
    spread = jnp.broadcast_to(mine[None], (devices,) + mine.shape)
    table = lax.all_to_all(spread, BOTH, 0, 0).reshape(groups * slots, columns)
    base = (device * blocks)[None]
    mixed, order = near_call(
        ahead, base, query_head, edge_src, edge_rel, near_t, relation_t
    )
    far_count = -(-(groups * slots) // CHUNK) * CHUNK
    far = jnp.pad(table, ((0, far_count - groups * slots), (0, 0)))
    far = far.reshape(far_count // CHUNK, CHUNK, columns)

    head_row = query_head[None]
    weights = (in_weight, out_weight, loop_weight, loop_rel[None])
    edges = (edge_src, edge_dst, edge_rel)
    cap = min(queries, -(-3 * queries // (8 * devices)) * 8)
    hidden, heads, query_factor, rank, most = far_call(
        relations // 2,
        False,
        ahead,
        devices,
        (base, order),
        edges,
        entity_emb,
        far,
        weights,
        (head_row, query_rel[None], relation_t, rel_weight),
        mixed,
        (
            jax.ShapeDtypeStruct((-(-queries // cap) * cap, columns), BF16),
            jax.ShapeDtypeStruct((queries, columns), F32),
            jax.ShapeDtypeStruct((1, queries), jnp.int32),
            jax.ShapeDtypeStruct((1,), jnp.int32),
        ),
    )

    def send_round(turn):
        some = lax.dynamic_slice_in_dim(heads, turn * cap, cap, 0)
        spread = jnp.broadcast_to(some[None], (devices,) + some.shape)
        return lax.all_to_all(spread, BOTH, 0, 0).reshape(devices * cap, columns)

    def another_round(state):
        turn, more = state
        slot = rank[0] - turn * cap
        place = query_head // rows_dev * cap + slot
        rows = jnp.take(send_round(turn), jnp.clip(place, 0, devices * cap - 1), axis=0)
        inside = (slot >= 0) & (slot < cap)
        return turn + 1, jnp.where(inside[:, None], rows, more)

    sent = send_round(0)
    (hidden,) = far_call(
        relations // 2,
        True,
        ahead,
        devices,
        (base, order),
        edges,
        entity_emb,
        far,
        weights,
        (near_t, relation_t),
        hidden,
        (),
    )
    _, more_heads = lax.while_loop(
        lambda state: state[0] * cap <= most[0],
        another_round,
        (jnp.int32(1), jnp.zeros((queries, columns), BF16)),
    )

    batch_rows = queries // copies
    first = (member * batch_rows)[None]
    part = (2 * batch_rows + 16, LANES)
    few = pltpu.CompilerParams(vmem_limit_bytes=SCORE_LIMIT)
    scores, payload = pl.pallas_call(
        functools.partial(score_kernel, devices),
        out_shape=(
            jax.ShapeDtypeStruct((queries, rows_dev), F32),
            jax.ShapeDtypeStruct((copies,) + part, BF16),
        ),
        in_specs=[WHOLE] * 4 + [HBM] * 2,
        out_specs=(WHOLE, WHOLE),
        scratch_shapes=[
            pltpu.VMEM((queries, columns), F32),
            pltpu.VMEM((rows_dev, columns), BF16),
            pltpu.SemaphoreType.DMA((2,)),
        ],
        compiler_params=few,
    )(sent, more_heads, rank, head_row, query_factor, hidden)
    payload = pl.pallas_call(
        merge_kernel,
        out_shape=jax.ShapeDtypeStruct((groups,) + part, BF16),
        in_specs=[SMEM, WHOLE],
        out_specs=WHOLE,
        compiler_params=few,
    )(first, lax.all_to_all(payload, "rep", 0, 0))
    log_probs, expected_tail = pl.pallas_call(
        last_kernel,
        out_shape=(
            jax.ShapeDtypeStruct((queries, rows_dev), F32),
            jax.ShapeDtypeStruct((batch_rows, columns), F32),
        ),
        in_specs=[SMEM, WHOLE, WHOLE],
        out_specs=(HBM, WHOLE),
        scratch_shapes=[
            pltpu.VMEM((queries, rows_dev), F32),
            pltpu.SemaphoreType.DMA((2,)),
        ],
        compiler_params=few,
    )(first, lax.all_to_all(payload, "ent", 0, 0), scores)
    return (log_probs, expected_tail)


def solution(mesh):
    placed = (
        P(("ent", "rep"), None),
        P(),
        P(),
        P(),
        P(),
        P(),
        P(),
        P(("ent", "rep"), None),
        P(("ent", "rep"), None),
        P(("ent", "rep"), None),
        P("ent", None),
        P(),
        P(),
    )
    return jax.shard_map(
        body,
        mesh=mesh,
        in_specs=placed,
        out_specs=(P(None, ("ent", "rep")), P("rep", None)),
        check_vma=False,
    )
```

```python
import functools

import jax
import jax.numpy as jnp
from jax import lax
from jax.experimental import pallas as pl
from jax.experimental.pallas import tpu as pltpu
from jax.sharding import PartitionSpec as P

BLK = 128
CHUNK = 1024
LANES = 128
BF16 = jnp.bfloat16
F32 = jnp.float32
BOTH = ("ent", "rep")
NT = (((1,), (1,)), ((), ()))
TN = (((0,), (0,)), ((), ()))
VMEM_LIMIT = 56 * 2**20
STEP = 2
AHEAD = 5
SCORE_LIMIT = 24 * 2**20


def one_hot(index, rows):
    where = lax.broadcasted_iota(jnp.int16, (rows, index.shape[1]), 0) == index.astype(jnp.int16)
    return jnp.where(where, jnp.asarray(1, BF16), jnp.asarray(0, BF16))


def one_hot_wide(index, rows):
    where = lax.broadcasted_iota(jnp.int32, (rows, index.shape[1]), 0) == index
    return where.astype(F32).astype(BF16)


def is_outside(src, rows_dev):
    return jnp.where(src < rows_dev, 0.0, 1.0).astype(BF16)


def order_blocks(head_ref, first_block, blocks, order_ref):
    def mark(q, marks):
        block = lax.shift_right_arithmetic(head_ref[q], BLK.bit_length() - 1) - first_block
        inside = (block >= 0) & (block < blocks)
        return marks | jnp.where(inside, lax.shift_left(1, jnp.where(inside, block, 0)), 0)

    marks = lax.fori_loop(0, head_ref.shape[0], mark, jnp.int32(0), unroll=16)
    position = jnp.int32(0)
    for wanted in (1, 0):
        for b in range(blocks):
            taken = (lax.shift_right_logical(marks, b) & 1) == wanted
            order_ref[jnp.where(taken, position, blocks + 1)] = jnp.int32(b)
            position = position + taken.astype(jnp.int32)
        if wanted:
            found = position
    order_ref[blocks] = found


def middle_step(order_ref, blocks, ahead):
    return jnp.maximum((order_ref[blocks] + STEP - 1) // STEP, ahead)


def near_kernel(
    ahead,
    base_ref,
    head_ref,
    src_ref,
    rel_ref,
    near_ref,
    relation_ref,
    mixed_ref,
    order_ref,
    held_ref,
    sems,
):
    blocks = src_ref.shape[0]
    rows_dev = near_ref.shape[1]
    order_blocks(head_ref, base_ref[0], blocks, order_ref)
    count = middle_step(order_ref, blocks, ahead)

    def save(step, slot):
        return pltpu.make_async_copy(held_ref.at[slot], mixed_ref.at[step], sems.at[slot])

    def one_step(i, carry):
        slot = lax.rem(i, 2)

        @pl.when(i >= 2)
        def _():
            save(i - 2, slot).wait()

        for u in range(STEP):
            block = order_ref[i * STEP + u]
            src = src_ref[pl.ds(block, 1), :]
            rel = rel_ref[pl.ds(block, 1), :]
            gathered = jnp.dot(near_ref[...], one_hot(src, rows_dev), preferred_element_type=F32)
            relation = jnp.dot(
                relation_ref[...],
                one_hot(rel, relation_ref.shape[1]),
                preferred_element_type=F32,
            )
            is_far = is_outside(src, rows_dev)
            held_ref[slot, u] = (gathered.astype(BF16) + is_far) * relation.astype(BF16)
        save(i, slot).start()
        return carry

    lax.fori_loop(0, count, one_step, 0)
    for back in (2, 1):

        @pl.when(count >= back)
        def _():
            save(count - back, lax.rem(count - back, 2)).wait()


def owners(head_row, devices, rows_dev):
    limits = lax.broadcasted_iota(jnp.int32, (devices, head_row.shape[1]), 0) * rows_dev
    return jnp.sum((limits <= head_row).astype(F32), axis=0, keepdims=True) - 1.0


def ranks(owner_row):
    queries = owner_row.shape[1]
    across = jnp.broadcast_to(owner_row, (queries, queries))
    earlier = lax.broadcasted_iota(jnp.int32, (queries, queries), 0) < lax.broadcasted_iota(
        jnp.int32, (queries, queries), 1
    )
    same = (jnp.transpose(across) == across) & earlier
    return jnp.sum(same.astype(F32), axis=0, keepdims=True)


def far_kernel(
    half_rel,
    last,
    ahead,
    devices,
    base_ref,
    order_ref,
    src_ref,
    dst_ref,
    rel_ref,
    emb_ref,
    far_ref,
    in_ref,
    out_ref,
    loop_ref,
    loop_rel_ref,
    *rest,
):
    far_t_ref, gathered_ref, agg_ref, held_ref, own_ref, made_ref, sems, own_sems, out_sems = rest[-9:]
    if last:
        near_ref, relation_ref, _, hidden_ref = rest[:4]
    else:
        head_ref, query_rel_ref, relation_ref, rel_weight_ref, mixed_ref = rest[:5]
        hidden_ref, heads_ref, factor_ref, rank_ref, most_ref = rest[5:10]
    blocks = src_ref.shape[0]
    rows_dev = blocks * BLK
    far_chunks = far_ref.shape[0]
    middle = middle_step(order_ref, blocks, ahead)
    start, stop = (middle, blocks // STEP) if last else (0, middle)

    def load(step, slot):
        return pltpu.make_async_copy(mixed_ref.at[step], held_ref.at[slot], sems.at[slot])

    def block_rows(step, u):
        return pl.ds(pl.multiple_of(order_ref[step * STEP + u] * BLK, BLK), BLK)

    def load_own(step, u):
        slot = lax.rem(step, 2)
        return pltpu.make_async_copy(
            emb_ref.at[block_rows(step, u)], own_ref.at[slot, u], own_sems.at[slot, u]
        )

    def give(step, u):
        rows = block_rows(step, u)
        return pltpu.make_async_copy(
            made_ref.at[rows], hidden_ref.at[rows], out_sems.at[step * STEP + u]
        )

    if not last:

        @pl.when(start < stop)
        def _():
            load(start, 0).start()

    def turn(j, carry):
        far_t_ref[j] = jnp.transpose(far_ref[j])
        return carry

    lax.fori_loop(0, far_chunks, turn, 0)
    if not last:
        made_ref[...] = jnp.zeros_like(made_ref)

    def look_up(src, u):
        if far_chunks == 1:
            return jnp.dot(
                far_t_ref[0], one_hot(src - rows_dev, CHUNK), preferred_element_type=F32
            )
        gathered_ref[u] = jnp.zeros(gathered_ref.shape[1:], F32)

        def one_chunk(j, carry):
            gathered_ref[u] += jnp.dot(
                far_t_ref[j],
                one_hot(src - rows_dev - j * CHUNK, CHUNK),
                preferred_element_type=F32,
            )
            return carry

        lax.fori_loop(0, far_chunks, one_chunk, 0)
        return gathered_ref[u]

    def finish(step, slot):
        own = own_ref[slot].reshape(STEP * BLK, own_ref.shape[-1])
        own = (own.astype(F32) * loop_rel_ref[...]).astype(BF16)
        preact = jnp.dot(agg_ref[0, slot], in_ref[...], preferred_element_type=F32)
        preact += jnp.dot(agg_ref[1, slot], out_ref[...], preferred_element_type=F32)
        preact += jnp.dot(own, loop_ref[...], preferred_element_type=F32)
        hidden = jnp.tanh(preact).astype(BF16)
        for u in range(STEP):
            made_ref[block_rows(step, u), :] = hidden[u * BLK : (u + 1) * BLK]

    def one_step(i, carry):
        slot = lax.rem(i, 2)
        step = start + i
        before = jnp.maximum(step - 1, start)

        @pl.when(i > 0)
        def _():
            for u in range(STEP):
                load_own(before, u).wait()

        for u in range(STEP):
            load_own(step, u).start()

        if not last:

            @pl.when(step + 1 < stop)
            def _():
                load(step + 1, 1 - slot).start()

            load(step, slot).wait()
        finish(before, lax.rem(step + 1, 2))
        rows = [pl.ds(order_ref[(start + i) * STEP + u], 1) for u in range(STEP)]
        srcs = [src_ref[row, :] for row in rows]
        found = [look_up(src, u) for u, src in enumerate(srcs)]
        composed = []
        for u, row in enumerate(rows):
            if last:
                near = jnp.dot(
                    near_ref[...], one_hot(srcs[u], rows_dev), preferred_element_type=F32
                )
                relation = jnp.dot(
                    relation_ref[...],
                    one_hot(rel_ref[row, :], relation_ref.shape[1]),
                    preferred_element_type=F32,
                )
                composed.append((found[u] + near).astype(BF16) * relation.astype(BF16))
            else:
                is_near = 1 - is_outside(srcs[u], rows_dev)
                composed.append((found[u].astype(BF16) + is_near) * held_ref[slot, u])
        for u, row in enumerate(rows):
            key = dst_ref[row, :] + jnp.where(rel_ref[row, :] >= half_rel, BLK, 0)
            selector = one_hot(key, 2 * BLK)
            counts = selector[:, :128]
            for lane in range(128, selector.shape[1], 128):
                counts = counts + selector[:, lane : lane + 128]
            counts = jnp.sum(counts.astype(F32), axis=1, keepdims=True)
            sums = lax.dot_general(selector, composed[u], NT, preferred_element_type=F32)
            agg = (sums * (1.0 / jnp.maximum(counts, 1.0))).astype(BF16)
            here = pl.ds(u * BLK, BLK)
            agg_ref[0, lax.rem(step, 2), here, :] = agg[:BLK]
            agg_ref[1, lax.rem(step, 2), here, :] = agg[BLK:]

        @pl.when(i > 0)
        def _():
            for u in range(STEP):
                give(before, u).start()

        return carry

    lax.fori_loop(0, stop - start, one_step, 0)

    @pl.when(start < stop)
    def _():
        for u in range(STEP):
            load_own(stop - 1, u).wait()
        finish(stop - 1, lax.rem(stop - 1, 2))
        for u in range(STEP):
            give(stop - 1, u).start()

    if not last:
        picks = one_hot(query_rel_ref[...], relation_ref.shape[1])
        rows = lax.dot_general(
            picks, relation_ref[...], (((0,), (1,)), ((), ())), preferred_element_type=F32
        )
        factor_ref[...] = jnp.dot(
            rows.astype(BF16), rel_weight_ref[...], preferred_element_type=F32
        )
        picks = one_hot_wide(head_ref[...] - base_ref[0] * BLK, rows_dev)
        rows = lax.dot_general(picks, made_ref[...], TN, preferred_element_type=F32)
        rank = ranks(owners(head_ref[...], devices, rows_dev))
        slots = one_hot(rank.astype(jnp.int32), heads_ref.shape[0])
        heads_ref[...] = jnp.dot(slots, rows.astype(BF16), preferred_element_type=F32).astype(BF16)
        rank_ref[...] = rank.astype(jnp.int32)
        most_ref[0] = jnp.max(rank).astype(jnp.int32)

    def gave(step, carry):
        for u in range(STEP):
            give(step, u).wait()
        return carry

    lax.fori_loop(start, stop, gave, 0)


def pick_kernel(base_ref, index_ref, emb_ref, offered_ref):
    picks = one_hot(index_ref[...] - base_ref[0], emb_ref.shape[0])
    offered_ref[...] = lax.dot_general(
        picks, emb_ref[...], TN, preferred_element_type=F32
    ).astype(BF16)


SMEM = pl.BlockSpec(memory_space=pltpu.SMEM)
WHOLE = pl.BlockSpec(memory_space=pltpu.VMEM)
HBM = pl.BlockSpec(memory_space=pltpu.HBM)


def near_call(ahead, base, query_head, src, rel, near, relation):
    columns, edges = near.shape[0], src.shape[1]
    blocks = src.shape[0]
    count = STEP * ahead
    flops = 2 * count * edges * columns * (near.shape[1] + relation.shape[1])
    return pl.pallas_call(
        functools.partial(near_kernel, ahead),
        out_shape=(
            jax.ShapeDtypeStruct((blocks // STEP, STEP, columns, edges), BF16),
            jax.ShapeDtypeStruct((blocks + 2,), jnp.int32),
        ),
        in_specs=[SMEM] * 2 + [WHOLE] * 4,
        out_specs=(HBM, SMEM),
        scratch_shapes=[
            pltpu.VMEM((2, STEP, columns, edges), BF16),
            pltpu.SemaphoreType.DMA((2,)),
        ],
        compiler_params=pltpu.CompilerParams(vmem_limit_bytes=VMEM_LIMIT),
        cost_estimate=pl.CostEstimate(
            flops=flops, bytes_accessed=2 * count * edges * columns, transcendentals=0
        ),
    )(base, query_head, src, rel, near, relation)


def far_call(half_rel, last, ahead, devices, scalars, edges, emb, far, weights, more, kept, outs):
    rows_dev, columns = emb.shape
    blocks, width = edges[0].shape
    return pl.pallas_call(
        functools.partial(far_kernel, half_rel, last, ahead, devices),
        out_shape=(jax.ShapeDtypeStruct((rows_dev, columns), BF16),) + outs,
        in_specs=[SMEM] * 2 + [WHOLE] * 3 + [HBM] + [WHOLE] * (5 + len(more)) + [HBM],
        out_specs=(HBM,) if last else (HBM, WHOLE, WHOLE, WHOLE, SMEM),
        input_output_aliases={11 + len(more): 0} if last else {},
        scratch_shapes=[
            pltpu.VMEM((far.shape[0], columns, CHUNK), BF16),
            pltpu.VMEM((STEP, columns, width if far.shape[0] > 1 else 128), F32),
            pltpu.VMEM((2, 2, STEP * BLK, columns), BF16),
            pltpu.VMEM((2, STEP, columns, 128 if last else width), BF16),
            pltpu.VMEM((2, STEP, BLK, columns), BF16),
            pltpu.VMEM((rows_dev, columns), BF16),
            pltpu.SemaphoreType.DMA((2,)),
            pltpu.SemaphoreType.DMA((2, STEP)),
            pltpu.SemaphoreType.DMA((blocks,)),
        ],
        compiler_params=pltpu.CompilerParams(vmem_limit_bytes=VMEM_LIMIT),
        cost_estimate=pl.CostEstimate(
            flops=blocks * width * columns * far.shape[0] * CHUNK,
            bytes_accessed=blocks * width * columns,
            transcendentals=0,
        ),
    )(*scalars, *edges, emb, far, *weights, *more, kept)


def score_kernel(
    devices,
    sent_ref,
    more_ref,
    rank_ref,
    head_ref,
    factor_hbm,
    hidden_hbm,
    scores_ref,
    payload_ref,
    factor_ref,
    hidden_ref,
    sems,
):
    copies = (
        pltpu.make_async_copy(factor_hbm, factor_ref, sems.at[0]),
        pltpu.make_async_copy(hidden_hbm, hidden_ref, sems.at[1]),
    )
    for copy in copies:
        copy.start()
    slots = sent_ref.shape[0] // devices
    owner = owners(head_ref[...], devices, hidden_ref.shape[0]).astype(jnp.int32)
    place = jnp.where(rank_ref[...] < slots, owner * slots + rank_ref[...], -1)
    picks = one_hot(place, sent_ref.shape[0])
    heads = lax.dot_general(picks, sent_ref[...], TN, preferred_element_type=F32)
    heads = heads + more_ref[...].astype(F32)
    for copy in copies:
        copy.wait()
    query = (heads * factor_ref[...]).astype(BF16)
    scores = lax.dot_general(query, hidden_ref[...], NT, preferred_element_type=F32)
    scores_ref[...] = scores
    top = jnp.max(scores, axis=1, keepdims=True)
    high = top.astype(BF16).astype(F32)
    low = (top - high).astype(BF16).astype(F32)
    top = high + low
    weights = jnp.exp(scores - top)
    total = jnp.sum(weights, axis=1, keepdims=True)
    weighted = jnp.dot(weights.astype(BF16), hidden_ref[...], preferred_element_type=F32)
    total_high = total.astype(BF16).astype(F32)
    lanes = lax.broadcasted_iota(jnp.int32, (query.shape[0], LANES), 1) % 4
    wide = jnp.where(lanes == 0, high, total - total_high)
    wide = jnp.where(lanes == 1, low, wide)
    wide = jnp.where(lanes == 2, total_high, wide)
    stats = jnp.transpose(wide)
    upper = lax.broadcasted_iota(jnp.int32, (8, LANES), 0) < 4
    figures = jnp.where(upper, stats[:8, :LANES], stats[:8, LANES:])
    share = query.shape[0] // payload_ref.shape[0]
    for peer in range(payload_ref.shape[0]):
        rows = weighted[peer * share : (peer + 1) * share]
        payload_ref[peer] = pack(rows[:, :LANES], rows[:, LANES:], figures)


def pack(left, right, figures):
    return jnp.concatenate([left, right, figures, figures], axis=0).astype(BF16)


def merge(data, first):
    share = (data.shape[1] - 16) // 2
    figures = data[:, 2 * share : 2 * share + 8]
    tops, totals, scales = [], [], []
    for half in (0, 4):
        each = figures[:, half : half + 1] + figures[:, half + 1 : half + 2]
        top = jnp.max(each, axis=0)
        scale = jnp.exp(each - top[None])
        total = figures[:, half + 2 : half + 3] + figures[:, half + 3 : half + 4]
        tops.append(top)
        totals.append(jnp.sum(total * scale, axis=0))
        scales.append(scale)
    left = right = 0.0
    for i in range(data.shape[0]):
        scale = jnp.where(first >= LANES, scales[1][i], scales[0][i])
        factor = column(scale, lax.rem(first, LANES), share)
        left += factor * data[i, :share]
        right += factor * data[i, share : 2 * share]
    return left, right, tops, totals


def column(row, first, rows):
    lanes = lax.broadcasted_iota(jnp.int32, (rows, LANES), 1)
    wanted = lax.broadcasted_iota(jnp.int32, (rows, LANES), 0) + first
    return jnp.sum(jnp.where(lanes == wanted, row, 0.0), axis=1, keepdims=True)


def merge_kernel(first_ref, received_ref, payload_ref):
    left, right, tops, totals = merge(received_ref[...].astype(F32), first_ref[0])
    row = lax.broadcasted_iota(jnp.int32, (8, LANES), 0)
    figures = jnp.zeros((8, LANES), F32)
    for half in range(2):
        for at, value in ((0, tops[half]), (2, totals[half])):
            high = value.astype(BF16).astype(F32)
            figures = jnp.where(row == 4 * half + at, high, figures)
            figures = jnp.where(row == 4 * half + at + 1, value - high, figures)
    block = pack(left, right, figures)
    for peer in range(payload_ref.shape[0]):
        payload_ref[peer] = block


def last_kernel(first_ref, received_ref, scores_ref, log_probs_ref, expected_ref):
    first = first_ref[0]
    left, right, tops, totals = merge(received_ref[...].astype(F32), first)
    for half in range(2):
        norm = column(tops[half] + jnp.log(totals[half]), 0, LANES)
        rows = pl.ds(half * LANES, LANES)
        log_probs_ref[rows, :] = scores_ref[rows, :] - norm
    total = jnp.where(first >= LANES, totals[1], totals[0])
    total = column(total, lax.rem(first, LANES), left.shape[0])
    expected_ref[:, :LANES] = left / total
    expected_ref[:, LANES:] = right / total


def body(
    entity_emb,
    relation_emb,
    in_weight,
    out_weight,
    loop_weight,
    rel_weight,
    loop_rel,
    edge_src,
    edge_dst,
    edge_rel,
    export_rows,
    query_head,
    query_rel,
):
    groups = lax.axis_size("ent")
    copies = lax.axis_size("rep")
    devices = groups * copies
    group = lax.axis_index("ent")
    member = lax.axis_index("rep")
    device = group * copies + member
    rows_dev, columns = entity_emb.shape
    queries = query_head.shape[0]

    blocks = edge_src.shape[0]
    relations = relation_emb.shape[0]
    ahead = min(AHEAD, blocks // STEP)

    slots = export_rows.shape[1]
    offered = pl.pallas_call(
        pick_kernel,
        out_shape=jax.ShapeDtypeStruct((slots, columns), BF16),
        in_specs=[SMEM, WHOLE, WHOLE],
        out_specs=WHOLE,
        compiler_params=pltpu.CompilerParams(vmem_limit_bytes=VMEM_LIMIT),
    )((member * rows_dev)[None], export_rows, entity_emb)
    offered, later_relation = lax.optimization_barrier((offered, relation_emb))
    rel_count = -(-relations // 256) * 256
    relation_t = jnp.pad(later_relation, ((0, rel_count - relations), (0, 0))).T
    near_t = entity_emb.T
    pieces = lax.all_to_all(offered, "rep", 0, 0, tiled=True)
    mine = jnp.sum(
        pieces.reshape(copies, slots // copies, columns).astype(F32), axis=0
    ).astype(BF16)
    mine, near_t = lax.optimization_barrier((mine, near_t))
    spread = jnp.broadcast_to(mine[None], (devices,) + mine.shape)
    table = lax.all_to_all(spread, BOTH, 0, 0).reshape(groups * slots, columns)
    base = (device * blocks)[None]
    mixed, order = near_call(
        ahead, base, query_head, edge_src, edge_rel, near_t, relation_t
    )
    far_count = -(-(groups * slots) // CHUNK) * CHUNK
    far = jnp.pad(table, ((0, far_count - groups * slots), (0, 0)))
    far = far.reshape(far_count // CHUNK, CHUNK, columns)

    head_row = query_head[None]
    weights = (in_weight, out_weight, loop_weight, loop_rel[None])
    edges = (edge_src, edge_dst, edge_rel)
    cap = min(queries, -(-3 * queries // (8 * devices)) * 8)
    hidden, heads, query_factor, rank, most = far_call(
        relations // 2,
        False,
        ahead,
        devices,
        (base, order),
        edges,
        entity_emb,
        far,
        weights,
        (head_row, query_rel[None], relation_t, rel_weight),
        mixed,
        (
            jax.ShapeDtypeStruct((-(-queries // cap) * cap, columns), BF16),
            jax.ShapeDtypeStruct((queries, columns), F32),
            jax.ShapeDtypeStruct((1, queries), jnp.int32),
            jax.ShapeDtypeStruct((1,), jnp.int32),
        ),
    )

    def send_round(turn):
        some = lax.dynamic_slice_in_dim(heads, turn * cap, cap, 0)
        spread = jnp.broadcast_to(some[None], (devices,) + some.shape)
        return lax.all_to_all(spread, BOTH, 0, 0).reshape(devices * cap, columns)

    def another_round(state):
        turn, more = state
        slot = rank[0] - turn * cap
        place = query_head // rows_dev * cap + slot
        rows = jnp.take(send_round(turn), jnp.clip(place, 0, devices * cap - 1), axis=0)
        inside = (slot >= 0) & (slot < cap)
        return turn + 1, jnp.where(inside[:, None], rows, more)

    sent = send_round(0)
    (hidden,) = far_call(
        relations // 2,
        True,
        ahead,
        devices,
        (base, order),
        edges,
        entity_emb,
        far,
        weights,
        (near_t, relation_t),
        hidden,
        (),
    )
    _, more_heads = lax.while_loop(
        lambda state: state[0] * cap <= most[0],
        another_round,
        (jnp.int32(1), jnp.zeros((queries, columns), BF16)),
    )

    batch_rows = queries // copies
    first = (member * batch_rows)[None]
    part = (2 * batch_rows + 16, LANES)
    few = pltpu.CompilerParams(vmem_limit_bytes=SCORE_LIMIT)
    scores, payload = pl.pallas_call(
        functools.partial(score_kernel, devices),
        out_shape=(
            jax.ShapeDtypeStruct((queries, rows_dev), F32),
            jax.ShapeDtypeStruct((copies,) + part, BF16),
        ),
        in_specs=[WHOLE] * 4 + [HBM] * 2,
        out_specs=(WHOLE, WHOLE),
        scratch_shapes=[
            pltpu.VMEM((queries, columns), F32),
            pltpu.VMEM((rows_dev, columns), BF16),
            pltpu.SemaphoreType.DMA((2,)),
        ],
        compiler_params=few,
    )(sent, more_heads, rank, head_row, query_factor, hidden)
    payload = pl.pallas_call(
        merge_kernel,
        out_shape=jax.ShapeDtypeStruct((groups,) + part, BF16),
        in_specs=[SMEM, WHOLE],
        out_specs=WHOLE,
        compiler_params=few,
    )(first, lax.all_to_all(payload, "rep", 0, 0))
    log_probs, expected_tail = pl.pallas_call(
        last_kernel,
        out_shape=(
            jax.ShapeDtypeStruct((queries, rows_dev), F32),
            jax.ShapeDtypeStruct((batch_rows, columns), F32),
        ),
        in_specs=[SMEM, WHOLE, WHOLE],
        out_specs=(WHOLE, WHOLE),
        compiler_params=few,
    )(first, lax.all_to_all(payload, "ent", 0, 0), scores)
    return (log_probs, expected_tail)


def solution(mesh):
    placed = (
        P(("ent", "rep"), None),
        P(),
        P(),
        P(),
        P(),
        P(),
        P(),
        P(("ent", "rep"), None),
        P(("ent", "rep"), None),
        P(("ent", "rep"), None),
        P("ent", None),
        P(),
        P(),
    )
    return jax.shard_map(
        body,
        mesh=mesh,
        in_specs=placed,
        out_specs=(P(None, ("ent", "rep")), P("rep", None)),
        check_vma=False,
    )
```
